512 devices in a mesh: outer: 8 (over z_hi, core), inner: 16 (over x, y), head: 4 (over z_lo).
Axes of the slice: x: 4, y: 4, z: 16 (z_hi: 4, z_lo: 4; z = z_hi * 4 + z_lo), core: 2. Of those that a mesh axis runs over, the one named last changes fastest.
Arguments:
- queries: bfloat16 [8192, 2560], P(('outer', 'inner'), 'head'), may hold values from -5 to 5
- keys: bfloat16 [8192, 2560], P(('outer', 'inner'), 'head'), may hold values from -5 to 5
- values: bfloat16 [8192, 2560], P(('outer', 'inner'), 'head'), may hold values from -6 to 6
- slot_blocks: int32 [256], replicated, may hold values from 0 to 255, as said below
- doc_blocks: int32 [4], replicated, may hold values from 1 to 128, 256 in all
Outputs:
- attended: bfloat16 [8192, 2560], P(('outer', 'inner'), 'head')
The draws below stay inside these ranges and needn't reach their ends.
Inputs may be any that keep to these rules, and one draw needn't show every extreme that they name: `slot_blocks`: slots 2 j and 2 j + 1 hold blocks i and 255 - i for some i below 128; every block stands in one slot.
All inputs are finite; a program needn't handle non-finite values.
Results may differ from the reference program's by a relative error of at most 0.008.
Values may be sent and summed in bfloat16 or wider, within the bound.
A program may use at most 128 MiB of HBM per device.

```python
import math
import jax
import jax.numpy as jnp
import numpy as np
from jax import lax

HEAD_DIM = 128
HEADS = 20
BLK = 32
NDOC = 4
NB = 256
SEQ = 8192


def draw_queries(key, part):
    key = jax.random.fold_in(key, 1)
    field = jnp.clip(jax.random.normal(key, (SEQ, HEADS * HEAD_DIM), jnp.float32), -5.0, 5.0)
    return field.astype(jnp.bfloat16)


def draw_keys(key, part):
    key = jax.random.fold_in(key, 2)
    field = jnp.clip(jax.random.normal(key, (SEQ, HEADS * HEAD_DIM), jnp.float32), -5.0, 5.0)
    return field.astype(jnp.bfloat16)


def draw_slot_blocks(key, part):
    key = jax.random.fold_in(key, 5)
    order = jax.random.permutation(key, jnp.arange(NB // 2, dtype=jnp.int32))
    paired = jnp.stack([order, NB - 1 - order], axis=1)
    return paired.reshape(NB).astype(jnp.int32)


def levels(rng, dims, pieces, low, high):
    loudness, own = 1.0, jax.random.fold_in(rng, 6)
    for dim, shards_of in pieces:
        steps = jnp.exp(jax.random.uniform(jax.random.fold_in(own, dim), (shards_of,), jnp.float32, low / len(pieces), high / len(pieces)))
        loudness = loudness * jnp.repeat(steps, dims[dim] // shards_of).reshape([-1 if axis == dim else 1 for axis in range(len(dims))])
    return loudness


def profile(amount, total, bound, skew):
    portions = [(1 << 20) // math.isqrt(grade ** skew) + 1 for grade in range(2, amount + 1)]
    rest, given = total - bound - (amount - 1), [1] * (amount - 1)
    while rest > 0:
        movable = [i for i in range(amount - 1) if given[i] < bound]
        mass, left = sum([portions[i] for i in movable]), rest
        for i in movable:
            addition = min(bound - given[i], max(1, left * portions[i] // mass), rest)
            given[i] = given[i] + addition
            rest = rest - addition
    return np.array([bound] + given)


def uneven(key, count, total, most, skew):
    if count == 2:
        one = jax.random.randint(key, (), max(1, total - most), min(most, total - 1) + 1)
        return jnp.stack([one, total - one])
    sizes = jnp.asarray(profile(count, total, most, skew), jnp.int32)
    pairs = (count - 1) // 2
    donor, taker = sizes[1:1 + 2 * pairs:2], sizes[2:2 + 2 * pairs:2]
    margin = jnp.minimum(donor - 1, most - taker)
    moved = jax.random.randint(jax.random.fold_in(key, 1), (pairs,), 0, 1 << 20) % (margin + 1)
    sizes = sizes.at[1:1 + 2 * pairs:2].set(donor - moved).at[2:2 + 2 * pairs:2].set(taker + moved)
    return sizes[jax.random.permutation(jax.random.fold_in(key, 2), count)]


def bell_draw(key, extent, deviation, limit, shards=(), kind=jnp.bfloat16):
    gain = levels(key, extent, shards, -0.22, 0.18) if shards else 1.0
    drawn = jax.random.normal(key, extent, jnp.float32) * deviation * gain
    return jnp.minimum(jnp.maximum(drawn, -limit), limit).astype(kind)


def setup_inputs(seed: int = 0) -> dict:
    key_of = jax.random.split(jax.random.key(seed), 6)
    queries = draw_queries(jax.random.fold_in(key_of[5], 71), 0)
    keys = draw_keys(jax.random.fold_in(key_of[5], 71), 0)
    values = bell_draw(key_of[2], (SEQ, HEADS * HEAD_DIM), 1.0, 6.0, ((0, 128), (1, 4)))
    slot_blocks = draw_slot_blocks(jax.random.fold_in(key_of[5], 71), 0)
    doc_blocks = uneven(key_of[4], NDOC, NB, NB // 2, 0).astype(jnp.int32)
    return dict(queries=queries, keys=keys, values=values, slot_blocks=slot_blocks, doc_blocks=doc_blocks)


def token_tables(slot_blocks, doc_blocks):
    slot_count = slot_blocks.shape[0]
    offsets = jnp.arange(SEQ, dtype=jnp.int32) % BLK
    spread = jnp.broadcast_to(slot_blocks[:, None], (slot_count, BLK)).reshape(SEQ).astype(jnp.int32)
    position = (spread * BLK + offsets).astype(jnp.int32)
    doc_ends = jnp.cumsum(doc_blocks).astype(jnp.int32)
    doc_of_slot = jnp.sum((slot_blocks[:, None] >= doc_ends[None, :]).astype(jnp.int32), axis=1).astype(jnp.int32)
    document = jnp.broadcast_to(doc_of_slot[:, None], (slot_count, BLK)).reshape(SEQ).astype(jnp.int32)
    return position, document


def reference(queries, keys, values, slot_blocks, doc_blocks):
    position, document = token_tables(slot_blocks, doc_blocks)
    allowed = (position[None, :] <= position[:, None]) & (document[None, :] == document[:, None])
    score_scale = HEAD_DIM ** -0.5

    def by_heads(matrix):
        return jnp.moveaxis(matrix.reshape(SEQ, HEADS, HEAD_DIM), 1, 0)

    def one_head(triple):
        query_head, key_head, value_head = triple
        scores = jnp.dot(query_head, key_head.T, preferred_element_type=jnp.float32) * score_scale
        scores = jnp.where(allowed, scores, -1e30)
        row_max = jnp.max(scores, axis=1, keepdims=True)
        exp_terms = jnp.where(allowed, jnp.exp(scores - row_max), 0.0)
        row_sum = jnp.sum(exp_terms, axis=1, keepdims=True)
        weights = exp_terms.astype(jnp.bfloat16)
        return jnp.dot(weights, value_head, preferred_element_type=jnp.float32) / row_sum

    result = lax.map(one_head, (by_heads(queries), by_heads(keys), by_heads(values)))
    return jnp.moveaxis(result, 0, 1).reshape(SEQ, HEADS * HEAD_DIM).astype(jnp.bfloat16)
```

```python
import functools
import math

import jax
import jax.numpy as jnp
from jax import lax
from jax.experimental import pallas as pl
from jax.experimental.pallas import tpu as pltpu
from jax.sharding import PartitionSpec as P

D = 128
BLK = 32
R = 64
NX = 4
NZ = 2
NC = 2
NQ = NX * NZ * R
NK = NC * NZ * NX * R
STAT = 16
SCALE2 = D ** (-0.5) * math.log2(math.e)
HIDE = -1e30
FLOOR = -1e29
MESH = pl.DeviceIdType.MESH
F32 = jnp.float32
BF16 = jnp.bfloat16


def nt(a, b):
    return lax.dot_general(a, b, (((1,), (1,)), ((), ())), preferred_element_type=F32)


def tn(a, b):
    return lax.dot_general(a, b, (((0,), (0,)), ((), ())), preferred_element_type=F32)


def kernel(
    heads,
    q_ref, k_ref, v_ref, slot_ref, doc_ref, out_ref,
    qg, kvg, bias, op, orecv, own, zs, zr_buf,
    loc_sem, zkv_s, zkv_r, zq_s, zq_r, y_s, y_r, x_s, x_r, c_s, c_r, o_s, o_r, zo_s, zo_r,
):
    outer = lax.axis_index("outer")
    inner = lax.axis_index("inner")
    z, c = outer // 2, outer % 2
    x, y = inner // NX, inner % NX
    za = z + 1 - 2 * (z % 2)
    zb = 3 - z
    dev_a = {"outer": za * 2 + c, "inner": inner}
    dev_b = {"outer": zb * 2 + c, "inner": inner}
    dev_c = {"outer": z * 2 + 1 - c, "inner": inner}

    def dev_x(j):
        return {"outer": outer, "inner": lax.rem(x + j, NX) * NX + y}

    def dev_y(j):
        return {"outer": outer, "inner": x * NX + lax.rem(y + j, NX)}

    def local(h):
        cols = pl.ds(h * D, D)
        return (
            pltpu.make_async_copy(k_ref.at[:, cols], kvg.at[h, 0, 0, 0, y], loc_sem.at[0, h]),
            pltpu.make_async_copy(v_ref.at[:, cols], kvg.at[h, 1, 0, 0, y], loc_sem.at[1, h]),
            pltpu.make_async_copy(q_ref.at[:, cols], qg.at[h, x, 0], loc_sem.at[2, h]),
        )

    for h in range(heads):
        for copy in local(h):
            copy.start()

    barrier = pltpu.get_barrier_semaphore()
    partners = [dev_a, dev_b, dev_c] + [dev_x(j) for j in (1, 2, 3)] + [dev_y(j) for j in (1, 2, 3)]
    for dev in partners:
        pl.semaphore_signal(barrier, inc=1, device_id=dev, device_id_type=MESH)
    pl.semaphore_wait(barrier, len(partners))

    def remote(src, dst, send, recv, dev):
        return pltpu.make_async_remote_copy(
            src_ref=src, dst_ref=dst, send_sem=send, recv_sem=recv, device_id=dev, device_id_type=MESH
        )

    def z_kv(h):
        return remote(kvg.at[h, :, 0, 0, y], kvg.at[h, :, 0, 1, y], zkv_s.at[h], zkv_r.at[h], dev_b)

    def z_q(h):
        return remote(qg.at[h, x, 0], qg.at[h, x, 1], zq_s.at[h], zq_r.at[h], dev_a)

    def y_kv(h, zr, j):
        block = kvg.at[h, :, 0, zr, y]
        return remote(block, block, y_s.at[h, zr, j - 1], y_r.at[h, zr, j - 1], dev_y(j))

    def x_q(h, zr, j):
        block = qg.at[h, x, zr]
        return remote(block, block, x_s.at[h, zr, j - 1], x_r.at[h, zr, j - 1], dev_x(j))

    def c_kv(h, zr):
        return remote(kvg.at[h, :, 0, zr], kvg.at[h, :, 1, zr], c_s.at[h, zr], c_r.at[h, zr], dev_c)

    def x_o(h, j):
        return remote(
            op.at[h, lax.rem(x + j, NX)], orecv.at[h, j - 1], o_s.at[h, j - 1], o_r.at[h, j - 1], dev_x(j)
        )

    def z_o(h):
        return remote(zs.at[h], zr_buf.at[h], zo_s.at[h], zo_r.at[h], dev_a)

    def first(h, carry):
        for copy in local(h):
            copy.wait()
        z_kv(h).start()
        z_q(h).start()
        for j in (1, 3, 2):
            y_kv(h, 0, j).start()
        for j in (1, 3, 2):
            x_q(h, 0, j).start()
        return carry

    lax.fori_loop(0, heads, first, 0)

    ends = [doc_ref[0]]
    for n in range(1, doc_ref.shape[0]):
        ends.append(ends[-1] + doc_ref[n])

    def doc_start(slot):
        start = jnp.int32(0)
        for end in ends:
            start = jnp.where(slot >= end, end, start)
        return start

    lane = lax.broadcasted_iota(jnp.int32, (8, NQ), 1)
    part = lane // BLK
    q_pos = jnp.zeros((8, NQ), jnp.int32)
    q_low = jnp.zeros((8, NQ), jnp.int32)
    for t in range(NQ // BLK):
        xt, zt, half = t // 4, (t // 2) % 2, t % 2
        row_block = ((z if zt == 0 else za) * 2 + c) * 16 + xt * NX + y
        slot = slot_ref[2 * row_block + half]
        hit = part == t
        q_pos = jnp.where(hit, slot * BLK, q_pos)
        q_low = jnp.where(hit, doc_start(slot) * BLK, q_low)
    q_pos = q_pos + lane % BLK

    down = lax.broadcasted_iota(jnp.int32, (8, NQ), 0)

    def mask(t, carry):
        ct, zt, yt, half = t // 16, (t // 8) % 2, (t // 2) % 4, t % 2
        zk = z + zt * (zb - z)
        ck = c + ct * (1 - 2 * c)
        slot = slot_ref[2 * ((zk * 2 + ck) * 16 + x * NX + yt) + half]
        for step in range(BLK // 8):
            k_pos = down + (slot * BLK + step * 8)
            seen = (k_pos <= q_pos) & (k_pos >= q_low)
            bias[pl.ds(pl.multiple_of(t * BLK + step * 8, 8), 8), :] = jnp.where(seen, 0.0, HIDE)
        return carry

    lax.fori_loop(0, NK // BLK, mask, 0)

    def arrive_z(h):
        z_kv(h).wait_recv()
        for j in (1, 3, 2):
            y_kv(h, 1, j).start()
        z_q(h).wait_recv()
        for j in (1, 3, 2):
            x_q(h, 1, j).start()

    def swap_cores(h, zr):
        for j in (1, 2, 3):
            y_kv(h, zr, j).wait_recv()
        c_kv(h, zr).start()

    def attend(h):
        for zr in (0, 1):
            for j in (1, 2, 3):
                x_q(h, zr, j).wait_recv()
            c_kv(h, zr).wait_recv()
        queries = qg[h].reshape(NQ, D)
        keys = kvg[h, 0].reshape(NK, D)
        values = kvg[h, 1].reshape(NK, D)
        width = 256
        for tile in range(NQ // width):
            cols = slice(tile * width, (tile + 1) * width)
            scaled = nt(keys, queries[cols]) * SCALE2 + bias[:, cols]
            top = jnp.max(scaled, axis=0, keepdims=True)
            top = jnp.maximum(top, FLOOR).astype(BF16).astype(F32)
            terms = jnp.exp2(scaled - top)
            total = jnp.sum(terms, axis=0, keepdims=True)
            result = tn(values, terms.astype(BF16)).astype(BF16)
            total_hi = total.astype(BF16).astype(F32)
            row = lax.broadcasted_iota(jnp.int32, (STAT, width), 0)
            stats = jnp.where(row == 0, top, jnp.where(row == 1, total_hi, total - total_hi)).astype(BF16)
            for n in range(width // D):
                target = tile * (width // D) + n
                op[h, target, 0:D, :] = result[:, n * D : (n + 1) * D]
                op[h, target, D : D + STAT, :] = stats[:, n * D : (n + 1) * D]
        for j in (1, 3, 2):
            x_o(h, j).start()

    left = lax.broadcasted_iota(jnp.int32, (8, D), 1) < R

    def unstat(block):
        stat = block.astype(F32)
        return (
            jnp.broadcast_to(stat[0:1], (8, D)),
            jnp.broadcast_to(stat[1:2] + stat[2:3], (8, D)),
        )

    def swap_half(a):
        return pltpu.roll(a, R, axis=1)

    def merge_x(h):
        for j in (1, 2, 3):
            x_o(h, j).wait_recv()
        parts = [(op[h, x, 0:D, :], op[h, x, D : D + STAT, :])]
        for j in (1, 2, 3):
            parts.append((orecv[h, j - 1, 0:D, :], orecv[h, j - 1, D : D + STAT, :]))
        stats = [unstat(p[1]) for p in parts]
        top = functools.reduce(jnp.maximum, [s[0] for s in stats])
        total = jnp.zeros((8, D), F32)
        result = jnp.zeros((D, D), F32)
        for (block, _), (m, l) in zip(parts, stats):
            w = jnp.exp2(m - top)
            total = total + w * l
            result = result + block.astype(F32) * w[0:1]
        low, high = result[0:R], result[R:D]
        mine = jnp.where(left[0:1], low, swap_half(high))
        other = jnp.where(left[0:1], swap_half(low), high)
        top_swapped, total_swapped = swap_half(top), swap_half(total)
        own[h, 0:R, :] = mine
        own[h, R : R + 8, :] = jnp.where(left, top, top_swapped)
        own[h, R + 8 : R + 16, :] = jnp.where(left, total, total_swapped)
        m_other = jnp.where(left, top_swapped, top)[0:1]
        l_other = jnp.where(left, total_swapped, total)[0:1]
        l_hi = l_other.astype(BF16).astype(F32)
        row = lax.broadcasted_iota(jnp.int32, (STAT, D), 0)
        zs[h, 0:R, :] = other.astype(BF16)
        zs[h, R : R + STAT, :] = jnp.where(
            row == 0, m_other, jnp.where(row == 1, l_hi, l_other - l_hi)
        ).astype(BF16)
        z_o(h).start()

    def finish(h):
        z_o(h).wait_recv()
        m_far, l_far = unstat(zr_buf[h, R : R + STAT, :])
        m_own, l_own = own[h, R : R + 8, :], own[h, R + 8 : R + 16, :]
        top = jnp.maximum(m_far, m_own)
        w_far, w_own = jnp.exp2(m_far - top), jnp.exp2(m_own - top)
        total = w_far * l_far + w_own * l_own
        w_far, w_own = w_far / total, w_own / total
        packed = own[h, 0:R, :] * w_own[0:1] + zr_buf[h, 0:R, :].astype(F32) * w_far[0:1]
        tall = jnp.concatenate([packed, swap_half(packed)], axis=0)
        out_ref[:, pl.ds(pl.multiple_of(h * D, D), D)] = tall.T[0:R].astype(BF16)

    def step(i, carry):
        @pl.when(i < heads)
        def _():
            arrive_z(i)
            swap_cores(i, 0)

        @pl.when((i >= 1) & (i < heads + 1))
        def _():
            swap_cores(i - 1, 1)

        @pl.when((i >= 2) & (i < heads + 2))
        def _():
            attend(i - 2)

        @pl.when((i >= 3) & (i < heads + 3))
        def _():
            merge_x(i - 3)

        @pl.when(i >= 4)
        def _():
            finish(i - 4)

        return carry

    lax.fori_loop(0, heads + 4, step, 0)

    def drain(h, carry):
        z_kv(h).wait_send()
        z_q(h).wait_send()
        for zr in (0, 1):
            for j in (1, 2, 3):
                y_kv(h, zr, j).wait_send()
                x_q(h, zr, j).wait_send()
            c_kv(h, zr).wait_send()
        for j in (1, 2, 3):
            x_o(h, j).wait_send()
        z_o(h).wait_send()
        return carry

    lax.fori_loop(0, heads, drain, 0)


def per_device(queries, keys, values, slot_blocks, doc_blocks):
    heads = queries.shape[1] // D
    dma = pltpu.SemaphoreType.DMA
    anywhere = pl.BlockSpec(memory_space=pl.ANY)
    scalars = pl.BlockSpec(memory_space=pltpu.SMEM)
    return pl.pallas_call(
        functools.partial(kernel, heads),
        out_shape=jax.ShapeDtypeStruct(queries.shape, BF16),
        in_specs=[anywhere, anywhere, anywhere, scalars, scalars],
        out_specs=pl.BlockSpec(memory_space=pltpu.VMEM),
        scratch_shapes=[
            pltpu.VMEM((heads, NX, NZ, R, D), BF16),
            pltpu.VMEM((heads, 2, NC, NZ, NX, R, D), BF16),
            pltpu.VMEM((NK, NQ), F32),
            pltpu.VMEM((heads, NX, D + STAT, D), BF16),
            pltpu.VMEM((heads, NX - 1, D + STAT, D), BF16),
            pltpu.VMEM((heads, R + 16, D), F32),
            pltpu.VMEM((heads, R + STAT, D), BF16),
            pltpu.VMEM((heads, R + STAT, D), BF16),
            dma((3, heads)),
            dma((heads,)), dma((heads,)), dma((heads,)), dma((heads,)),
            dma((heads, 2, 3)), dma((heads, 2, 3)), dma((heads, 2, 3)), dma((heads, 2, 3)),
            dma((heads, 2)), dma((heads, 2)),
            dma((heads, 3)), dma((heads, 3)),
            dma((heads,)), dma((heads,)),
        ],
        compiler_params=pltpu.CompilerParams(
            collective_id=0, has_side_effects=True, vmem_limit_bytes=48 * 1024 * 1024
        ),
        cost_estimate=pl.CostEstimate(
            flops=4 * heads * NQ * NK * D, bytes_accessed=4 * queries.size * 2, transcendentals=heads * NQ * NK
        ),
    )(queries, keys, values, slot_blocks, doc_blocks)


def solution(mesh):
    rows = P(("outer", "inner"), "head")
    return jax.shard_map(
        per_device,
        mesh=mesh,
        in_specs=(rows, rows, rows, P(), P()),
        out_specs=rows,
        check_vma=False,
    )
```

```python
import functools
import math

import jax
import jax.numpy as jnp
from jax import lax
from jax.experimental import pallas as pl
from jax.experimental.pallas import tpu as pltpu
from jax.sharding import PartitionSpec as P

D = 128
BLK = 32
R = 64
NX = 4
NZ = 2
NC = 2
NQ = NX * NZ * R
NK = NC * NZ * NX * R
STAT = 16
SCALE2 = D ** (-0.5) * math.log2(math.e)
HIDE = -1e30
FLOOR = -1e29
MESH = pl.DeviceIdType.MESH
F32 = jnp.float32
BF16 = jnp.bfloat16


def nt(a, b):
    return lax.dot_general(a, b, (((1,), (1,)), ((), ())), preferred_element_type=F32)


def tn(a, b):
    return lax.dot_general(a, b, (((0,), (0,)), ((), ())), preferred_element_type=F32)


def kernel(
    heads,
    q_ref, k_ref, v_ref, slot_hbm, doc_hbm, out_ref,
    slot_ref, doc_ref, qg, kvg, bias, op, orecv, own, zs, zr_buf,
    tab_sem, loc_sem, zkv_s, zkv_r, zq_s, zq_r, kv_s, kv_r, q_s, q_r, c_s, c_r, o_s, o_r, zo_s, zo_r,
):
    outer = lax.axis_index("outer")
    inner = lax.axis_index("inner")
    z, c = outer // 2, outer % 2
    x, y = inner // NX, inner % NX
    za = z + 1 - 2 * (z % 2)
    zb = 3 - z
    dev_c = {"outer": z * 2 + 1 - c, "inner": inner}

    def pick(h, even, odd):
        return even + (h % 2) * (odd - even)

    def plane_q(h):
        return {"outer": pick(h, za, zb) * 2 + c, "inner": inner}

    def plane_kv(h):
        return {"outer": pick(h, zb, za) * 2 + c, "inner": inner}

    def along_x(j):
        return lax.rem(x + j, NX) * NX + y

    def along_y(j):
        return x * NX + lax.rem(y + j, NX)

    def ring_q(h, j):
        return {"outer": outer, "inner": pick(h, along_x(j), along_y(j))}

    def ring_kv(h, j):
        return {"outer": outer, "inner": pick(h, along_y(j), along_x(j))}

    def at_q(h, j=0):
        return lax.rem(pick(h, x, y) + j, NX)

    def at_kv(h, j=0):
        return lax.rem(pick(h, y, x) + j, NX)

    tables = (
        pltpu.make_async_copy(slot_hbm, slot_ref, tab_sem.at[0]),
        pltpu.make_async_copy(doc_hbm, doc_ref, tab_sem.at[1]),
    )

    def local(h):
        cols = pl.ds(h * D, D)
        here = at_kv(h)
        return (
            pltpu.make_async_copy(k_ref.at[:, cols], kvg.at[h, 0, 0, 0, here], loc_sem.at[0, h]),
            pltpu.make_async_copy(v_ref.at[:, cols], kvg.at[h, 1, 0, 0, here], loc_sem.at[1, h]),
            pltpu.make_async_copy(q_ref.at[:, cols], qg.at[h, at_q(h), 0], loc_sem.at[2, h]),
        )

    for h in range(heads):
        for copy in local(h):
            copy.start()
    for copy in tables:
        copy.start()

    barrier = pltpu.get_barrier_semaphore()
    partners = [plane_q(0), plane_kv(0), dev_c]
    partners += [ring_q(0, j) for j in (1, 2, 3)] + [ring_kv(0, j) for j in (1, 2, 3)]
    for dev in partners:
        pl.semaphore_signal(barrier, inc=1, device_id=dev, device_id_type=MESH)
    pl.semaphore_wait(barrier, len(partners))

    def remote(src, dst, send, recv, dev):
        return pltpu.make_async_remote_copy(
            src_ref=src, dst_ref=dst, send_sem=send, recv_sem=recv, device_id=dev, device_id_type=MESH
        )

    def z_kv(h):
        here = at_kv(h)
        return remote(
            kvg.at[h, :, 0, 0, here], kvg.at[h, :, 0, 1, here], zkv_s.at[h], zkv_r.at[h], plane_kv(h)
        )

    def z_q(h):
        here = at_q(h)
        return remote(qg.at[h, here, 0], qg.at[h, here, 1], zq_s.at[h], zq_r.at[h], plane_q(h))

    def kv_own(h, zr, way):
        block = kvg.at[h, :, 0, zr, at_kv(h)]
        return remote(block, block, kv_s.at[h, zr, way], kv_r.at[h, zr, way], ring_kv(h, 1 + 2 * way))

    def kv_on(h, zr, way):
        block = kvg.at[h, way, 0, zr, at_kv(h, 3 - 2 * way)]
        return remote(block, block, kv_s.at[h, zr, 2 + way], kv_r.at[h, zr, 2 + way], ring_kv(h, 1 + 2 * way))

    def q_own(h, zr, way):
        block = qg.at[h, at_q(h), zr]
        return remote(block, block, q_s.at[h, zr, way], q_r.at[h, zr, way], ring_q(h, 1 + 2 * way))

    def q_on(h, zr, way):
        block = qg.at[h, at_q(h, 3 - 2 * way), zr, pl.ds(way * (R // 2), R // 2)]
        return remote(block, block, q_s.at[h, zr, 2 + way], q_r.at[h, zr, 2 + way], ring_q(h, 1 + 2 * way))

    def c_kv(h, zr):
        return remote(kvg.at[h, :, 0, zr], kvg.at[h, :, 1, zr], c_s.at[h, zr], c_r.at[h, zr], dev_c)

    def ring_o(h, j):
        return remote(
            op.at[h, at_q(h, j)], orecv.at[h, j - 1], o_s.at[h, j - 1], o_r.at[h, j - 1], ring_q(h, j)
        )

    def z_o(h):
        return remote(zs.at[h], zr_buf.at[h], zo_s.at[h], zo_r.at[h], plane_q(h))

    def first(h, carry):
        for copy in local(h):
            copy.wait()
        z_kv(h).start()
        z_q(h).start()
        for way in (0, 1):
            kv_own(h, 0, way).start()
            q_own(h, 0, way).start()
        return carry

    lax.fori_loop(0, heads, first, 0)
    for copy in tables:
        copy.wait()

    ends = [doc_ref[0]]
    for n in range(1, doc_ref.shape[0]):
        ends.append(ends[-1] + doc_ref[n])

    def doc_start(slot):
        start = jnp.int32(0)
        for end in ends:
            start = jnp.where(slot >= end, end, start)
        return start

    lane = lax.broadcasted_iota(jnp.int32, (8, NQ), 1)
    down = lax.broadcasted_iota(jnp.int32, (8, NQ), 0)
    part = lane // BLK
    for odd in (0, 1):
        q_pos = jnp.zeros((8, NQ), jnp.int32)
        q_low = jnp.zeros((8, NQ), jnp.int32)
        for t in range(NQ // BLK):
            rt, zt, half = t // 4, (t // 2) % 2, t % 2
            zq = z if zt == 0 else (zb if odd else za)
            iq = x * NX + rt if odd else rt * NX + y
            slot = slot_ref[2 * ((zq * 2 + c) * 16 + iq) + half]
            hit = part == t
            q_pos = jnp.where(hit, slot * BLK, q_pos)
            q_low = jnp.where(hit, doc_start(slot) * BLK, q_low)
        q_pos = q_pos + lane % BLK

        def mask(t, carry):
            ct, zt, rt, half = t // 16, (t // 8) % 2, (t // 2) % 4, t % 2
            zk = z + zt * ((za if odd else zb) - z)
            ck = c + ct * (1 - 2 * c)
            ik = rt * NX + y if odd else x * NX + rt
            slot = slot_ref[2 * ((zk * 2 + ck) * 16 + ik) + half]
            for row in range(0, BLK, 8):
                k_pos = down + (slot * BLK + row)
                seen = (k_pos <= q_pos) & (k_pos >= q_low)
                bias[odd, pl.ds(pl.multiple_of(t * BLK + row, 8), 8), :] = jnp.where(seen, 0.0, HIDE)
            return carry

        lax.fori_loop(0, NK // BLK, mask, 0)

    def arrive_z(h):
        z_kv(h).wait_recv()
        for way in (0, 1):
            kv_own(h, 1, way).start()
        z_q(h).wait_recv()
        for way in (0, 1):
            q_own(h, 1, way).start()

    def pass_on(h, zr):
        for way in (0, 1):
            kv_own(h, zr, way).wait_recv()
            kv_on(h, zr, way).start()
        for way in (0, 1):
            q_own(h, zr, way).wait_recv()
            q_on(h, zr, way).start()

    def swap_cores(h, zr):
        for way in (0, 1):
            kv_on(h, zr, way).wait_recv()
        c_kv(h, zr).start()

    def attend(h, tile):
        if tile == 0:
            for zr in (0, 1):
                for way in (0, 1):
                    q_on(h, zr, way).wait_recv()
                c_kv(h, zr).wait_recv()
        width = 256
        each = width // D
        cols = slice(tile * width, (tile + 1) * width)
        queries = qg[h, tile * each : (tile + 1) * each].reshape(width, D)
        keys = kvg[h, 0].reshape(NK, D)
        values = kvg[h, 1].reshape(NK, D)
        scaled = nt(keys, queries) * SCALE2 + bias[h % 2, :, cols]
        top = jnp.max(scaled, axis=0, keepdims=True)
        top = jnp.maximum(top, FLOOR).astype(BF16).astype(F32)
        terms = jnp.exp2(scaled - top)
        total = jnp.sum(terms, axis=0, keepdims=True)
        result = tn(values, terms.astype(BF16)).astype(BF16)
        total_hi = total.astype(BF16).astype(F32)
        row = lax.broadcasted_iota(jnp.int32, (STAT, width), 0)
        stats = jnp.where(row == 0, top, jnp.where(row == 1, total_hi, total - total_hi)).astype(BF16)
        for n in range(each):
            op[h, tile * each + n, 0:D, :] = result[:, n * D : (n + 1) * D]
            op[h, tile * each + n, D : D + STAT, :] = stats[:, n * D : (n + 1) * D]

    left = lax.broadcasted_iota(jnp.int32, (8, D), 1) < R

    def unstat(block):
        stat = block.astype(F32)
        return (
            jnp.broadcast_to(stat[0:1], (8, D)),
            jnp.broadcast_to(stat[1:2] + stat[2:3], (8, D)),
        )

    def swap_half(a):
        return pltpu.roll(a, R, axis=1)

    def merge_ring(h):
        for j in (1, 2, 3):
            ring_o(h, j).wait_recv()
        here = at_q(h)
        parts = [(op[h, here, 0:D, :], op[h, here, D : D + STAT, :])]
        for j in (1, 2, 3):
            parts.append((orecv[h, j - 1, 0:D, :], orecv[h, j - 1, D : D + STAT, :]))
        stats = [unstat(p[1]) for p in parts]
        top = functools.reduce(jnp.maximum, [s[0] for s in stats])
        total = jnp.zeros((8, D), F32)
        result = jnp.zeros((D, D), F32)
        for (block, _), (m, l) in zip(parts, stats):
            w = jnp.exp2(m - top)
            total = total + w * l
            result = result + block.astype(F32) * w[0:1]
        low, high = result[0:R], result[R:D]
        mine = jnp.where(left[0:1], low, swap_half(high))
        other = jnp.where(left[0:1], swap_half(low), high)
        top_swapped, total_swapped = swap_half(top), swap_half(total)
        own[h, 0:R, :] = mine
        own[h, R : R + 8, :] = jnp.where(left, top, top_swapped)
        own[h, R + 8 : R + 16, :] = jnp.where(left, total, total_swapped)
        m_other = jnp.where(left, top_swapped, top)[0:1]
        l_other = jnp.where(left, total_swapped, total)[0:1]
        l_hi = l_other.astype(BF16).astype(F32)
        row = lax.broadcasted_iota(jnp.int32, (STAT, D), 0)
        zs[h, 0:R, :] = other.astype(BF16)
        zs[h, R : R + STAT, :] = jnp.where(
            row == 0, m_other, jnp.where(row == 1, l_hi, l_other - l_hi)
        ).astype(BF16)
        z_o(h).start()

    def finish(h):
        z_o(h).wait_recv()
        m_far, l_far = unstat(zr_buf[h, R : R + STAT, :])
        m_own, l_own = own[h, R : R + 8, :], own[h, R + 8 : R + 16, :]
        top = jnp.maximum(m_far, m_own)
        w_far, w_own = jnp.exp2(m_far - top), jnp.exp2(m_own - top)
        total = w_far * l_far + w_own * l_own
        w_far, w_own = w_far / total, w_own / total
        packed = own[h, 0:R, :] * w_own[0:1] + zr_buf[h, 0:R, :].astype(F32) * w_far[0:1]
        tall = jnp.concatenate([packed, swap_half(packed)], axis=0)
        out_ref[:, pl.ds(pl.multiple_of(h * D, D), D)] = tall.T[0:R].astype(BF16)

    def step(i, carry):
        @pl.when(i < heads)
        def _():
            pass_on(i, 0)
            arrive_z(i)
            swap_cores(i, 0)

        @pl.when((i >= 1) & (i < heads + 1))
        def _():
            swap_cores(i - 1, 1)

        @pl.when((i >= 2) & (i < heads + 2))
        def _():
            attend(i - 2, 0)

        @pl.when(i < heads)
        def _():
            pass_on(i, 1)

        @pl.when((i >= 2) & (i < heads + 2))
        def _():
            attend(i - 2, 1)
            for j in (1, 3, 2):
                ring_o(i - 2, j).start()

        @pl.when((i >= 3) & (i < heads + 3))
        def _():
            merge_ring(i - 3)

        @pl.when(i >= 4)
        def _():
            finish(i - 4)

        return carry

    lax.fori_loop(0, heads + 4, step, 0)

    def drain(h, carry):
        z_kv(h).wait_send()
        z_q(h).wait_send()
        for zr in (0, 1):
            for way in (0, 1):
                kv_own(h, zr, way).wait_send()
                kv_on(h, zr, way).wait_send()
                q_own(h, zr, way).wait_send()
                q_on(h, zr, way).wait_send()
            c_kv(h, zr).wait_send()
        for j in (1, 2, 3):
            ring_o(h, j).wait_send()
        z_o(h).wait_send()
        return carry

    lax.fori_loop(0, heads, drain, 0)


def per_device(queries, keys, values, slot_blocks, doc_blocks):
    heads = queries.shape[1] // D
    dma = pltpu.SemaphoreType.DMA
    anywhere = pl.BlockSpec(memory_space=pltpu.HBM)
    return pl.pallas_call(
        functools.partial(kernel, heads),
        out_shape=jax.ShapeDtypeStruct(queries.shape, BF16),
        in_specs=[anywhere] * 5,
        out_specs=pl.BlockSpec(memory_space=pltpu.VMEM),
        scratch_shapes=[
            pltpu.SMEM(slot_blocks.shape, jnp.int32),
            pltpu.SMEM(doc_blocks.shape, jnp.int32),
            pltpu.VMEM((heads, NX, NZ, R, D), BF16),
            pltpu.VMEM((heads, 2, NC, NZ, NX, R, D), BF16),
            pltpu.VMEM((2, NK, NQ), F32),
            pltpu.VMEM((heads, NX, D + STAT, D), BF16),
            pltpu.VMEM((heads, NX - 1, D + STAT, D), BF16),
            pltpu.VMEM((heads, R + 16, D), F32),
            pltpu.VMEM((heads, R + STAT, D), BF16),
            pltpu.VMEM((heads, R + STAT, D), BF16),
            dma((2,)),
            dma((3, heads)),
            dma((heads,)), dma((heads,)), dma((heads,)), dma((heads,)),
            dma((heads, 2, 4)), dma((heads, 2, 4)), dma((heads, 2, 4)), dma((heads, 2, 4)),
            dma((heads, 2)), dma((heads, 2)),
            dma((heads, 3)), dma((heads, 3)),
            dma((heads,)), dma((heads,)),
        ],
        compiler_params=pltpu.CompilerParams(
            collective_id=0, has_side_effects=True, vmem_limit_bytes=64 * 1024 * 1024
        ),
        cost_estimate=pl.CostEstimate(
            flops=4 * heads * NQ * NK * D, bytes_accessed=4 * queries.size * 2, transcendentals=heads * NQ * NK
        ),
    )(queries, keys, values, slot_blocks, doc_blocks)


def solution(mesh):
    rows = P(("outer", "inner"), "head")
    return jax.shard_map(
        per_device,
        mesh=mesh,
        in_specs=(rows, rows, rows, P(), P()),
        out_specs=rows,
        check_vma=False,
    )
```

```python
import functools
import math

import jax
import jax.numpy as jnp
from jax import lax
from jax.experimental import pallas as pl
from jax.experimental.pallas import tpu as pltpu
from jax.sharding import PartitionSpec as P

D = 128
BLK = 32
R = 64
NX = 4
NZ = 2
NC = 2
NQ = NX * NZ * R
NK = NC * NZ * NX * R
STAT = 16
SCALE2 = D ** (-0.5) * math.log2(math.e)
HIDE = -1e30
FLOOR = -1e29
MESH = pl.DeviceIdType.MESH
F32 = jnp.float32
BF16 = jnp.bfloat16


def nt(a, b):
    return lax.dot_general(a, b, (((1,), (1,)), ((), ())), preferred_element_type=F32)


def tn(a, b):
    return lax.dot_general(a, b, (((0,), (0,)), ((), ())), preferred_element_type=F32)


def place():
    outer = lax.axis_index("outer")
    inner = lax.axis_index("inner")
    z, c = outer // 2, outer % 2
    x, y = inner // NX, inner % NX
    za = z + 1 - 2 * (z % 2)
    zb = 3 - z
    return outer, inner, z, c, x, y, za, zb


def remote(src, dst, send, recv, dev):
    return pltpu.make_async_remote_copy(
        src_ref=src, dst_ref=dst, send_sem=send, recv_sem=recv, device_id=dev, device_id_type=MESH
    )


def greet(partners):
    barrier = pltpu.get_barrier_semaphore()
    for dev in partners:
        pl.semaphore_signal(barrier, inc=1, device_id=dev, device_id_type=MESH)
    pl.semaphore_wait(barrier, len(partners))


def gather_kernel(
    q_ref, k_ref, v_ref, qg, kvg,
    loc_sem, zkv_s, zkv_r, zq_s, zq_r, y_s, y_r, x_s, x_r, c_s, c_r,
):
    outer, inner, z, c, x, y, za, zb = place()
    dev_a = {"outer": za * 2 + c, "inner": inner}
    dev_b = {"outer": zb * 2 + c, "inner": inner}
    dev_c = {"outer": z * 2 + 1 - c, "inner": inner}

    def dev_x(j):
        return {"outer": outer, "inner": lax.rem(x + j, NX) * NX + y}

    def dev_y(j):
        return {"outer": outer, "inner": x * NX + lax.rem(y + j, NX)}

    local = (
        pltpu.make_async_copy(k_ref, kvg.at[0, 0, 0, y], loc_sem.at[0]),
        pltpu.make_async_copy(v_ref, kvg.at[1, 0, 0, y], loc_sem.at[1]),
        pltpu.make_async_copy(q_ref, qg.at[x, 0], loc_sem.at[2]),
    )
    for copy in local:
        copy.start()
    greet([dev_a, dev_b, dev_c] + [dev_x(j) for j in (1, 2, 3)] + [dev_y(j) for j in (1, 2, 3)])
    for copy in local:
        copy.wait()

    z_kv = remote(kvg.at[:, 0, 0, y], kvg.at[:, 0, 1, y], zkv_s, zkv_r, dev_b)
    z_q = remote(qg.at[x, 0], qg.at[x, 1], zq_s, zq_r, dev_a)

    def y_kv(zr, j):
        block = kvg.at[:, 0, zr, y]
        return remote(block, block, y_s.at[zr, j - 1], y_r.at[zr, j - 1], dev_y(j))

    def x_q(zr, j):
        block = qg.at[x, zr]
        return remote(block, block, x_s.at[zr, j - 1], x_r.at[zr, j - 1], dev_x(j))

    def c_kv(zr):
        return remote(kvg.at[:, 0, zr], kvg.at[:, 1, zr], c_s.at[zr], c_r.at[zr], dev_c)

    z_kv.start()
    z_q.start()
    for j in (1, 3, 2):
        y_kv(0, j).start()
    for j in (1, 3, 2):
        x_q(0, j).start()
    for j in (1, 3, 2):
        y_kv(0, j).wait_recv()
    c_kv(0).start()
    z_q.wait_recv()
    for j in (1, 3, 2):
        x_q(1, j).start()
    z_kv.wait_recv()
    for j in (1, 3, 2):
        y_kv(1, j).start()
    for j in (1, 3, 2):
        y_kv(1, j).wait_recv()
    c_kv(1).start()
    for zr in (0, 1):
        for j in (1, 3, 2):
            x_q(zr, j).wait_recv()
        c_kv(zr).wait_recv()
    z_kv.wait_send()
    z_q.wait_send()
    for zr in (0, 1):
        for j in (1, 3, 2):
            y_kv(zr, j).wait_send()
            x_q(zr, j).wait_send()
        c_kv(zr).wait_send()


def attend_kernel(heads, slot_ref, doc_ref, qg, kvg, op, bias):
    outer, inner, z, c, x, y, za, zb = place()
    ends = [doc_ref[0]]
    for n in range(1, doc_ref.shape[0]):
        ends.append(ends[-1] + doc_ref[n])

    def doc_start(slot):
        start = jnp.int32(0)
        for end in ends:
            start = jnp.where(slot >= end, end, start)
        return start

    lane = lax.broadcasted_iota(jnp.int32, (8, NQ), 1)
    part = lane // BLK
    q_pos = jnp.zeros((8, NQ), jnp.int32)
    q_low = jnp.zeros((8, NQ), jnp.int32)
    for t in range(NQ // BLK):
        xt, zt, half = t // 4, (t // 2) % 2, t % 2
        row_block = ((z if zt == 0 else za) * 2 + c) * 16 + xt * NX + y
        slot = slot_ref[2 * row_block + half]
        hit = part == t
        q_pos = jnp.where(hit, slot * BLK, q_pos)
        q_low = jnp.where(hit, doc_start(slot) * BLK, q_low)
    q_pos = q_pos + lane % BLK

    down = lax.broadcasted_iota(jnp.int32, (8, NQ), 0)

    def mask(t, carry):
        ct, zt, yt, half = t // 16, (t // 8) % 2, (t // 2) % 4, t % 2
        zk = z + zt * (zb - z)
        ck = c + ct * (1 - 2 * c)
        slot = slot_ref[2 * ((zk * 2 + ck) * 16 + x * NX + yt) + half]
        for row in range(0, BLK, 8):
            k_pos = down + (slot * BLK + row)
            seen = (k_pos <= q_pos) & (k_pos >= q_low)
            bias[pl.ds(pl.multiple_of(t * BLK + row, 8), 8), :] = jnp.where(seen, 0.0, HIDE)
        return carry

    lax.fori_loop(0, NK // BLK, mask, 0)

    def attend(h, carry):
        at = pl.ds(pl.multiple_of(h * D, D), D)
        queries = qg[:, :, :, at].reshape(NQ, D)
        keys = kvg[0, :, :, :, :, at].reshape(NK, D)
        values = kvg[1, :, :, :, :, at].reshape(NK, D)
        width = 256
        for tile in range(NQ // width):
            cols = slice(tile * width, (tile + 1) * width)
            scaled = nt(keys, queries[cols]) * SCALE2 + bias[:, cols]
            top = jnp.max(scaled, axis=0, keepdims=True)
            top = jnp.maximum(top, FLOOR).astype(BF16).astype(F32)
            terms = jnp.exp2(scaled - top)
            total = jnp.sum(terms, axis=0, keepdims=True)
            result = tn(values, terms.astype(BF16)).astype(BF16)
            total_hi = total.astype(BF16).astype(F32)
            row = lax.broadcasted_iota(jnp.int32, (STAT, width), 0)
            stats = jnp.where(row == 0, top, jnp.where(row == 1, total_hi, total - total_hi)).astype(BF16)
            for n in range(width // D):
                target = tile * (width // D) + n
                op[target, h, 0:D, :] = result[:, n * D : (n + 1) * D]
                op[target, h, D : D + STAT, :] = stats[:, n * D : (n + 1) * D]
        return carry

    lax.fori_loop(0, heads, attend, 0)


def reduce_kernel(heads, op, out_ref, orecv, own, zs, zr_buf, o_s, o_r, zo_s, zo_r):
    outer, inner, z, c, x, y, za, zb = place()
    dev_a = {"outer": za * 2 + c, "inner": inner}

    def dev_x(j):
        return {"outer": outer, "inner": lax.rem(x + j, NX) * NX + y}

    def x_o(j):
        return remote(op.at[lax.rem(x + j, NX)], orecv.at[j - 1], o_s.at[j - 1], o_r.at[j - 1], dev_x(j))

    def z_o(h):
        return remote(zs.at[h], zr_buf.at[h], zo_s.at[h], zo_r.at[h], dev_a)

    greet([dev_a] + [dev_x(j) for j in (1, 2, 3)])
    for j in (1, 3, 2):
        x_o(j).start()
    for j in (1, 3, 2):
        x_o(j).wait_recv()

    left = lax.broadcasted_iota(jnp.int32, (8, D), 1) < R

    def unstat(block):
        stat = block.astype(F32)
        return (
            jnp.broadcast_to(stat[0:1], (8, D)),
            jnp.broadcast_to(stat[1:2] + stat[2:3], (8, D)),
        )

    def swap_half(a):
        return pltpu.roll(a, R, axis=1)

    def merge_x(h, carry):
        parts = [(op[x, h, 0:D, :], op[x, h, D : D + STAT, :])]
        for j in (1, 2, 3):
            parts.append((orecv[j - 1, h, 0:D, :], orecv[j - 1, h, D : D + STAT, :]))
        stats = [unstat(p[1]) for p in parts]
        top = functools.reduce(jnp.maximum, [s[0] for s in stats])
        total = jnp.zeros((8, D), F32)
        result = jnp.zeros((D, D), F32)
        for (block, _), (m, l) in zip(parts, stats):
            w = jnp.exp2(m - top)
            total = total + w * l
            result = result + block.astype(F32) * w[0:1]
        low, high = result[0:R], result[R:D]
        mine = jnp.where(left[0:1], low, swap_half(high))
        other = jnp.where(left[0:1], swap_half(low), high)
        top_swapped, total_swapped = swap_half(top), swap_half(total)
        own[h, 0:R, :] = mine
        own[h, R : R + 8, :] = jnp.where(left, top, top_swapped)
        own[h, R + 8 : R + 16, :] = jnp.where(left, total, total_swapped)
        m_other = jnp.where(left, top_swapped, top)[0:1]
        l_other = jnp.where(left, total_swapped, total)[0:1]
        l_hi = l_other.astype(BF16).astype(F32)
        row = lax.broadcasted_iota(jnp.int32, (STAT, D), 0)
        zs[h, 0:R, :] = other.astype(BF16)
        zs[h, R : R + STAT, :] = jnp.where(
            row == 0, m_other, jnp.where(row == 1, l_hi, l_other - l_hi)
        ).astype(BF16)
        z_o(h).start()
        return carry

    lax.fori_loop(0, heads, merge_x, 0)

    def finish(h, carry):
        z_o(h).wait_recv()
        m_far, l_far = unstat(zr_buf[h, R : R + STAT, :])
        m_own, l_own = own[h, R : R + 8, :], own[h, R + 8 : R + 16, :]
        top = jnp.maximum(m_far, m_own)
        w_far, w_own = jnp.exp2(m_far - top), jnp.exp2(m_own - top)
        total = w_far * l_far + w_own * l_own
        w_far, w_own = w_far / total, w_own / total
        packed = own[h, 0:R, :] * w_own[0:1] + zr_buf[h, 0:R, :].astype(F32) * w_far[0:1]
        tall = jnp.concatenate([packed, swap_half(packed)], axis=0)
        out_ref[:, pl.ds(pl.multiple_of(h * D, D), D)] = tall.T[0:R].astype(BF16)
        z_o(h).wait_send()
        return carry

    lax.fori_loop(0, heads, finish, 0)
    for j in (1, 3, 2):
        x_o(j).wait_send()


def per_device(queries, keys, values, slot_blocks, doc_blocks):
    width = queries.shape[1]
    heads = width // D
    dma = pltpu.SemaphoreType.DMA
    anywhere = pl.BlockSpec(memory_space=pl.ANY)
    vmem = pl.BlockSpec(memory_space=pltpu.VMEM)
    scalars = pl.BlockSpec(memory_space=pltpu.SMEM)
    limit = 24 * 1024 * 1024
    gathered_q, gathered_kv = pl.pallas_call(
        gather_kernel,
        out_shape=(
            jax.ShapeDtypeStruct((NX, NZ, R, width), BF16),
            jax.ShapeDtypeStruct((2, NC, NZ, NX, R, width), BF16),
        ),
        in_specs=[anywhere] * 3,
        out_specs=(vmem, vmem),
        scratch_shapes=[
            dma((3,)), dma, dma, dma, dma,
            dma((2, 3)), dma((2, 3)), dma((2, 3)), dma((2, 3)), dma((2,)), dma((2,)),
        ],
        compiler_params=pltpu.CompilerParams(collective_id=0, has_side_effects=True, vmem_limit_bytes=limit),
        name="gather",
    )(queries, keys, values)
    partial = pl.pallas_call(
        functools.partial(attend_kernel, heads),
        out_shape=jax.ShapeDtypeStruct((NX, heads, D + STAT, D), BF16),
        in_specs=[scalars, scalars, vmem, vmem],
        out_specs=vmem,
        scratch_shapes=[pltpu.VMEM((NK, NQ), F32)],
        compiler_params=pltpu.CompilerParams(vmem_limit_bytes=limit),
        name="attend",
    )(slot_blocks, doc_blocks, gathered_q, gathered_kv)
    return pl.pallas_call(
        functools.partial(reduce_kernel, heads),
        out_shape=jax.ShapeDtypeStruct(queries.shape, BF16),
        in_specs=[vmem],
        out_specs=vmem,
        scratch_shapes=[
            pltpu.VMEM((NX - 1, heads, D + STAT, D), BF16),
            pltpu.VMEM((heads, R + 16, D), F32),
            pltpu.VMEM((heads, R + STAT, D), BF16),
            pltpu.VMEM((heads, R + STAT, D), BF16),
            dma((3,)), dma((3,)), dma((heads,)), dma((heads,)),
        ],
        compiler_params=pltpu.CompilerParams(collective_id=1, has_side_effects=True, vmem_limit_bytes=limit),
        name="reduce",
    )(partial)


def solution(mesh):
    rows = P(("outer", "inner"), "head")
    return jax.shard_map(
        per_device,
        mesh=mesh,
        in_specs=(rows, rows, rows, P(), P()),
        out_specs=rows,
        check_vma=False,
    )
```

```python
import functools
import math

import jax
import jax.numpy as jnp
from jax import lax
from jax.experimental import pallas as pl
from jax.experimental.pallas import tpu as pltpu
from jax.sharding import PartitionSpec as P

D = 128
BLK = 32
R = 64
NX = 4
NZ = 2
NC = 2
NQ = NX * NZ * R
NK = NC * NZ * NX * R
STAT = 16
SCALE2 = D ** (-0.5) * math.log2(math.e)
HIDE = -1e30
FLOOR = -1e29
MESH = pl.DeviceIdType.MESH
F32 = jnp.float32
BF16 = jnp.bfloat16


def nt(a, b):
    return lax.dot_general(a, b, (((1,), (1,)), ((), ())), preferred_element_type=F32)


def tn(a, b):
    return lax.dot_general(a, b, (((0,), (0,)), ((), ())), preferred_element_type=F32)


def kernel(
    heads,
    q_ref, k_ref, v_ref, slot_hbm, doc_hbm, out_ref,
    slot_ref, doc_ref, qg, kvg, bias, half_o, half_stat, op, orecv, own, zs, zr_buf, out_buf,
    tab_sem, loc_sem, zkv_s, zkv_r, zq_s, zq_r, kv_s, kv_r, q_s, q_r, c_s, c_r, o_s, o_r, zo_s, zo_r, out_sem,
):
    outer = lax.axis_index("outer")
    inner = lax.axis_index("inner")
    z, c = outer // 2, outer % 2
    x, y = inner // NX, inner % NX
    za = z + 1 - 2 * (z % 2)
    zb = 3 - z
    dev_c = {"outer": z * 2 + 1 - c, "inner": inner}
    first_heads = (heads + 1) // 2
    groups = (0, 1)
    cols = (pl.ds(0, first_heads * D), pl.ds(first_heads * D, (heads - first_heads) * D))

    def pick(g, even, odd):
        return even + g * (odd - even)

    def group_of(h):
        return h // first_heads

    def plane_q(g):
        return {"outer": pick(g, za, zb) * 2 + c, "inner": inner}

    def plane_kv(g):
        return {"outer": pick(g, zb, za) * 2 + c, "inner": inner}

    def along_x(j):
        return lax.rem(x + j, NX) * NX + y

    def along_y(j):
        return x * NX + lax.rem(y + j, NX)

    def ring_q(g, j):
        return {"outer": outer, "inner": pick(g, along_x(j), along_y(j))}

    def ring_kv(g, j):
        return {"outer": outer, "inner": pick(g, along_y(j), along_x(j))}

    def at_q(g, j=0):
        return lax.rem(pick(g, x, y) + j, NX)

    def at_kv(g, j=0):
        return lax.rem(pick(g, y, x) + j, NX)

    tables = (
        pltpu.make_async_copy(slot_hbm, slot_ref, tab_sem.at[0]),
        pltpu.make_async_copy(doc_hbm, doc_ref, tab_sem.at[1]),
    )

    def local(g):
        at = cols[g]
        return (
            pltpu.make_async_copy(k_ref.at[:, at], kvg.at[0, 0, 0, at_kv(g), :, at], loc_sem.at[0, g]),
            pltpu.make_async_copy(v_ref.at[:, at], kvg.at[1, 0, 0, at_kv(g), :, at], loc_sem.at[1, g]),
            pltpu.make_async_copy(q_ref.at[:, at], qg.at[at_q(g), 0, :, at], loc_sem.at[2, g]),
        )

    for g in groups:
        for copy in local(g):
            copy.start()
    for copy in tables:
        copy.start()

    barrier = pltpu.get_barrier_semaphore()
    partners = [plane_q(0), plane_kv(0), dev_c]
    partners += [ring_q(0, j) for j in (1, 2, 3)] + [ring_kv(0, j) for j in (1, 2, 3)]
    for dev in partners:
        pl.semaphore_signal(barrier, inc=1, device_id=dev, device_id_type=MESH)
    pl.semaphore_wait(barrier, len(partners))

    def remote(src, dst, send, recv, dev):
        return pltpu.make_async_remote_copy(
            src_ref=src, dst_ref=dst, send_sem=send, recv_sem=recv, device_id=dev, device_id_type=MESH
        )

    def z_kv(g):
        here, at = at_kv(g), cols[g]
        return remote(
            kvg.at[:, 0, 0, here, :, at], kvg.at[:, 0, 1, here, :, at], zkv_s.at[g], zkv_r.at[g], plane_kv(g)
        )

    def z_q(g):
        here, at = at_q(g), cols[g]
        return remote(qg.at[here, 0, :, at], qg.at[here, 1, :, at], zq_s.at[g], zq_r.at[g], plane_q(g))

    def kv_own(g, zr, way):
        block = kvg.at[:, 0, zr, at_kv(g), :, cols[g]]
        return remote(block, block, kv_s.at[g, zr, way], kv_r.at[g, zr, way], ring_kv(g, 1 + 2 * way))

    def kv_on(g, zr, way):
        block = kvg.at[way, 0, zr, at_kv(g, 3 - 2 * way), :, cols[g]]
        return remote(block, block, kv_s.at[g, zr, 2 + way], kv_r.at[g, zr, 2 + way], ring_kv(g, 1 + 2 * way))

    def q_own(g, zr, way):
        block = qg.at[at_q(g), zr, :, cols[g]]
        return remote(block, block, q_s.at[g, zr, way], q_r.at[g, zr, way], ring_q(g, 1 + 2 * way))

    def q_on(g, zr, way):
        block = qg.at[at_q(g, 3 - 2 * way), zr, pl.ds(way * (R // 2), R // 2), cols[g]]
        return remote(block, block, q_s.at[g, zr, 2 + way], q_r.at[g, zr, 2 + way], ring_q(g, 1 + 2 * way))

    def c_kv(g, zr):
        at = cols[g]
        return remote(
            kvg.at[:, 0, zr, :, :, at], kvg.at[:, 1, zr, :, :, at], c_s.at[g, zr], c_r.at[g, zr], dev_c
        )

    def ring_o(h, j):
        g = group_of(h)
        return remote(
            op.at[h, at_q(g, j)], orecv.at[h, j - 1], o_s.at[h, j - 1], o_r.at[h, j - 1], ring_q(g, j)
        )

    def z_o(h):
        return remote(zs.at[h], zr_buf.at[h], zo_s.at[h], zo_r.at[h], plane_q(group_of(h)))

    def out_copy(h):
        return pltpu.make_async_copy(
            out_buf.at[h], out_ref.at[:, pl.ds(pl.multiple_of(h * D, D), D)], out_sem.at[h]
        )

    for g in groups:
        for copy in local(g):
            copy.wait()
        z_q(g).start()
        z_kv(g).start()
    for g in groups:
        for way in (0, 1):
            kv_own(g, 0, way).start()
        for way in (0, 1):
            q_own(g, 0, way).start()
    for copy in tables:
        copy.wait()

    ends = [doc_ref[0]]
    for n in range(1, doc_ref.shape[0]):
        ends.append(ends[-1] + doc_ref[n])

    def doc_start(slot):
        start = jnp.int32(0)
        for end in ends:
            start = jnp.where(slot >= end, end, start)
        return start

    lane = lax.broadcasted_iota(jnp.int32, (8, NQ), 1)
    down = lax.broadcasted_iota(jnp.int32, (8, NQ), 0)
    part = lane // BLK

    def build_mask(g):
        q_pos = jnp.zeros((8, NQ), jnp.int32)
        q_low = jnp.zeros((8, NQ), jnp.int32)
        for t in range(NQ // BLK):
            rt, zt, half = t // 4, (t // 2) % 2, t % 2
            zq = z if zt == 0 else (zb if g else za)
            iq = x * NX + rt if g else rt * NX + y
            slot = slot_ref[2 * ((zq * 2 + c) * 16 + iq) + half]
            hit = part == t
            q_pos = jnp.where(hit, slot * BLK, q_pos)
            q_low = jnp.where(hit, doc_start(slot) * BLK, q_low)
        q_pos = q_pos + lane % BLK

        def mask(t, carry):
            ct, zt, rt, half = t // 16, (t // 8) % 2, (t // 2) % 4, t % 2
            zk = z + zt * ((za if g else zb) - z)
            ck = c + ct * (1 - 2 * c)
            ik = rt * NX + y if g else x * NX + rt
            slot = slot_ref[2 * ((zk * 2 + ck) * 16 + ik) + half]
            for row in range(0, BLK, 8):
                k_pos = down + (slot * BLK + row)
                seen = (k_pos <= q_pos) & (k_pos >= q_low)
                at = (zt * 2 + ct) * (NX * R) + rt * R + half * BLK + row
                bias[g, pl.ds(pl.multiple_of(at, 8), 8), :] = jnp.where(seen, 0.0, HIDE)
            return carry

        lax.fori_loop(0, NK // BLK, mask, 0)

    def pass_on_kv(zr):
        for g in groups:
            for way in (0, 1):
                kv_own(g, zr, way).wait_recv()
                kv_on(g, zr, way).start()

    def pass_on_q(zr):
        for g in groups:
            for way in (0, 1):
                q_own(g, zr, way).wait_recv()
                q_on(g, zr, way).start()

    def swap_cores(zr):
        for g in groups:
            for way in (0, 1):
                kv_on(g, zr, way).wait_recv()
            c_kv(g, zr).start()

    def attend(h, zr):
        at = pl.ds(pl.multiple_of(h * D, D), D)
        g = group_of(h)
        count = NK // NZ
        keys = kvg[0, :, zr, :, :, at].reshape(count, D)
        values = kvg[1, :, zr, :, :, at].reshape(count, D)
        width = 256
        each = width // D
        for tile in range(NQ // width):
            span = slice(tile * width, (tile + 1) * width)
            queries = qg[tile * each : (tile + 1) * each, :, :, at].reshape(width, D)
            scaled = nt(keys, queries) * SCALE2 + bias[g, zr * count : (zr + 1) * count, span]
            top = jnp.max(scaled, axis=0, keepdims=True)
            top = jnp.maximum(top, FLOOR).astype(BF16).astype(F32)
            if zr:
                before = half_stat[h, 0:1, span]
                top = jnp.maximum(top, before)
            terms = jnp.exp2(scaled - top)
            total = jnp.sum(terms, axis=0, keepdims=True)
            result = tn(values, terms.astype(BF16))
            if not zr:
                half_stat[h, 0:1, span] = top
                half_stat[h, 1:2, span] = total
                half_o[h, :, span] = result
                continue
            shrink = jnp.exp2(before - top)
            total = total + half_stat[h, 1:2, span] * shrink
            result = (result + half_o[h, :, span] * shrink).astype(BF16)
            total_hi = total.astype(BF16).astype(F32)
            row = lax.broadcasted_iota(jnp.int32, (STAT, width), 0)
            stats = jnp.where(row == 0, top, jnp.where(row == 1, total_hi, total - total_hi)).astype(BF16)
            for n in range(each):
                op[h, tile * each + n, 0:D, :] = result[:, n * D : (n + 1) * D]
                op[h, tile * each + n, D : D + STAT, :] = stats[:, n * D : (n + 1) * D]

    left = lax.broadcasted_iota(jnp.int32, (8, D), 1) < R

    def unstat(block):
        stat = block.astype(F32)
        return (
            jnp.broadcast_to(stat[0:1], (8, D)),
            jnp.broadcast_to(stat[1:2] + stat[2:3], (8, D)),
        )

    def swap_half(a):
        return pltpu.roll(a, R, axis=1)

    def merge_ring(h):
        for j in (1, 3, 2):
            ring_o(h, j).wait_recv()
        here = at_q(group_of(h))
        parts = [(op[h, here, 0:D, :], op[h, here, D : D + STAT, :])]
        for j in (1, 2, 3):
            parts.append((orecv[h, j - 1, 0:D, :], orecv[h, j - 1, D : D + STAT, :]))
        stats = [unstat(p[1]) for p in parts]
        top = functools.reduce(jnp.maximum, [s[0] for s in stats])
        total = jnp.zeros((8, D), F32)
        result = jnp.zeros((D, D), F32)
        for (block, _), (m, l) in zip(parts, stats):
            w = jnp.exp2(m - top)
            total = total + w * l
            result = result + block.astype(F32) * w[0:1]
        low, high = result[0:R], result[R:D]
        mine = jnp.where(left[0:1], low, swap_half(high))
        other = jnp.where(left[0:1], swap_half(low), high)
        top_swapped, total_swapped = swap_half(top), swap_half(total)
        own[h, 0:R, :] = mine
        own[h, R : R + 8, :] = jnp.where(left, top, top_swapped)
        own[h, R + 8 : R + 16, :] = jnp.where(left, total, total_swapped)
        m_other = jnp.where(left, top_swapped, top)[0:1]
        l_other = jnp.where(left, total_swapped, total)[0:1]
        l_hi = l_other.astype(BF16).astype(F32)
        row = lax.broadcasted_iota(jnp.int32, (STAT, D), 0)
        zs[h, 0:R, :] = other.astype(BF16)
        zs[h, R : R + STAT, :] = jnp.where(
            row == 0, m_other, jnp.where(row == 1, l_hi, l_other - l_hi)
        ).astype(BF16)
        z_o(h).start()

    def finish(h):
        z_o(h).wait_recv()
        m_far, l_far = unstat(zr_buf[h, R : R + STAT, :])
        m_own, l_own = own[h, R : R + 8, :], own[h, R + 8 : R + 16, :]
        top = jnp.maximum(m_far, m_own)
        w_far, w_own = jnp.exp2(m_far - top), jnp.exp2(m_own - top)
        total = w_far * l_far + w_own * l_own
        w_far, w_own = w_far / total, w_own / total
        packed = own[h, 0:R, :] * w_own[0:1] + zr_buf[h, 0:R, :].astype(F32) * w_far[0:1]
        tall = jnp.concatenate([packed, swap_half(packed)], axis=0)
        out_buf[h] = tall.T[0:R].astype(BF16)
        out_copy(h).start()

    build_mask(0)
    pass_on_kv(0)
    pass_on_q(0)
    build_mask(1)
    swap_cores(0)
    for g in groups:
        z_q(g).wait_recv()
        for way in (0, 1):
            q_own(g, 1, way).start()
    pass_on_q(1)
    for g in groups:
        for zr in (0, 1):
            for way in (0, 1):
                q_on(g, zr, way).wait_recv()
        c_kv(g, 0).wait_recv()

    def early(i, carry):
        @pl.when(i == heads - 2)
        def _():
            for g in groups:
                z_kv(g).wait_recv()
                for way in (0, 1):
                    kv_own(g, 1, way).start()

        attend(i, 0)
        return carry

    lax.fori_loop(0, heads, early, 0)
    pass_on_kv(1)
    swap_cores(1)
    for g in groups:
        c_kv(g, 1).wait_recv()

    def turn(i):
        return lax.rem((i + 1) * first_heads, heads)

    def late(i, carry):
        @pl.when(i < heads)
        def _():
            h = turn(i)
            attend(h, 1)
            for j in (1, 3, 2):
                ring_o(h, j).start()

        @pl.when((i >= 2) & (i < heads + 2))
        def _():
            merge_ring(turn(i - 2))

        @pl.when(i >= 5)
        def _():
            finish(turn(i - 5))

        return carry

    lax.fori_loop(0, heads + 5, late, 0)

    for g in groups:
        z_kv(g).wait_send()
        z_q(g).wait_send()
        for zr in (0, 1):
            for way in (0, 1):
                kv_own(g, zr, way).wait_send()
                kv_on(g, zr, way).wait_send()
                q_own(g, zr, way).wait_send()
                q_on(g, zr, way).wait_send()
            c_kv(g, zr).wait_send()

    def drain(h, carry):
        for j in (1, 2, 3):
            ring_o(h, j).wait_send()
        z_o(h).wait_send()
        out_copy(h).wait()
        return carry

    lax.fori_loop(0, heads, drain, 0)


def per_device(queries, keys, values, slot_blocks, doc_blocks):
    width = queries.shape[1]
    heads = width // D
    dma = pltpu.SemaphoreType.DMA
    anywhere = pl.BlockSpec(memory_space=pltpu.HBM)
    return pl.pallas_call(
        functools.partial(kernel, heads),
        out_shape=jax.ShapeDtypeStruct(queries.shape, BF16),
        in_specs=[anywhere] * 5,
        out_specs=anywhere,
        scratch_shapes=[
            pltpu.SMEM(slot_blocks.shape, jnp.int32),
            pltpu.SMEM(doc_blocks.shape, jnp.int32),
            pltpu.VMEM((NX, NZ, R, width), BF16),
            pltpu.VMEM((2, NC, NZ, NX, R, width), BF16),
            pltpu.VMEM((2, NK, NQ), F32),
            pltpu.VMEM((heads, D, NQ), F32),
            pltpu.VMEM((heads, 8, NQ), F32),
            pltpu.VMEM((heads, NX, D + STAT, D), BF16),
            pltpu.VMEM((heads, NX - 1, D + STAT, D), BF16),
            pltpu.VMEM((heads, R + 16, D), F32),
            pltpu.VMEM((heads, R + STAT, D), BF16),
            pltpu.VMEM((heads, R + STAT, D), BF16),
            pltpu.VMEM((heads, R, D), BF16),
            dma((2,)),
            dma((3, 2)),
            dma((2,)), dma((2,)), dma((2,)), dma((2,)),
            dma((2, 2, 4)), dma((2, 2, 4)), dma((2, 2, 4)), dma((2, 2, 4)),
            dma((2, 2)), dma((2, 2)),
            dma((heads, 3)), dma((heads, 3)),
            dma((heads,)), dma((heads,)), dma((heads,)),
        ],
        compiler_params=pltpu.CompilerParams(
            collective_id=0, has_side_effects=True, vmem_limit_bytes=64 * 1024 * 1024
        ),
        cost_estimate=pl.CostEstimate(
            flops=4 * heads * NQ * NK * D, bytes_accessed=4 * queries.size * 2, transcendentals=heads * NQ * NK
        ),
    )(queries, keys, values, slot_blocks, doc_blocks)


def solution(mesh):
    rows = P(("outer", "inner"), "head")
    return jax.shard_map(
        per_device,
        mesh=mesh,
        in_specs=(rows, rows, rows, P(), P()),
        out_specs=rows,
        check_vma=False,
    )
```

```python
import functools
import math

import jax
import jax.numpy as jnp
from jax import lax
from jax.experimental import pallas as pl
from jax.experimental.pallas import tpu as pltpu
from jax.sharding import PartitionSpec as P

D = 128
BLK = 32
R = 64
NX = 4
NZ = 2
NC = 2
NQ = NX * NZ * R
NK = NC * NZ * NX * R
STAT = 16
SCALE2 = D ** (-0.5) * math.log2(math.e)
HIDE = -1e30
FLOOR = -1e29
MESH = pl.DeviceIdType.MESH
F32 = jnp.float32
BF16 = jnp.bfloat16


def nt(a, b):
    return lax.dot_general(a, b, (((1,), (1,)), ((), ())), preferred_element_type=F32)


def tn(a, b):
    return lax.dot_general(a, b, (((0,), (0,)), ((), ())), preferred_element_type=F32)


def place():
    outer = lax.axis_index("outer")
    inner = lax.axis_index("inner")
    z, c = outer // 2, outer % 2
    x, y = inner // NX, inner % NX
    za = z + 1 - 2 * (z % 2)
    zb = 3 - z
    return outer, inner, z, c, x, y, za, zb


def remote(src, dst, send, recv, dev):
    return pltpu.make_async_remote_copy(
        src_ref=src, dst_ref=dst, send_sem=send, recv_sem=recv, device_id=dev, device_id_type=MESH
    )


def greet(partners):
    barrier = pltpu.get_barrier_semaphore()
    for dev in partners:
        pl.semaphore_signal(barrier, inc=1, device_id=dev, device_id_type=MESH)
    pl.semaphore_wait(barrier, len(partners))


def pick(g, even, odd):
    return even + g * (odd - even)


def roads(g):
    outer, inner, z, c, x, y, za, zb = place()

    def along_x(j):
        return lax.rem(x + j, NX) * NX + y

    def along_y(j):
        return x * NX + lax.rem(y + j, NX)

    plane_q = {"outer": pick(g, za, zb) * 2 + c, "inner": inner}
    plane_kv = {"outer": pick(g, zb, za) * 2 + c, "inner": inner}

    def ring_q(j):
        return {"outer": outer, "inner": pick(g, along_x(j), along_y(j))}

    def ring_kv(j):
        return {"outer": outer, "inner": pick(g, along_y(j), along_x(j))}

    def at_q(j=0):
        return lax.rem(pick(g, x, y) + j, NX)

    def at_kv(j=0):
        return lax.rem(pick(g, y, x) + j, NX)

    return plane_q, plane_kv, ring_q, ring_kv, at_q, at_kv


def gather_kernel(
    heads, q_ref, k_ref, v_ref, qg, kvg,
    loc_sem, zkv_s, zkv_r, zq_s, zq_r, kv_s, kv_r, q_s, q_r, c_s, c_r,
):
    outer, inner, z, c, x, y, za, zb = place()
    dev_c = {"outer": z * 2 + 1 - c, "inner": inner}
    first_heads = (heads + 1) // 2
    groups = (0, 1)
    cols = (pl.ds(0, first_heads * D), pl.ds(first_heads * D, (heads - first_heads) * D))
    ways = [roads(g) for g in groups]

    def local(g):
        at, at_q, at_kv = cols[g], ways[g][4], ways[g][5]
        return (
            pltpu.make_async_copy(k_ref.at[:, at], kvg.at[0, 0, 0, at_kv(), :, at], loc_sem.at[0, g]),
            pltpu.make_async_copy(v_ref.at[:, at], kvg.at[1, 0, 0, at_kv(), :, at], loc_sem.at[1, g]),
            pltpu.make_async_copy(q_ref.at[:, at], qg.at[at_q(), 0, :, at], loc_sem.at[2, g]),
        )

    def z_kv(g):
        here, at = ways[g][5](), cols[g]
        return remote(
            kvg.at[:, 0, 0, here, :, at], kvg.at[:, 0, 1, here, :, at], zkv_s.at[g], zkv_r.at[g], ways[g][1]
        )

    def z_q(g):
        here, at = ways[g][4](), cols[g]
        return remote(qg.at[here, 0, :, at], qg.at[here, 1, :, at], zq_s.at[g], zq_r.at[g], ways[g][0])

    def kv_own(g, zr, way):
        block = kvg.at[:, 0, zr, ways[g][5](), :, cols[g]]
        return remote(block, block, kv_s.at[g, zr, way], kv_r.at[g, zr, way], ways[g][3](1 + 2 * way))

    def kv_on(g, zr, way):
        block = kvg.at[way, 0, zr, ways[g][5](3 - 2 * way), :, cols[g]]
        return remote(block, block, kv_s.at[g, zr, 2 + way], kv_r.at[g, zr, 2 + way], ways[g][3](1 + 2 * way))

    def q_own(g, zr, way):
        block = qg.at[ways[g][4](), zr, :, cols[g]]
        return remote(block, block, q_s.at[g, zr, way], q_r.at[g, zr, way], ways[g][2](1 + 2 * way))

    def q_on(g, zr, way):
        block = qg.at[ways[g][4](3 - 2 * way), zr, pl.ds(way * (R // 2), R // 2), cols[g]]
        return remote(block, block, q_s.at[g, zr, 2 + way], q_r.at[g, zr, 2 + way], ways[g][2](1 + 2 * way))

    def c_kv(g, zr):
        at = cols[g]
        return remote(
            kvg.at[:, 0, zr, :, :, at], kvg.at[:, 1, zr, :, :, at], c_s.at[g, zr], c_r.at[g, zr], dev_c
        )

    def pass_on_kv(zr):
        for g in groups:
            for way in (0, 1):
                kv_own(g, zr, way).wait_recv()
                kv_on(g, zr, way).start()

    def pass_on_q(zr):
        for g in groups:
            for way in (0, 1):
                q_own(g, zr, way).wait_recv()
                q_on(g, zr, way).start()

    def swap_cores(zr):
        for g in groups:
            for way in (0, 1):
                kv_on(g, zr, way).wait_recv()
            c_kv(g, zr).start()

    for g in groups:
        for copy in local(g):
            copy.start()
    plane_q, plane_kv, ring_q, ring_kv, _, _ = ways[0]
    greet([plane_q, plane_kv, dev_c] + [ring_q(j) for j in (1, 3)] + [ring_kv(j) for j in (1, 3)])
    for g in groups:
        for copy in local(g):
            copy.wait()
        z_q(g).start()
        z_kv(g).start()
    for g in groups:
        for way in (0, 1):
            kv_own(g, 0, way).start()
        for way in (0, 1):
            q_own(g, 0, way).start()
    pass_on_kv(0)
    pass_on_q(0)
    swap_cores(0)
    for g in groups:
        z_q(g).wait_recv()
        for way in (0, 1):
            q_own(g, 1, way).start()
    pass_on_q(1)
    for g in groups:
        z_kv(g).wait_recv()
        for way in (0, 1):
            kv_own(g, 1, way).start()
    pass_on_kv(1)
    swap_cores(1)
    for g in groups:
        for zr in (0, 1):
            for way in (0, 1):
                q_on(g, zr, way).wait_recv()
            c_kv(g, zr).wait_recv()
    for g in groups:
        z_kv(g).wait_send()
        z_q(g).wait_send()
        for zr in (0, 1):
            for way in (0, 1):
                kv_own(g, zr, way).wait_send()
                kv_on(g, zr, way).wait_send()
                q_own(g, zr, way).wait_send()
                q_on(g, zr, way).wait_send()
            c_kv(g, zr).wait_send()


def attend_kernel(heads, slot_ref, doc_ref, qg, kvg, op, bias):
    outer, inner, z, c, x, y, za, zb = place()
    ends = [doc_ref[0]]
    for n in range(1, doc_ref.shape[0]):
        ends.append(ends[-1] + doc_ref[n])

    def doc_start(slot):
        start = jnp.int32(0)
        for end in ends:
            start = jnp.where(slot >= end, end, start)
        return start

    lane = lax.broadcasted_iota(jnp.int32, (8, NQ), 1)
    part = lane // BLK
    down = lax.broadcasted_iota(jnp.int32, (8, NQ), 0)

    def build_mask(g):
        q_pos = jnp.zeros((8, NQ), jnp.int32)
        q_low = jnp.zeros((8, NQ), jnp.int32)
        for t in range(NQ // BLK):
            rt, zt, half = t // 4, (t // 2) % 2, t % 2
            zq = z if zt == 0 else (zb if g else za)
            iq = x * NX + rt if g else rt * NX + y
            slot = slot_ref[2 * ((zq * 2 + c) * 16 + iq) + half]
            hit = part == t
            q_pos = jnp.where(hit, slot * BLK, q_pos)
            q_low = jnp.where(hit, doc_start(slot) * BLK, q_low)
        q_pos = q_pos + lane % BLK

        def mask(t, carry):
            ct, zt, rt, half = t // 16, (t // 8) % 2, (t // 2) % 4, t % 2
            zk = z + zt * ((za if g else zb) - z)
            ck = c + ct * (1 - 2 * c)
            ik = rt * NX + y if g else x * NX + rt
            slot = slot_ref[2 * ((zk * 2 + ck) * 16 + ik) + half]
            for row in range(0, BLK, 8):
                k_pos = down + (slot * BLK + row)
                seen = (k_pos <= q_pos) & (k_pos >= q_low)
                at = t * BLK + row
                bias[g, pl.ds(pl.multiple_of(at, 8), 8), :] = jnp.where(seen, 0.0, HIDE)
            return carry

        lax.fori_loop(0, NK // BLK, mask, 0)

    build_mask(0)
    build_mask(1)

    def attend(h, carry):
        at = pl.ds(pl.multiple_of(h * D, D), D)
        queries = qg[:, :, :, at].reshape(NQ, D)
        keys = kvg[0, :, :, :, :, at].reshape(NK, D)
        values = kvg[1, :, :, :, :, at].reshape(NK, D)
        width = 256
        for tile in range(NQ // width):
            cols = slice(tile * width, (tile + 1) * width)
            scaled = nt(keys, queries[cols]) * SCALE2 + bias[h // ((heads + 1) // 2), :, cols]
            top = jnp.max(scaled, axis=0, keepdims=True)
            top = jnp.maximum(top, FLOOR).astype(BF16).astype(F32)
            terms = jnp.exp2(scaled - top)
            total = jnp.sum(terms, axis=0, keepdims=True)
            result = tn(values, terms.astype(BF16)).astype(BF16)
            total_hi = total.astype(BF16).astype(F32)
            row = lax.broadcasted_iota(jnp.int32, (STAT, width), 0)
            stats = jnp.where(row == 0, top, jnp.where(row == 1, total_hi, total - total_hi)).astype(BF16)
            for n in range(width // D):
                target = tile * (width // D) + n
                op[target, h, 0:D, :] = result[:, n * D : (n + 1) * D]
                op[target, h, D : D + STAT, :] = stats[:, n * D : (n + 1) * D]
        return carry

    lax.fori_loop(0, heads, attend, 0)


def reduce_kernel(heads, op, out_ref, orecv, own, zs, zr_buf, o_s, o_r, zo_s, zo_r):
    outer, inner, z, c, x, y, za, zb = place()
    first_heads = (heads + 1) // 2
    groups = (0, 1)
    of = (pl.ds(0, first_heads), pl.ds(first_heads, heads - first_heads))

    def ring_o(g, j):
        _, _, ring_q, _, at_q, _ = roads(g)
        return remote(
            op.at[at_q(j), of[g]], orecv.at[j - 1, of[g]], o_s.at[g, j - 1], o_r.at[g, j - 1], ring_q(j)
        )

    def z_o(h):
        return remote(zs.at[h], zr_buf.at[h], zo_s.at[h], zo_r.at[h], roads(h // first_heads)[0])

    plane_q, plane_kv, ring_q, ring_kv, _, _ = roads(0)
    greet([plane_q, plane_kv] + [ring_q(j) for j in (1, 2, 3)] + [ring_kv(j) for j in (1, 2, 3)])
    for j in (1, 3, 2):
        for g in groups:
            ring_o(g, j).start()
    for j in (1, 3, 2):
        for g in groups:
            ring_o(g, j).wait_recv()

    left = lax.broadcasted_iota(jnp.int32, (8, D), 1) < R

    def unstat(block):
        stat = block.astype(F32)
        return (
            jnp.broadcast_to(stat[0:1], (8, D)),
            jnp.broadcast_to(stat[1:2] + stat[2:3], (8, D)),
        )

    def swap_half(a):
        return pltpu.roll(a, R, axis=1)

    def merge_x(h, carry):
        here = roads(h // first_heads)[4]()
        parts = [(op[here, h, 0:D, :], op[here, h, D : D + STAT, :])]
        for j in (1, 2, 3):
            parts.append((orecv[j - 1, h, 0:D, :], orecv[j - 1, h, D : D + STAT, :]))
        stats = [unstat(p[1]) for p in parts]
        top = functools.reduce(jnp.maximum, [s[0] for s in stats])
        total = jnp.zeros((8, D), F32)
        result = jnp.zeros((D, D), F32)
        for (block, _), (m, l) in zip(parts, stats):
            w = jnp.exp2(m - top)
            total = total + w * l
            result = result + block.astype(F32) * w[0:1]
        low, high = result[0:R], result[R:D]
        mine = jnp.where(left[0:1], low, swap_half(high))
        other = jnp.where(left[0:1], swap_half(low), high)
        top_swapped, total_swapped = swap_half(top), swap_half(total)
        own[h, 0:R, :] = mine
        own[h, R : R + 8, :] = jnp.where(left, top, top_swapped)
        own[h, R + 8 : R + 16, :] = jnp.where(left, total, total_swapped)
        m_other = jnp.where(left, top_swapped, top)[0:1]
        l_other = jnp.where(left, total_swapped, total)[0:1]
        l_hi = l_other.astype(BF16).astype(F32)
        row = lax.broadcasted_iota(jnp.int32, (STAT, D), 0)
        zs[h, 0:R, :] = other.astype(BF16)
        zs[h, R : R + STAT, :] = jnp.where(
            row == 0, m_other, jnp.where(row == 1, l_hi, l_other - l_hi)
        ).astype(BF16)
        z_o(h).start()
        return carry

    lax.fori_loop(0, heads, merge_x, 0)

    def finish(h, carry):
        z_o(h).wait_recv()
        m_far, l_far = unstat(zr_buf[h, R : R + STAT, :])
        m_own, l_own = own[h, R : R + 8, :], own[h, R + 8 : R + 16, :]
        top = jnp.maximum(m_far, m_own)
        w_far, w_own = jnp.exp2(m_far - top), jnp.exp2(m_own - top)
        total = w_far * l_far + w_own * l_own
        w_far, w_own = w_far / total, w_own / total
        packed = own[h, 0:R, :] * w_own[0:1] + zr_buf[h, 0:R, :].astype(F32) * w_far[0:1]
        tall = jnp.concatenate([packed, swap_half(packed)], axis=0)
        out_ref[:, pl.ds(pl.multiple_of(h * D, D), D)] = tall.T[0:R].astype(BF16)
        z_o(h).wait_send()
        return carry

    lax.fori_loop(0, heads, finish, 0)
    for j in (1, 3, 2):
        for g in groups:
            ring_o(g, j).wait_send()


def per_device(queries, keys, values, slot_blocks, doc_blocks):
    width = queries.shape[1]
    heads = width // D
    dma = pltpu.SemaphoreType.DMA
    anywhere = pl.BlockSpec(memory_space=pl.ANY)
    vmem = pl.BlockSpec(memory_space=pltpu.VMEM)
    scalars = pl.BlockSpec(memory_space=pltpu.SMEM)
    limit = 24 * 1024 * 1024
    gathered_q, gathered_kv = pl.pallas_call(
        functools.partial(gather_kernel, heads),
        out_shape=(
            jax.ShapeDtypeStruct((NX, NZ, R, width), BF16),
            jax.ShapeDtypeStruct((2, NC, NZ, NX, R, width), BF16),
        ),
        in_specs=[anywhere] * 3,
        out_specs=(vmem, vmem),
        scratch_shapes=[
            dma((3, 2)), dma((2,)), dma((2,)), dma((2,)), dma((2,)),
            dma((2, 2, 4)), dma((2, 2, 4)), dma((2, 2, 4)), dma((2, 2, 4)), dma((2, 2)), dma((2, 2)),
        ],
        compiler_params=pltpu.CompilerParams(collective_id=0, has_side_effects=True, vmem_limit_bytes=limit),
        name="gather",
    )(queries, keys, values)
    partial = pl.pallas_call(
        functools.partial(attend_kernel, heads),
        out_shape=jax.ShapeDtypeStruct((NX, heads, D + STAT, D), BF16),
        in_specs=[scalars, scalars, vmem, vmem],
        out_specs=vmem,
        scratch_shapes=[pltpu.VMEM((2, NK, NQ), F32)],
        compiler_params=pltpu.CompilerParams(vmem_limit_bytes=limit),
        name="attend",
    )(slot_blocks, doc_blocks, gathered_q, gathered_kv)
    return pl.pallas_call(
        functools.partial(reduce_kernel, heads),
        out_shape=jax.ShapeDtypeStruct(queries.shape, BF16),
        in_specs=[vmem],
        out_specs=vmem,
        scratch_shapes=[
            pltpu.VMEM((NX - 1, heads, D + STAT, D), BF16),
            pltpu.VMEM((heads, R + 16, D), F32),
            pltpu.VMEM((heads, R + STAT, D), BF16),
            pltpu.VMEM((heads, R + STAT, D), BF16),
            dma((2, 3)), dma((2, 3)), dma((heads,)), dma((heads,)),
        ],
        compiler_params=pltpu.CompilerParams(collective_id=1, has_side_effects=True, vmem_limit_bytes=limit),
        name="reduce",
    )(partial)


def solution(mesh):
    rows = P(("outer", "inner"), "head")
    return jax.shard_map(
        per_device,
        mesh=mesh,
        in_specs=(rows, rows, rows, P(), P()),
        out_specs=rows,
        check_vma=False,
    )
```

```python
import functools
import math

import jax
import jax.numpy as jnp
from jax import lax
from jax.experimental import pallas as pl
from jax.experimental.pallas import tpu as pltpu
from jax.sharding import PartitionSpec as P

D = 128
BLK = 32
R = 64
NX = 4
NZ = 2
NC = 2
NQ = NX * NZ * R
NK = NC * NZ * NX * R
STAT = 16
SCALE2 = D ** (-0.5) * math.log2(math.e)
HIDE = -1e30
FLOOR = -1e29
MESH = pl.DeviceIdType.MESH
F32 = jnp.float32
BF16 = jnp.bfloat16


def nt(a, b):
    return lax.dot_general(a, b, (((1,), (1,)), ((), ())), preferred_element_type=F32)


def tn(a, b):
    return lax.dot_general(a, b, (((0,), (0,)), ((), ())), preferred_element_type=F32)


def kernel(
    heads,
    q_ref, k_ref, v_ref, slot_hbm, doc_hbm, out_ref,
    slot_ref, doc_ref, qg, kvg, bias, half_o, half_stat, op, orecv, own, zs, zr_buf, out_buf,
    tab_sem, loc_sem, zkv_s, zkv_r, zq_s, zq_r, kv_s, kv_r, q_s, q_r, c_s, c_r, o_s, o_r, zo_s, zo_r, out_sem,
):
    outer = lax.axis_index("outer")
    inner = lax.axis_index("inner")
    z, c = outer // 2, outer % 2
    x, y = inner // NX, inner % NX
    za = z + 1 - 2 * (z % 2)
    zb = 3 - z
    dev_c = {"outer": z * 2 + 1 - c, "inner": inner}
    first_heads = (heads + 1) // 2
    groups = (0, 1)
    of = (pl.ds(0, first_heads), pl.ds(first_heads, heads - first_heads))

    def pick(g, even, odd):
        return even + g * (odd - even)

    def group_of(h):
        return h // first_heads

    def plane_q(g):
        return {"outer": pick(g, za, zb) * 2 + c, "inner": inner}

    def plane_kv(g):
        return {"outer": pick(g, zb, za) * 2 + c, "inner": inner}

    def along_x(j):
        return lax.rem(x + j, NX) * NX + y

    def along_y(j):
        return x * NX + lax.rem(y + j, NX)

    def ring_q(g, j):
        return {"outer": outer, "inner": pick(g, along_x(j), along_y(j))}

    def ring_kv(g, j):
        return {"outer": outer, "inner": pick(g, along_y(j), along_x(j))}

    def at_q(g, j=0):
        return lax.rem(pick(g, x, y) + j, NX)

    def at_kv(g, j=0):
        return lax.rem(pick(g, y, x) + j, NX)

    tables = (
        pltpu.make_async_copy(slot_hbm, slot_ref, tab_sem.at[0]),
        pltpu.make_async_copy(doc_hbm, doc_ref, tab_sem.at[1]),
    )

    def local(h):
        at = pl.ds(h * D, D)
        g = group_of(h)
        return (
            pltpu.make_async_copy(q_ref.at[:, at], qg.at[at_q(g), 0, h], loc_sem.at[2, h]),
            pltpu.make_async_copy(k_ref.at[:, at], kvg.at[0, 0, 0, at_kv(g), h], loc_sem.at[0, h]),
            pltpu.make_async_copy(v_ref.at[:, at], kvg.at[1, 0, 0, at_kv(g), h], loc_sem.at[1, h]),
        )

    for h in range(heads):
        for copy in local(h):
            copy.start()
    for copy in tables:
        copy.start()

    barrier = pltpu.get_barrier_semaphore()
    partners = [plane_q(0), plane_kv(0), dev_c]
    partners += [ring_q(0, j) for j in (1, 2, 3)] + [ring_kv(0, j) for j in (1, 2, 3)]
    for dev in partners:
        pl.semaphore_signal(barrier, inc=1, device_id=dev, device_id_type=MESH)
    pl.semaphore_wait(barrier, len(partners))

    def remote(src, dst, send, recv, dev):
        return pltpu.make_async_remote_copy(
            src_ref=src, dst_ref=dst, send_sem=send, recv_sem=recv, device_id=dev, device_id_type=MESH
        )

    def z_kv(g):
        here = at_kv(g)
        return remote(
            kvg.at[:, 0, 0, here, of[g]], kvg.at[:, 0, 1, here, of[g]], zkv_s.at[g], zkv_r.at[g], plane_kv(g)
        )

    def z_q(g):
        here = at_q(g)
        return remote(qg.at[here, 0, of[g]], qg.at[here, 1, of[g]], zq_s.at[g], zq_r.at[g], plane_q(g))

    def r_kv(g, zr, j):
        block = kvg.at[:, 0, zr, at_kv(g), of[g]]
        return remote(block, block, kv_s.at[g, zr, j - 1], kv_r.at[g, zr, j - 1], ring_kv(g, j))

    def r_q(g, zr, j):
        block = qg.at[at_q(g), zr, of[g]]
        return remote(block, block, q_s.at[g, zr, j - 1], q_r.at[g, zr, j - 1], ring_q(g, j))

    def c_kv(g, zr):
        return remote(
            kvg.at[:, 0, zr, :, of[g]], kvg.at[:, 1, zr, :, of[g]], c_s.at[g, zr], c_r.at[g, zr], dev_c
        )

    def ring_o(h, j):
        g = group_of(h)
        return remote(
            op.at[h, at_q(g, j)], orecv.at[h, j - 1], o_s.at[h, j - 1], o_r.at[h, j - 1], ring_q(g, j)
        )

    def z_o(h):
        return remote(zs.at[h], zr_buf.at[h], zo_s.at[h], zo_r.at[h], plane_q(group_of(h)))

    def out_copy(h):
        return pltpu.make_async_copy(
            out_buf.at[h], out_ref.at[:, pl.ds(pl.multiple_of(h * D, D), D)], out_sem.at[h]
        )

    for h in range(heads):
        for copy in local(h):
            copy.wait()
    for g in groups:
        z_q(g).start()
        z_kv(g).start()
    for j in (1, 3, 2):
        for g in groups:
            r_kv(g, 0, j).start()
            r_q(g, 0, j).start()
    for copy in tables:
        copy.wait()

    ends = [doc_ref[0]]
    for n in range(1, doc_ref.shape[0]):
        ends.append(ends[-1] + doc_ref[n])

    def doc_start(slot):
        start = jnp.int32(0)
        for end in ends:
            start = jnp.where(slot >= end, end, start)
        return start

    lane = lax.broadcasted_iota(jnp.int32, (8, NQ), 1)
    down = lax.broadcasted_iota(jnp.int32, (8, NQ), 0)
    part = lane // BLK

    def build_mask(g):
        q_pos = jnp.zeros((8, NQ), jnp.int32)
        q_low = jnp.zeros((8, NQ), jnp.int32)
        for t in range(NQ // BLK):
            rt, zt, half = t // 4, (t // 2) % 2, t % 2
            zq = z if zt == 0 else (zb if g else za)
            iq = x * NX + rt if g else rt * NX + y
            slot = slot_ref[2 * ((zq * 2 + c) * 16 + iq) + half]
            hit = part == t
            q_pos = jnp.where(hit, slot * BLK, q_pos)
            q_low = jnp.where(hit, doc_start(slot) * BLK, q_low)
        q_pos = q_pos + lane % BLK

        def mask(t, carry):
            ct, zt, rt, half = t // 16, (t // 8) % 2, (t // 2) % 4, t % 2
            zk = z + zt * ((za if g else zb) - z)
            ck = c + ct * (1 - 2 * c)
            ik = rt * NX + y if g else x * NX + rt
            slot = slot_ref[2 * ((zk * 2 + ck) * 16 + ik) + half]
            for row in range(0, BLK, 8):
                k_pos = down + (slot * BLK + row)
                seen = (k_pos <= q_pos) & (k_pos >= q_low)
                at = (zt * 2 + ct) * (NX * R) + rt * R + half * BLK + row
                bias[g, pl.ds(pl.multiple_of(at, 8), 8), :] = jnp.where(seen, 0.0, HIDE)
            return carry

        lax.fori_loop(0, NK // BLK, mask, 0)

    def swap_cores(zr):
        for g in (1, 0):
            for j in (1, 3, 2):
                r_kv(g, zr, j).wait_recv()
            c_kv(g, zr).start()

    def attend(h, zr):
        g = group_of(h)
        count = NK // NZ
        keys = kvg[0, :, zr, :, h].reshape(count, D)
        values = kvg[1, :, zr, :, h].reshape(count, D)
        width = 256
        each = width // D
        for tile in range(NQ // width):
            span = slice(tile * width, (tile + 1) * width)
            queries = qg[tile * each : (tile + 1) * each, :, h].reshape(width, D)
            scaled = nt(keys, queries) * SCALE2 + bias[g, zr * count : (zr + 1) * count, span]
            top = jnp.max(scaled, axis=0, keepdims=True)
            top = jnp.maximum(top, FLOOR).astype(BF16).astype(F32)
            if zr:
                before = half_stat[h, 0:1, span]
                top = jnp.maximum(top, before)
            terms = jnp.exp2(scaled - top)
            total = jnp.sum(terms, axis=0, keepdims=True)
            result = tn(values, terms.astype(BF16))
            if not zr:
                half_stat[h, 0:1, span] = top
                half_stat[h, 1:2, span] = total
                half_o[h, :, span] = result
                continue
            shrink = jnp.exp2(before - top)
            total = total + half_stat[h, 1:2, span] * shrink
            result = (result + half_o[h, :, span] * shrink).astype(BF16)
            total_hi = total.astype(BF16).astype(F32)
            row = lax.broadcasted_iota(jnp.int32, (STAT, width), 0)
            stats = jnp.where(row == 0, top, jnp.where(row == 1, total_hi, total - total_hi)).astype(BF16)
            for n in range(each):
                op[h, tile * each + n, 0:D, :] = result[:, n * D : (n + 1) * D]
                op[h, tile * each + n, D : D + STAT, :] = stats[:, n * D : (n + 1) * D]

    left = lax.broadcasted_iota(jnp.int32, (8, D), 1) < R

    def unstat(block):
        stat = block.astype(F32)
        return (
            jnp.broadcast_to(stat[0:1], (8, D)),
            jnp.broadcast_to(stat[1:2] + stat[2:3], (8, D)),
        )

    def swap_half(a):
        return pltpu.roll(a, R, axis=1)

    def merge_ring(h):
        for j in (1, 3, 2):
            ring_o(h, j).wait_recv()
        here = at_q(group_of(h))
        parts = [(op[h, here, 0:D, :], op[h, here, D : D + STAT, :])]
        for j in (1, 2, 3):
            parts.append((orecv[h, j - 1, 0:D, :], orecv[h, j - 1, D : D + STAT, :]))
        stats = [unstat(p[1]) for p in parts]
        top = functools.reduce(jnp.maximum, [s[0] for s in stats])
        total = jnp.zeros((8, D), F32)
        result = jnp.zeros((D, D), F32)
        for (block, _), (m, l) in zip(parts, stats):
            w = jnp.exp2(m - top)
            total = total + w * l
            result = result + block.astype(F32) * w[0:1]
        low, high = result[0:R], result[R:D]
        mine = jnp.where(left[0:1], low, swap_half(high))
        other = jnp.where(left[0:1], swap_half(low), high)
        top_swapped, total_swapped = swap_half(top), swap_half(total)
        own[h, 0:R, :] = mine
        own[h, R : R + 8, :] = jnp.where(left, top, top_swapped)
        own[h, R + 8 : R + 16, :] = jnp.where(left, total, total_swapped)
        m_other = jnp.where(left, top_swapped, top)[0:1]
        l_other = jnp.where(left, total_swapped, total)[0:1]
        l_hi = l_other.astype(BF16).astype(F32)
        row = lax.broadcasted_iota(jnp.int32, (STAT, D), 0)
        zs[h, 0:R, :] = other.astype(BF16)
        zs[h, R : R + STAT, :] = jnp.where(
            row == 0, m_other, jnp.where(row == 1, l_hi, l_other - l_hi)
        ).astype(BF16)
        z_o(h).start()

    def finish(h):
        z_o(h).wait_recv()
        m_far, l_far = unstat(zr_buf[h, R : R + STAT, :])
        m_own, l_own = own[h, R : R + 8, :], own[h, R + 8 : R + 16, :]
        top = jnp.maximum(m_far, m_own)
        w_far, w_own = jnp.exp2(m_far - top), jnp.exp2(m_own - top)
        total = w_far * l_far + w_own * l_own
        w_far, w_own = w_far / total, w_own / total
        packed = own[h, 0:R, :] * w_own[0:1] + zr_buf[h, 0:R, :].astype(F32) * w_far[0:1]
        tall = jnp.concatenate([packed, swap_half(packed)], axis=0)
        out_buf[h] = tall.T[0:R].astype(BF16)
        out_copy(h).start()

    build_mask(0)
    build_mask(1)
    swap_cores(0)
    for g in groups:
        z_q(g).wait_recv()
        for j in (1, 3, 2):
            r_q(g, 1, j).start()
    for g in (1, 0):
        z_kv(g).wait_recv()
        for j in (1, 3, 2):
            r_kv(g, 1, j).start()
    for g in groups:
        for zr in (0, 1):
            for j in (1, 3, 2):
                r_q(g, zr, j).wait_recv()
        c_kv(g, 0).wait_recv()

    def early(i, carry):
        attend(i, 0)
        return carry

    lax.fori_loop(0, heads, early, 0)
    swap_cores(1)
    for g in (1, 0):
        c_kv(g, 1).wait_recv()

    def turn(i):
        return lax.rem((i + 1) * first_heads, heads)

    def late(i, carry):
        @pl.when(i < heads)
        def _():
            h = turn(i)
            attend(h, 1)
            for j in (1, 3, 2):
                ring_o(h, j).start()

        @pl.when((i >= 2) & (i < heads + 2))
        def _():
            merge_ring(turn(i - 2))

        @pl.when(i >= 5)
        def _():
            finish(turn(i - 5))

        return carry

    lax.fori_loop(0, heads + 5, late, 0)

    for g in groups:
        z_kv(g).wait_send()
        z_q(g).wait_send()
        for zr in (0, 1):
            for j in (1, 3, 2):
                r_kv(g, zr, j).wait_send()
                r_q(g, zr, j).wait_send()
            c_kv(g, zr).wait_send()

    def drain(h, carry):
        for j in (1, 2, 3):
            ring_o(h, j).wait_send()
        z_o(h).wait_send()
        out_copy(h).wait()
        return carry

    lax.fori_loop(0, heads, drain, 0)


def per_device(queries, keys, values, slot_blocks, doc_blocks):
    width = queries.shape[1]
    heads = width // D
    dma = pltpu.SemaphoreType.DMA
    anywhere = pl.BlockSpec(memory_space=pltpu.HBM)
    return pl.pallas_call(
        functools.partial(kernel, heads),
        out_shape=jax.ShapeDtypeStruct(queries.shape, BF16),
        in_specs=[anywhere] * 5,
        out_specs=anywhere,
        scratch_shapes=[
            pltpu.SMEM(slot_blocks.shape, jnp.int32),
            pltpu.SMEM(doc_blocks.shape, jnp.int32),
            pltpu.VMEM((NX, NZ, heads, R, D), BF16),
            pltpu.VMEM((2, NC, NZ, NX, heads, R, D), BF16),
            pltpu.VMEM((2, NK, NQ), F32),
            pltpu.VMEM((heads, D, NQ), F32),
            pltpu.VMEM((heads, 8, NQ), F32),
            pltpu.VMEM((heads, NX, D + STAT, D), BF16),
            pltpu.VMEM((heads, NX - 1, D + STAT, D), BF16),
            pltpu.VMEM((heads, R + 16, D), F32),
            pltpu.VMEM((heads, R + STAT, D), BF16),
            pltpu.VMEM((heads, R + STAT, D), BF16),
            pltpu.VMEM((heads, R, D), BF16),
            dma((2,)),
            dma((3, heads)),
            dma((2,)), dma((2,)), dma((2,)), dma((2,)),
            dma((2, 2, 3)), dma((2, 2, 3)), dma((2, 2, 3)), dma((2, 2, 3)),
            dma((2, 2)), dma((2, 2)),
            dma((heads, 3)), dma((heads, 3)),
            dma((heads,)), dma((heads,)), dma((heads,)),
        ],
        compiler_params=pltpu.CompilerParams(
            collective_id=0, has_side_effects=True, vmem_limit_bytes=64 * 1024 * 1024
        ),
        cost_estimate=pl.CostEstimate(
            flops=4 * heads * NQ * NK * D, bytes_accessed=4 * queries.size * 2, transcendentals=heads * NQ * NK
        ),
    )(queries, keys, values, slot_blocks, doc_blocks)


def solution(mesh):
    rows = P(("outer", "inner"), "head")
    return jax.shard_map(
        per_device,
        mesh=mesh,
        in_specs=(rows, rows, rows, P(), P()),
        out_specs=rows,
        check_vma=False,
    )
```

```python
import functools
import math

import jax
import jax.numpy as jnp
from jax import lax
from jax.experimental import pallas as pl
from jax.experimental.pallas import tpu as pltpu
from jax.sharding import PartitionSpec as P

D = 128
BLK = 32
R = 64
NX = 4
NZ = 2
NC = 2
NQ = NX * NZ * R
NK = NC * NZ * NX * R
STAT = 16
SCALE2 = D ** (-0.5) * math.log2(math.e)
HIDE = -1e30
FLOOR = -1e29
MESH = pl.DeviceIdType.MESH
F32 = jnp.float32
BF16 = jnp.bfloat16


def nt(a, b):
    return lax.dot_general(a, b, (((1,), (1,)), ((), ())), preferred_element_type=F32)


def tn(a, b):
    return lax.dot_general(a, b, (((0,), (0,)), ((), ())), preferred_element_type=F32)


def kernel(
    heads,
    q_ref, k_ref, v_ref, slot_hbm, doc_hbm, out_ref,
    slot_ref, doc_ref, qg, kvg, bias, half_o, half_stat, op, orecv, own, zs, zr_buf, out_buf,
    tab_sem, loc_sem, zkv_s, zkv_r, zq_s, zq_r, kv_s, kv_r, q_s, q_r, c_s, c_r, o_s, o_r, zo_s, zo_r, out_sem,
):
    outer = lax.axis_index("outer")
    inner = lax.axis_index("inner")
    z, c = outer // 2, outer % 2
    x, y = inner // NX, inner % NX
    za = z + 1 - 2 * (z % 2)
    zb = 3 - z
    dev_c = {"outer": z * 2 + 1 - c, "inner": inner}
    first_heads = (heads + 1) // 2
    counts = (first_heads, heads - first_heads)

    def pick(g, even, odd):
        return even + g * (odd - even)

    def group_of(h):
        return h // first_heads

    def plane_q(g):
        return {"outer": pick(g, za, zb) * 2 + c, "inner": inner}

    def plane_kv(g):
        return {"outer": pick(g, zb, za) * 2 + c, "inner": inner}

    def along_x(j):
        return lax.rem(x + j, NX) * NX + y

    def along_y(j):
        return x * NX + lax.rem(y + j, NX)

    def ring_q(g, j):
        return {"outer": outer, "inner": pick(g, along_x(j), along_y(j))}

    def ring_kv(g, j):
        return {"outer": outer, "inner": pick(g, along_y(j), along_x(j))}

    def at_q(g, j=0):
        return lax.rem(pick(g, x, y) + j, NX)

    def at_kv(g, j=0):
        return lax.rem(pick(g, y, x) + j, NX)

    tables = (
        pltpu.make_async_copy(slot_hbm, slot_ref, tab_sem.at[0]),
        pltpu.make_async_copy(doc_hbm, doc_ref, tab_sem.at[1]),
    )

    def local(h):
        at = pl.ds(h * D, D)
        g = group_of(h)
        return (
            pltpu.make_async_copy(q_ref.at[:, at], qg.at[at_q(g), 0, h], loc_sem.at[2, h]),
            pltpu.make_async_copy(k_ref.at[:, at], kvg.at[0, 0, 0, at_kv(g), h], loc_sem.at[0, h]),
            pltpu.make_async_copy(v_ref.at[:, at], kvg.at[1, 0, 0, at_kv(g), h], loc_sem.at[1, h]),
        )

    for w in range(first_heads):
        for h in (w, first_heads + w):
            if h < heads:
                for copy in local(h):
                    copy.start()
    for copy in tables:
        copy.start()

    barrier = pltpu.get_barrier_semaphore()
    partners = [plane_q(0), plane_kv(0), dev_c]
    partners += [ring_q(0, j) for j in (1, 2, 3)] + [ring_kv(0, j) for j in (1, 2, 3)]
    for dev in partners:
        pl.semaphore_signal(barrier, inc=1, device_id=dev, device_id_type=MESH)
    pl.semaphore_wait(barrier, len(partners))

    def remote(src, dst, send, recv, dev):
        return pltpu.make_async_remote_copy(
            src_ref=src, dst_ref=dst, send_sem=send, recv_sem=recv, device_id=dev, device_id_type=MESH
        )

    def z_kv(h):
        g = group_of(h)
        here = at_kv(g)
        return remote(
            kvg.at[:, 0, 0, here, h], kvg.at[:, 0, 1, here, h], zkv_s.at[h], zkv_r.at[h], plane_kv(g)
        )

    def z_q(h):
        g = group_of(h)
        here = at_q(g)
        return remote(qg.at[here, 0, h], qg.at[here, 1, h], zq_s.at[h], zq_r.at[h], plane_q(g))

    def r_kv(h, zr, j):
        g = group_of(h)
        block = kvg.at[:, 0, zr, at_kv(g), h]
        return remote(block, block, kv_s.at[h, zr, j - 1], kv_r.at[h, zr, j - 1], ring_kv(g, j))

    def r_q(h, zr, j):
        g = group_of(h)
        block = qg.at[at_q(g), zr, h]
        return remote(block, block, q_s.at[h, zr, j - 1], q_r.at[h, zr, j - 1], ring_q(g, j))

    def c_kv(h, zr):
        return remote(kvg.at[:, 0, zr, :, h], kvg.at[:, 1, zr, :, h], c_s.at[h, zr], c_r.at[h, zr], dev_c)

    def ring_o(h, j):
        g = group_of(h)
        return remote(
            op.at[h, at_q(g, j)], orecv.at[h, j - 1], o_s.at[h, j - 1], o_r.at[h, j - 1], ring_q(g, j)
        )

    def z_o(h):
        return remote(zs.at[h], zr_buf.at[h], zo_s.at[h], zo_r.at[h], plane_q(group_of(h)))

    def out_copy(h):
        return pltpu.make_async_copy(
            out_buf.at[h], out_ref.at[:, pl.ds(pl.multiple_of(h * D, D), D)], out_sem.at[h]
        )

    order = [h for w in range(first_heads) for h in (w, first_heads + w) if h < heads]
    for h in order:
        for copy in local(h):
            copy.wait()
        z_q(h).start()
        z_kv(h).start()
        for j in (1, 3, 2):
            r_kv(h, 0, j).start()
            r_q(h, 0, j).start()
    for copy in tables:
        copy.wait()

    ends = [doc_ref[0]]
    for n in range(1, doc_ref.shape[0]):
        ends.append(ends[-1] + doc_ref[n])

    def doc_start(slot):
        start = jnp.int32(0)
        for end in ends:
            start = jnp.where(slot >= end, end, start)
        return start

    lane = lax.broadcasted_iota(jnp.int32, (8, NQ), 1)
    down = lax.broadcasted_iota(jnp.int32, (8, NQ), 0)
    part = lane // BLK

    def build_mask(g):
        q_pos = jnp.zeros((8, NQ), jnp.int32)
        q_low = jnp.zeros((8, NQ), jnp.int32)
        for t in range(NQ // BLK):
            rt, zt, half = t // 4, (t // 2) % 2, t % 2
            zq = z if zt == 0 else (zb if g else za)
            iq = x * NX + rt if g else rt * NX + y
            slot = slot_ref[2 * ((zq * 2 + c) * 16 + iq) + half]
            hit = part == t
            q_pos = jnp.where(hit, slot * BLK, q_pos)
            q_low = jnp.where(hit, doc_start(slot) * BLK, q_low)
        q_pos = q_pos + lane % BLK

        def mask(t, carry):
            ct, zt, rt, half = t // 16, (t // 8) % 2, (t // 2) % 4, t % 2
            zk = z + zt * ((za if g else zb) - z)
            ck = c + ct * (1 - 2 * c)
            ik = rt * NX + y if g else x * NX + rt
            slot = slot_ref[2 * ((zk * 2 + ck) * 16 + ik) + half]
            for row in range(0, BLK, 8):
                k_pos = down + (slot * BLK + row)
                seen = (k_pos <= q_pos) & (k_pos >= q_low)
                at = (zt * 2 + ct) * (NX * R) + rt * R + half * BLK + row
                bias[g, pl.ds(pl.multiple_of(at, 8), 8), :] = jnp.where(seen, 0.0, HIDE)
            return carry

        lax.fori_loop(0, NK // BLK, mask, 0)

    def swap_cores(h, zr):
        for j in (1, 3, 2):
            r_kv(h, zr, j).wait_recv()
        c_kv(h, zr).start()

    def spread_q(h):
        z_q(h).wait_recv()
        for j in (1, 3, 2):
            r_q(h, 1, j).start()

    def spread_kv(h):
        z_kv(h).wait_recv()
        for j in (1, 3, 2):
            r_kv(h, 1, j).start()

    def attend(h, zr):
        g = group_of(h)
        count = NK // NZ
        keys = kvg[0, :, zr, :, h].reshape(count, D)
        values = kvg[1, :, zr, :, h].reshape(count, D)
        width = 256
        each = width // D
        for tile in range(NQ // width):
            span = slice(tile * width, (tile + 1) * width)
            queries = qg[tile * each : (tile + 1) * each, :, h].reshape(width, D)
            scaled = nt(keys, queries) * SCALE2 + bias[g, zr * count : (zr + 1) * count, span]
            top = jnp.max(scaled, axis=0, keepdims=True)
            top = jnp.maximum(top, FLOOR).astype(BF16).astype(F32)
            if zr:
                before = half_stat[h, 0:1, span]
                top = jnp.maximum(top, before)
            terms = jnp.exp2(scaled - top)
            total = jnp.sum(terms, axis=0, keepdims=True)
            result = tn(values, terms.astype(BF16))
            if not zr:
                half_stat[h, 0:1, span] = top
                half_stat[h, 1:2, span] = total
                half_o[h, :, span] = result
                continue
            shrink = jnp.exp2(before - top)
            total = total + half_stat[h, 1:2, span] * shrink
            result = (result + half_o[h, :, span] * shrink).astype(BF16)
            total_hi = total.astype(BF16).astype(F32)
            row = lax.broadcasted_iota(jnp.int32, (STAT, width), 0)
            stats = jnp.where(row == 0, top, jnp.where(row == 1, total_hi, total - total_hi)).astype(BF16)
            for n in range(each):
                op[h, tile * each + n, 0:D, :] = result[:, n * D : (n + 1) * D]
                op[h, tile * each + n, D : D + STAT, :] = stats[:, n * D : (n + 1) * D]

    left = lax.broadcasted_iota(jnp.int32, (8, D), 1) < R

    def unstat(block):
        stat = block.astype(F32)
        return (
            jnp.broadcast_to(stat[0:1], (8, D)),
            jnp.broadcast_to(stat[1:2] + stat[2:3], (8, D)),
        )

    def swap_half(a):
        return pltpu.roll(a, R, axis=1)

    def merge_ring(h):
        for j in (1, 3, 2):
            ring_o(h, j).wait_recv()
        here = at_q(group_of(h))
        parts = [(op[h, here, 0:D, :], op[h, here, D : D + STAT, :])]
        for j in (1, 2, 3):
            parts.append((orecv[h, j - 1, 0:D, :], orecv[h, j - 1, D : D + STAT, :]))
        stats = [unstat(p[1]) for p in parts]
        top = functools.reduce(jnp.maximum, [s[0] for s in stats])
        total = jnp.zeros((8, D), F32)
        result = jnp.zeros((D, D), F32)
        for (block, _), (m, l) in zip(parts, stats):
            w = jnp.exp2(m - top)
            total = total + w * l
            result = result + block.astype(F32) * w[0:1]
        low, high = result[0:R], result[R:D]
        mine = jnp.where(left[0:1], low, swap_half(high))
        other = jnp.where(left[0:1], swap_half(low), high)
        top_swapped, total_swapped = swap_half(top), swap_half(total)
        own[h, 0:R, :] = mine
        own[h, R : R + 8, :] = jnp.where(left, top, top_swapped)
        own[h, R + 8 : R + 16, :] = jnp.where(left, total, total_swapped)
        m_other = jnp.where(left, top_swapped, top)[0:1]
        l_other = jnp.where(left, total_swapped, total)[0:1]
        l_hi = l_other.astype(BF16).astype(F32)
        row = lax.broadcasted_iota(jnp.int32, (STAT, D), 0)
        zs[h, 0:R, :] = other.astype(BF16)
        zs[h, R : R + STAT, :] = jnp.where(
            row == 0, m_other, jnp.where(row == 1, l_hi, l_other - l_hi)
        ).astype(BF16)
        z_o(h).start()

    def finish(h):
        z_o(h).wait_recv()
        m_far, l_far = unstat(zr_buf[h, R : R + STAT, :])
        m_own, l_own = own[h, R : R + 8, :], own[h, R + 8 : R + 16, :]
        top = jnp.maximum(m_far, m_own)
        w_far, w_own = jnp.exp2(m_far - top), jnp.exp2(m_own - top)
        total = w_far * l_far + w_own * l_own
        w_far, w_own = w_far / total, w_own / total
        packed = own[h, 0:R, :] * w_own[0:1] + zr_buf[h, 0:R, :].astype(F32) * w_far[0:1]
        tall = jnp.concatenate([packed, swap_half(packed)], axis=0)
        out_buf[h] = tall.T[0:R].astype(BF16)
        out_copy(h).start()

    build_mask(0)
    build_mask(1)

    def early(h):
        for zr in (0, 1):
            for j in (1, 3, 2):
                r_q(h, zr, j).wait_recv()
        c_kv(h, 0).wait_recv()
        attend(h, 0)

    def late(h):
        c_kv(h, 1).wait_recv()
        attend(h, 1)
        for j in (1, 3, 2):
            ring_o(h, j).start()

    def wave(w, *works):
        def one(g, carry):
            h = g * first_heads + w
            for work in works:
                work(h)
            return carry

        @pl.when((w >= 0) & (w < first_heads))
        def _():
            lax.fori_loop(0, jnp.where(w < counts[1], 2, 1), one, 0)

    def step(s, carry):
        wave(s, lambda h: swap_cores(h, 0), spread_q)
        wave(s - 1, lambda h: swap_cores(h, 1))
        wave(s, spread_kv)
        wave(s - 2, merge_ring)
        wave(s - 1, late)
        wave(s, early)
        wave(s - 3, finish)
        return carry

    lax.fori_loop(0, first_heads + 3, step, 0)

    def drain(h, carry):
        z_kv(h).wait_send()
        z_q(h).wait_send()
        for zr in (0, 1):
            for j in (1, 3, 2):
                r_kv(h, zr, j).wait_send()
                r_q(h, zr, j).wait_send()
            c_kv(h, zr).wait_send()
        for j in (1, 2, 3):
            ring_o(h, j).wait_send()
        z_o(h).wait_send()
        out_copy(h).wait()
        return carry

    lax.fori_loop(0, heads, drain, 0)


def per_device(queries, keys, values, slot_blocks, doc_blocks):
    width = queries.shape[1]
    heads = width // D
    dma = pltpu.SemaphoreType.DMA
    anywhere = pl.BlockSpec(memory_space=pltpu.HBM)
    return pl.pallas_call(
        functools.partial(kernel, heads),
        out_shape=jax.ShapeDtypeStruct(queries.shape, BF16),
        in_specs=[anywhere] * 5,
        out_specs=anywhere,
        scratch_shapes=[
            pltpu.SMEM(slot_blocks.shape, jnp.int32),
            pltpu.SMEM(doc_blocks.shape, jnp.int32),
            pltpu.VMEM((NX, NZ, heads, R, D), BF16),
            pltpu.VMEM((2, NC, NZ, NX, heads, R, D), BF16),
            pltpu.VMEM((2, NK, NQ), F32),
            pltpu.VMEM((heads, D, NQ), F32),
            pltpu.VMEM((heads, 8, NQ), F32),
            pltpu.VMEM((heads, NX, D + STAT, D), BF16),
            pltpu.VMEM((heads, NX - 1, D + STAT, D), BF16),
            pltpu.VMEM((heads, R + 16, D), F32),
            pltpu.VMEM((heads, R + STAT, D), BF16),
            pltpu.VMEM((heads, R + STAT, D), BF16),
            pltpu.VMEM((heads, R, D), BF16),
            dma((2,)),
            dma((3, heads)),
            dma((heads,)), dma((heads,)), dma((heads,)), dma((heads,)),
            dma((heads, 2, 3)), dma((heads, 2, 3)), dma((heads, 2, 3)), dma((heads, 2, 3)),
            dma((heads, 2)), dma((heads, 2)),
            dma((heads, 3)), dma((heads, 3)),
            dma((heads,)), dma((heads,)), dma((heads,)),
        ],
        compiler_params=pltpu.CompilerParams(
            collective_id=0, has_side_effects=True, vmem_limit_bytes=64 * 1024 * 1024
        ),
        cost_estimate=pl.CostEstimate(
            flops=4 * heads * NQ * NK * D, bytes_accessed=4 * queries.size * 2, transcendentals=heads * NQ * NK
        ),
    )(queries, keys, values, slot_blocks, doc_blocks)


def solution(mesh):
    rows = P(("outer", "inner"), "head")
    return jax.shard_map(
        per_device,
        mesh=mesh,
        in_specs=(rows, rows, rows, P(), P()),
        out_specs=rows,
        check_vma=False,
    )
```

```python
import functools
import math

import jax
import jax.numpy as jnp
from jax import lax
from jax.experimental import pallas as pl
from jax.experimental.pallas import tpu as pltpu
from jax.sharding import PartitionSpec as P

D = 128
BLK = 32
R = 64
NX = 4
NZ = 2
NC = 2
NQ = NX * NZ * R
NK = NC * NZ * NX * R
STAT = 16
SCALE2 = D ** (-0.5) * math.log2(math.e)
HIDE = -1e30
FLOOR = -1e29
MESH = pl.DeviceIdType.MESH
F32 = jnp.float32
BF16 = jnp.bfloat16


def nt(a, b):
    return lax.dot_general(a, b, (((1,), (1,)), ((), ())), preferred_element_type=F32)


def tn(a, b):
    return lax.dot_general(a, b, (((0,), (0,)), ((), ())), preferred_element_type=F32)


def kernel(
    heads,
    q_ref, k_ref, v_ref, slot_hbm, doc_hbm, out_ref,
    slot_ref, doc_ref, qg, kvg, bias, half_o, half_stat, op, orecv, own, zs, zr_buf, out_buf,
    tab_sem, loc_sem, zkv_s, zkv_r, zq_s, zq_r, kv_s, kv_r, q_s, q_r, c_s, c_r, o_s, o_r, zo_s, zo_r, out_sem,
):
    outer = lax.axis_index("outer")
    inner = lax.axis_index("inner")
    z, c = outer // 2, outer % 2
    x, y = inner // NX, inner % NX
    za = z + 1 - 2 * (z % 2)
    zb = 3 - z
    dev_c = {"outer": z * 2 + 1 - c, "inner": inner}
    first_heads = (heads + 1) // 2
    counts = (first_heads, heads - first_heads)

    def pick(g, even, odd):
        return even + g * (odd - even)

    def group_of(h):
        return h // first_heads

    def plane_q(g):
        return {"outer": pick(g, za, zb) * 2 + c, "inner": inner}

    def plane_kv(g):
        return {"outer": pick(g, zb, za) * 2 + c, "inner": inner}

    def along_x(j):
        return lax.rem(x + j, NX) * NX + y

    def along_y(j):
        return x * NX + lax.rem(y + j, NX)

    def ring_q(g, j):
        return {"outer": outer, "inner": pick(g, along_x(j), along_y(j))}

    def ring_kv(g, j):
        return {"outer": outer, "inner": pick(g, along_y(j), along_x(j))}

    def at_q(g, j=0):
        return lax.rem(pick(g, x, y) + j, NX)

    def at_kv(g, j=0):
        return lax.rem(pick(g, y, x) + j, NX)

    tables = (
        pltpu.make_async_copy(slot_hbm, slot_ref, tab_sem.at[0]),
        pltpu.make_async_copy(doc_hbm, doc_ref, tab_sem.at[1]),
    )

    def local(h):
        at = pl.ds(h * D, D)
        g = group_of(h)
        return (
            pltpu.make_async_copy(q_ref.at[:, at], qg.at[at_q(g), 0, h], loc_sem.at[2, h]),
            pltpu.make_async_copy(k_ref.at[:, at], kvg.at[0, 0, 0, at_kv(g), h], loc_sem.at[0, h]),
            pltpu.make_async_copy(v_ref.at[:, at], kvg.at[1, 0, 0, at_kv(g), h], loc_sem.at[1, h]),
        )

    for w in range(first_heads):
        for h in (w, first_heads + w):
            if h < heads:
                for copy in local(h):
                    copy.start()
    for copy in tables:
        copy.start()

    barrier = pltpu.get_barrier_semaphore()
    partners = [plane_q(0), plane_kv(0), dev_c]
    partners += [ring_q(0, j) for j in (1, 2, 3)] + [ring_kv(0, j) for j in (1, 2, 3)]
    for dev in partners:
        pl.semaphore_signal(barrier, inc=1, device_id=dev, device_id_type=MESH)
    pl.semaphore_wait(barrier, len(partners))

    def remote(src, dst, send, recv, dev):
        return pltpu.make_async_remote_copy(
            src_ref=src, dst_ref=dst, send_sem=send, recv_sem=recv, device_id=dev, device_id_type=MESH
        )

    def z_kv(h):
        g = group_of(h)
        here = at_kv(g)
        return remote(
            kvg.at[:, 0, 0, here, h], kvg.at[:, 0, 1, here, h], zkv_s, zkv_r.at[h], plane_kv(g)
        )

    def z_q(h):
        g = group_of(h)
        here = at_q(g)
        return remote(qg.at[here, 0, h], qg.at[here, 1, h], zq_s, zq_r.at[h], plane_q(g))

    def r_kv(h, zr, j):
        g = group_of(h)
        block = kvg.at[:, 0, zr, at_kv(g), h]
        return remote(block, block, kv_s, kv_r.at[h, zr], ring_kv(g, j))

    def r_q(h, zr, j):
        g = group_of(h)
        block = qg.at[at_q(g), zr, h]
        return remote(block, block, q_s, q_r.at[h], ring_q(g, j))

    def c_kv(h, zr):
        return remote(kvg.at[:, 0, zr, :, h], kvg.at[:, 1, zr, :, h], c_s, c_r.at[h, zr], dev_c)

    def ring_o(h, j):
        g = group_of(h)
        return remote(
            op.at[h, at_q(g, j)], orecv.at[h, j - 1], o_s, o_r.at[h], ring_q(g, j)
        )

    def z_o(h):
        return remote(zs.at[h], zr_buf.at[h], zo_s, zo_r.at[h], plane_q(group_of(h)))

    def take(ref, sem):
        pltpu.make_async_copy(ref, ref, sem).wait()

    def out_copy(h):
        return pltpu.make_async_copy(
            out_buf.at[h], out_ref.at[:, pl.ds(pl.multiple_of(h * D, D), D)], out_sem
        )

    def begin_ring(h):
        for j in (1, 3, 2):
            r_kv(h, 0, j).start()
            r_q(h, 0, j).start()

    order = [h for w in range(first_heads) for h in (w, first_heads + w) if h < heads]
    for h in order:
        for copy in local(h):
            copy.wait()
        if h % first_heads == 0:
            z_q(h).start()
            z_kv(h).start()
            begin_ring(h)
    for copy in tables:
        copy.wait()

    ends = [doc_ref[0]]
    for n in range(1, doc_ref.shape[0]):
        ends.append(ends[-1] + doc_ref[n])

    def doc_start(slot):
        start = jnp.int32(0)
        for end in ends:
            start = jnp.where(slot >= end, end, start)
        return start

    lane = lax.broadcasted_iota(jnp.int32, (8, NQ), 1)
    down = lax.broadcasted_iota(jnp.int32, (8, NQ), 0)
    part = lane // BLK

    def build_mask(g):
        q_pos = jnp.zeros((8, NQ), jnp.int32)
        q_low = jnp.zeros((8, NQ), jnp.int32)
        for t in range(NQ // BLK):
            rt, zt, half = t // 4, (t // 2) % 2, t % 2
            zq = z if zt == 0 else (zb if g else za)
            iq = x * NX + rt if g else rt * NX + y
            slot = slot_ref[2 * ((zq * 2 + c) * 16 + iq) + half]
            hit = part == t
            q_pos = jnp.where(hit, slot * BLK, q_pos)
            q_low = jnp.where(hit, doc_start(slot) * BLK, q_low)
        q_pos = q_pos + lane % BLK

        def mask(t, carry):
            ct, zt, rt, half = t // 16, (t // 8) % 2, (t // 2) % 4, t % 2
            zk = z + zt * ((za if g else zb) - z)
            ck = c + ct * (1 - 2 * c)
            ik = rt * NX + y if g else x * NX + rt
            slot = slot_ref[2 * ((zk * 2 + ck) * 16 + ik) + half]
            for row in range(0, BLK, 8):
                k_pos = down + (slot * BLK + row)
                seen = (k_pos <= q_pos) & (k_pos >= q_low)
                at = (zt * 2 + ct) * (NX * R) + rt * R + half * BLK + row
                bias[g, pl.ds(pl.multiple_of(at, 8), 8), :] = jnp.where(seen, 0.0, HIDE)
            return carry

        lax.fori_loop(0, NK // BLK, mask, 0)

    def swap_cores(h, zr):
        take(kvg.at[:, 0, zr, pl.ds(0, NX - 1), h], kv_r.at[h, zr])
        c_kv(h, zr).start()

    def has_next(h):
        return (h != first_heads - 1) & (h != heads - 1)

    def spread_q(h):
        z_q(h).wait_recv()

        @pl.when(has_next(h))
        def _():
            z_q(h + 1).start()
            begin_ring(h + 1)

        for j in (1, 3, 2):
            r_q(h, 1, j).start()

    def spread_kv(h):
        z_kv(h).wait_recv()

        @pl.when(has_next(h))
        def _():
            z_kv(h + 1).start()

        for j in (1, 3, 2):
            r_kv(h, 1, j).start()

    def attend(h, zr):
        g = group_of(h)
        count = NK // NZ
        keys = kvg[0, :, zr, :, h].reshape(count, D)
        values = kvg[1, :, zr, :, h].reshape(count, D)
        width = 256
        each = width // D
        for tile in range(NQ // width):
            span = slice(tile * width, (tile + 1) * width)
            queries = qg[tile * each : (tile + 1) * each, :, h].reshape(width, D)
            scaled = nt(keys, queries) * SCALE2 + bias[g, zr * count : (zr + 1) * count, span]
            top = jnp.max(scaled, axis=0, keepdims=True)
            top = jnp.maximum(top, FLOOR).astype(BF16).astype(F32)
            if zr:
                before = half_stat[h, 0:1, span]
                top = jnp.maximum(top, before)
            terms = jnp.exp2(scaled - top)
            total = jnp.sum(terms, axis=0, keepdims=True)
            result = tn(values, terms.astype(BF16))
            if not zr:
                half_stat[h, 0:1, span] = top
                half_stat[h, 1:2, span] = total
                half_o[h, :, span] = result
                continue
            shrink = jnp.exp2(before - top)
            total = total + half_stat[h, 1:2, span] * shrink
            result = (result + half_o[h, :, span] * shrink).astype(BF16)
            total_hi = total.astype(BF16).astype(F32)
            row = lax.broadcasted_iota(jnp.int32, (STAT, width), 0)
            stats = jnp.where(row == 0, top, jnp.where(row == 1, total_hi, total - total_hi)).astype(BF16)
            for n in range(each):
                op[h, tile * each + n, 0:D, :] = result[:, n * D : (n + 1) * D]
                op[h, tile * each + n, D : D + STAT, :] = stats[:, n * D : (n + 1) * D]

    left = lax.broadcasted_iota(jnp.int32, (8, D), 1) < R

    def unstat(block):
        stat = block.astype(F32)
        return (
            jnp.broadcast_to(stat[0:1], (8, D)),
            jnp.broadcast_to(stat[1:2] + stat[2:3], (8, D)),
        )

    def swap_half(a):
        return pltpu.roll(a, R, axis=1)

    def merge_ring(h):
        take(orecv.at[h], o_r.at[h])
        here = at_q(group_of(h))
        parts = [(op[h, here, 0:D, :], op[h, here, D : D + STAT, :])]
        for j in (1, 2, 3):
            parts.append((orecv[h, j - 1, 0:D, :], orecv[h, j - 1, D : D + STAT, :]))
        stats = [unstat(p[1]) for p in parts]
        top = functools.reduce(jnp.maximum, [s[0] for s in stats])
        total = jnp.zeros((8, D), F32)
        result = jnp.zeros((D, D), F32)
        for (block, _), (m, l) in zip(parts, stats):
            w = jnp.exp2(m - top)
            total = total + w * l
            result = result + block.astype(F32) * w[0:1]
        low, high = result[0:R], result[R:D]
        mine = jnp.where(left[0:1], low, swap_half(high))
        other = jnp.where(left[0:1], swap_half(low), high)
        top_swapped, total_swapped = swap_half(top), swap_half(total)
        own[h, 0:R, :] = mine
        own[h, R : R + 8, :] = jnp.where(left, top, top_swapped)
        own[h, R + 8 : R + 16, :] = jnp.where(left, total, total_swapped)
        m_other = jnp.where(left, top_swapped, top)[0:1]
        l_other = jnp.where(left, total_swapped, total)[0:1]
        l_hi = l_other.astype(BF16).astype(F32)
        row = lax.broadcasted_iota(jnp.int32, (STAT, D), 0)
        zs[h, 0:R, :] = other.astype(BF16)
        zs[h, R : R + STAT, :] = jnp.where(
            row == 0, m_other, jnp.where(row == 1, l_hi, l_other - l_hi)
        ).astype(BF16)
        z_o(h).start()

    def finish(h):
        z_o(h).wait_recv()
        m_far, l_far = unstat(zr_buf[h, R : R + STAT, :])
        m_own, l_own = own[h, R : R + 8, :], own[h, R + 8 : R + 16, :]
        top = jnp.maximum(m_far, m_own)
        w_far, w_own = jnp.exp2(m_far - top), jnp.exp2(m_own - top)
        total = w_far * l_far + w_own * l_own
        w_far, w_own = w_far / total, w_own / total
        packed = own[h, 0:R, :] * w_own[0:1] + zr_buf[h, 0:R, :].astype(F32) * w_far[0:1]
        tall = jnp.concatenate([packed, swap_half(packed)], axis=0)
        out_buf[h] = tall.T[0:R].astype(BF16)
        out_copy(h).start()

    build_mask(0)
    build_mask(1)

    def early(h):
        take(qg.at[pl.ds(0, NX - 1), :, h], q_r.at[h])
        c_kv(h, 0).wait_recv()
        attend(h, 0)

    def late(h):
        c_kv(h, 1).wait_recv()
        attend(h, 1)
        for j in (1, 3, 2):
            ring_o(h, j).start()

    def wave(w, *works):
        def one(g, carry):
            h = g * first_heads + w
            for work in works:
                work(h)
            return carry

        @pl.when((w >= 0) & (w < first_heads))
        def _():
            lax.fori_loop(0, jnp.where(w < counts[1], 2, 1), one, 0)

    def step(s, carry):
        wave(s, spread_q, lambda h: swap_cores(h, 0))
        wave(s - 1, lambda h: swap_cores(h, 1))
        wave(s - 2, merge_ring)
        wave(s, early)
        wave(s, spread_kv)
        wave(s - 1, late)
        wave(s - 3, finish)
        return carry

    lax.fori_loop(0, first_heads + 3, step, 0)

    take(kvg.at[:, 0, 0, 0], zkv_s)
    take(qg.at[0, 0], zq_s)
    take(kvg.at[:, 0, :, pl.ds(0, NX - 1)], kv_s)
    take(qg.at[pl.ds(0, NX - 1)], q_s)
    take(kvg.at[:, 0], c_s)
    take(orecv, o_s)
    take(zs, zo_s)
    take(out_buf, out_sem)


def per_device(queries, keys, values, slot_blocks, doc_blocks):
    width = queries.shape[1]
    heads = width // D
    dma = pltpu.SemaphoreType.DMA
    anywhere = pl.BlockSpec(memory_space=pltpu.HBM)
    return pl.pallas_call(
        functools.partial(kernel, heads),
        out_shape=jax.ShapeDtypeStruct(queries.shape, BF16),
        in_specs=[anywhere] * 5,
        out_specs=anywhere,
        scratch_shapes=[
            pltpu.SMEM(slot_blocks.shape, jnp.int32),
            pltpu.SMEM(doc_blocks.shape, jnp.int32),
            pltpu.VMEM((NX, NZ, heads, R, D), BF16),
            pltpu.VMEM((2, NC, NZ, NX, heads, R, D), BF16),
            pltpu.VMEM((2, NK, NQ), F32),
            pltpu.VMEM((heads, D, NQ), F32),
            pltpu.VMEM((heads, 8, NQ), F32),
            pltpu.VMEM((heads, NX, D + STAT, D), BF16),
            pltpu.VMEM((heads, NX - 1, D + STAT, D), BF16),
            pltpu.VMEM((heads, R + 16, D), F32),
            pltpu.VMEM((heads, R + STAT, D), BF16),
            pltpu.VMEM((heads, R + STAT, D), BF16),
            pltpu.VMEM((heads, R, D), BF16),
            dma((2,)),
            dma((3, heads)),
            dma, dma((heads,)), dma, dma((heads,)),
            dma, dma((heads, 2)), dma, dma((heads,)),
            dma, dma((heads, 2)),
            dma, dma((heads,)),
            dma, dma((heads,)), dma,
        ],
        compiler_params=pltpu.CompilerParams(
            collective_id=0, has_side_effects=True, vmem_limit_bytes=64 * 1024 * 1024
        ),
        cost_estimate=pl.CostEstimate(
            flops=4 * heads * NQ * NK * D, bytes_accessed=4 * queries.size * 2, transcendentals=heads * NQ * NK
        ),
    )(queries, keys, values, slot_blocks, doc_blocks)


def solution(mesh):
    rows = P(("outer", "inner"), "head")
    return jax.shard_map(
        per_device,
        mesh=mesh,
        in_specs=(rows, rows, rows, P(), P()),
        out_specs=rows,
        check_vma=False,
    )
```

```python
import functools
import math

import jax
import jax.numpy as jnp
from jax import lax
from jax.experimental import pallas as pl
from jax.experimental.pallas import tpu as pltpu
from jax.sharding import PartitionSpec as P

D = 128
BLK = 32
R = 64
NX = 4
NZ = 2
NC = 2
NQ = NX * NZ * R
NK = NC * NZ * NX * R
STAT = 16
SCALE2 = D ** (-0.5) * math.log2(math.e)
HIDE = -1e30
FLOOR = -1e29
MESH = pl.DeviceIdType.MESH
F32 = jnp.float32
BF16 = jnp.bfloat16


def nt(a, b):
    return lax.dot_general(a, b, (((1,), (1,)), ((), ())), preferred_element_type=F32)


def tn(a, b):
    return lax.dot_general(a, b, (((0,), (0,)), ((), ())), preferred_element_type=F32)


def kernel(
    heads,
    q_ref, k_ref, v_ref, slot_hbm, doc_hbm, out_ref,
    slot_ref, doc_ref, qg, kvg, bias, half_o, half_stat, op, orecv, own, zs, zr_buf, out_buf,
    tab_sem, loc_sem, zkv_s, zkv_r, zq_s, zq_r, kv_s, kv_r, q_s, q_r, c_s, c_r, o_s, o_r, zo_s, zo_r, out_sem,
):
    outer = lax.axis_index("outer")
    inner = lax.axis_index("inner")
    z, c = outer // 2, outer % 2
    x, y = inner // NX, inner % NX
    za = z + 1 - 2 * (z % 2)
    zb = 3 - z
    dev_c = {"outer": z * 2 + 1 - c, "inner": inner}
    first_heads = (heads + 1) // 2

    def pick(g, even, odd):
        return even + g * (odd - even)

    def group_of(h):
        return h // first_heads

    def plane_q(g):
        return {"outer": pick(g, za, zb) * 2 + c, "inner": inner}

    def plane_kv(g):
        return {"outer": pick(g, zb, za) * 2 + c, "inner": inner}

    def along_x(j):
        return lax.rem(x + j, NX) * NX + y

    def along_y(j):
        return x * NX + lax.rem(y + j, NX)

    def ring_q(g, j):
        return {"outer": outer, "inner": pick(g, along_x(j), along_y(j))}

    def ring_kv(g, j):
        return {"outer": outer, "inner": pick(g, along_y(j), along_x(j))}

    def at_q(g, j=0):
        return lax.rem(pick(g, x, y) + j, NX)

    def at_kv(g, j=0):
        return lax.rem(pick(g, y, x) + j, NX)

    tables = (
        pltpu.make_async_copy(slot_hbm, slot_ref, tab_sem.at[0]),
        pltpu.make_async_copy(doc_hbm, doc_ref, tab_sem.at[1]),
    )

    def local(h):
        at = pl.ds(h * D, D)
        g = group_of(h)
        return (
            pltpu.make_async_copy(q_ref.at[:, at], qg.at[at_q(g), 0, h], loc_sem.at[2, h]),
            pltpu.make_async_copy(k_ref.at[:, at], kvg.at[0, 0, 0, at_kv(g), h], loc_sem.at[0, h]),
            pltpu.make_async_copy(v_ref.at[:, at], kvg.at[1, 0, 0, at_kv(g), h], loc_sem.at[1, h]),
        )

    for h in (0, 1, 3, 2, 4):
        for copy in local(h):
            copy.start()
    for copy in tables:
        copy.start()

    barrier = pltpu.get_barrier_semaphore()
    partners = [plane_q(0), plane_kv(0), dev_c]
    partners += [ring_q(0, j) for j in (1, 2, 3)] + [ring_kv(0, j) for j in (1, 2, 3)]
    for dev in partners:
        pl.semaphore_signal(barrier, inc=1, device_id=dev, device_id_type=MESH)
    pl.semaphore_wait(barrier, len(partners))

    def remote(src, dst, send, recv, dev):
        return pltpu.make_async_remote_copy(
            src_ref=src, dst_ref=dst, send_sem=send, recv_sem=recv, device_id=dev, device_id_type=MESH
        )

    def z_kv(h):
        g = group_of(h)
        here = at_kv(g)
        return remote(
            kvg.at[:, 0, 0, here, h], kvg.at[:, 0, 1, here, h], zkv_s, zkv_r.at[h], plane_kv(g)
        )

    def z_q(h):
        g = group_of(h)
        here = at_q(g)
        return remote(qg.at[here, 0, h], qg.at[here, 1, h], zq_s, zq_r.at[h], plane_q(g))

    def kv_own(h, zr, way):
        g = group_of(h)
        block = kvg.at[:, 0, zr, at_kv(g), h]
        return remote(block, block, kv_s, kv_r.at[h, zr, way], ring_kv(g, 1 + 2 * way))

    def kv_on(h, zr, way):
        g = group_of(h)
        block = kvg.at[way, 0, zr, at_kv(g, 3 - 2 * way), h]
        return remote(block, block, kv_s, kv_r.at[h, zr, 2], ring_kv(g, 1 + 2 * way))

    def q_own(h, zr, way):
        g = group_of(h)
        block = qg.at[at_q(g), zr, h]
        return remote(block, block, q_s, q_r.at[h, zr, way], ring_q(g, 1 + 2 * way))

    def q_on(h, zr, way):
        g = group_of(h)
        block = qg.at[at_q(g, 3 - 2 * way), zr, h, pl.ds(way * (R // 2), R // 2)]
        return remote(block, block, q_s, q_r.at[h, zr, 2], ring_q(g, 1 + 2 * way))

    def c_kv(h, zr):
        return remote(kvg.at[:, 0, zr, :, h], kvg.at[:, 1, zr, :, h], c_s, c_r.at[h, zr], dev_c)

    def ring_o(h, j):
        g = group_of(h)
        return remote(
            op.at[h, at_q(g, j)], orecv.at[h, j - 1], o_s, o_r.at[h], ring_q(g, j)
        )

    def z_o(h):
        return remote(zs.at[h], zr_buf.at[h], zo_s, zo_r.at[h], plane_q(group_of(h)))

    def take(ref, sem):
        pltpu.make_async_copy(ref, ref, sem).wait()

    def out_copy(h):
        return pltpu.make_async_copy(
            out_buf.at[h], out_ref.at[:, pl.ds(pl.multiple_of(h * D, D), D)], out_sem
        )

    def begin_ring(h):
        for way in (0, 1):
            kv_own(h, 0, way).start()
            q_own(h, 0, way).start()

    waves = ((0, 1, 3), (2, 4))

    for h in waves[0]:
        for copy in local(h):
            copy.wait()
        z_q(h).start()
        z_kv(h).start()
        begin_ring(h)
    for h in waves[1]:
        for copy in local(h):
            copy.wait()
    for copy in tables:
        copy.wait()

    ends = [doc_ref[0]]
    for n in range(1, doc_ref.shape[0]):
        ends.append(ends[-1] + doc_ref[n])

    def doc_start(slot):
        start = jnp.int32(0)
        for end in ends:
            start = jnp.where(slot >= end, end, start)
        return start

    lane = lax.broadcasted_iota(jnp.int32, (8, NQ), 1)
    down = lax.broadcasted_iota(jnp.int32, (8, NQ), 0)
    part = lane // BLK

    def build_mask(g):
        q_pos = jnp.zeros((8, NQ), jnp.int32)
        q_low = jnp.zeros((8, NQ), jnp.int32)
        for t in range(NQ // BLK):
            rt, zt, half = t // 4, (t // 2) % 2, t % 2
            zq = z if zt == 0 else (zb if g else za)
            iq = x * NX + rt if g else rt * NX + y
            slot = slot_ref[2 * ((zq * 2 + c) * 16 + iq) + half]
            hit = part == t
            q_pos = jnp.where(hit, slot * BLK, q_pos)
            q_low = jnp.where(hit, doc_start(slot) * BLK, q_low)
        q_pos = q_pos + lane % BLK

        def mask(t, carry):
            ct, zt, rt, half = t // 16, (t // 8) % 2, (t // 2) % 4, t % 2
            zk = z + zt * ((za if g else zb) - z)
            ck = c + ct * (1 - 2 * c)
            ik = rt * NX + y if g else x * NX + rt
            slot = slot_ref[2 * ((zk * 2 + ck) * 16 + ik) + half]
            for row in range(0, BLK, 8):
                k_pos = down + (slot * BLK + row)
                seen = (k_pos <= q_pos) & (k_pos >= q_low)
                at = (zt * 2 + ct) * (NX * R) + rt * R + half * BLK + row
                bias[g, pl.ds(pl.multiple_of(at, 8), 8), :] = jnp.where(seen, 0.0, HIDE)
            return carry

        lax.fori_loop(0, NK // BLK, mask, 0)

    def pass_on_kv(h, zr):
        for way in (0, 1):
            kv_own(h, zr, way).wait_recv()
            kv_on(h, zr, way).start()

    def pass_on_q(h, zr):
        for way in (0, 1):
            q_own(h, zr, way).wait_recv()
            q_on(h, zr, way).start()

    def swap_cores(h, zr):
        take(kvg.at[:, 0, zr, 0, h], kv_r.at[h, zr, 2])
        c_kv(h, zr).start()

    def has_next(h):
        return (h == 1) | (h == 3)

    def spread_q(h):
        z_q(h).wait_recv()

        @pl.when(has_next(h))
        def _():
            z_q(h + 1).start()
            begin_ring(h + 1)

        for way in (0, 1):
            q_own(h, 1, way).start()

    def spread_kv(h):
        z_kv(h).wait_recv()

        @pl.when(has_next(h))
        def _():
            z_kv(h + 1).start()

        for way in (0, 1):
            kv_own(h, 1, way).start()

    def attend(h, zr):
        g = group_of(h)
        count = NK // NZ
        keys = kvg[0, :, zr, :, h].reshape(count, D)
        values = kvg[1, :, zr, :, h].reshape(count, D)
        width = 256
        each = width // D
        for tile in range(NQ // width):
            span = slice(tile * width, (tile + 1) * width)
            queries = qg[tile * each : (tile + 1) * each, :, h].reshape(width, D)
            scaled = nt(keys, queries) * SCALE2 + bias[g, zr * count : (zr + 1) * count, span]
            top = jnp.max(scaled, axis=0, keepdims=True)
            top = jnp.maximum(top, FLOOR).astype(BF16).astype(F32)
            if zr:
                before = half_stat[h, 0:1, span]
                top = jnp.maximum(top, before)
            terms = jnp.exp2(scaled - top)
            total = jnp.sum(terms, axis=0, keepdims=True)
            result = tn(values, terms.astype(BF16))
            if not zr:
                half_stat[h, 0:1, span] = top
                half_stat[h, 1:2, span] = total
                half_o[h, :, span] = result
                continue
            shrink = jnp.exp2(before - top)
            total = total + half_stat[h, 1:2, span] * shrink
            result = (result + half_o[h, :, span] * shrink).astype(BF16)
            total_hi = total.astype(BF16).astype(F32)
            row = lax.broadcasted_iota(jnp.int32, (STAT, width), 0)
            stats = jnp.where(row == 0, top, jnp.where(row == 1, total_hi, total - total_hi)).astype(BF16)
            for n in range(each):
                op[h, tile * each + n, 0:D, :] = result[:, n * D : (n + 1) * D]
                op[h, tile * each + n, D : D + STAT, :] = stats[:, n * D : (n + 1) * D]

    left = lax.broadcasted_iota(jnp.int32, (8, D), 1) < R

    def unstat(block):
        stat = block.astype(F32)
        return (
            jnp.broadcast_to(stat[0:1], (8, D)),
            jnp.broadcast_to(stat[1:2] + stat[2:3], (8, D)),
        )

    def swap_half(a):
        return pltpu.roll(a, R, axis=1)

    def merge_ring(h):
        take(orecv.at[h], o_r.at[h])
        here = at_q(group_of(h))
        parts = [(op[h, here, 0:D, :], op[h, here, D : D + STAT, :])]
        for j in (1, 2, 3):
            parts.append((orecv[h, j - 1, 0:D, :], orecv[h, j - 1, D : D + STAT, :]))
        stats = [unstat(p[1]) for p in parts]
        top = functools.reduce(jnp.maximum, [s[0] for s in stats])
        total = jnp.zeros((8, D), F32)
        result = jnp.zeros((D, D), F32)
        for (block, _), (m, l) in zip(parts, stats):
            w = jnp.exp2(m - top)
            total = total + w * l
            result = result + block.astype(F32) * w[0:1]
        low, high = result[0:R], result[R:D]
        mine = jnp.where(left[0:1], low, swap_half(high))
        other = jnp.where(left[0:1], swap_half(low), high)
        top_swapped, total_swapped = swap_half(top), swap_half(total)
        own[h, 0:R, :] = mine
        own[h, R : R + 8, :] = jnp.where(left, top, top_swapped)
        own[h, R + 8 : R + 16, :] = jnp.where(left, total, total_swapped)
        m_other = jnp.where(left, top_swapped, top)[0:1]
        l_other = jnp.where(left, total_swapped, total)[0:1]
        l_hi = l_other.astype(BF16).astype(F32)
        row = lax.broadcasted_iota(jnp.int32, (STAT, D), 0)
        zs[h, 0:R, :] = other.astype(BF16)
        zs[h, R : R + STAT, :] = jnp.where(
            row == 0, m_other, jnp.where(row == 1, l_hi, l_other - l_hi)
        ).astype(BF16)
        z_o(h).start()

    def finish(h):
        z_o(h).wait_recv()
        m_far, l_far = unstat(zr_buf[h, R : R + STAT, :])
        m_own, l_own = own[h, R : R + 8, :], own[h, R + 8 : R + 16, :]
        top = jnp.maximum(m_far, m_own)
        w_far, w_own = jnp.exp2(m_far - top), jnp.exp2(m_own - top)
        total = w_far * l_far + w_own * l_own
        w_far, w_own = w_far / total, w_own / total
        packed = own[h, 0:R, :] * w_own[0:1] + zr_buf[h, 0:R, :].astype(F32) * w_far[0:1]
        tall = jnp.concatenate([packed, swap_half(packed)], axis=0)
        out_buf[h] = tall.T[0:R].astype(BF16)
        out_copy(h).start()

    build_mask(0)
    build_mask(1)

    def early(h):
        for zr in (0, 1):
            take(qg.at[0, zr, h], q_r.at[h, zr, 2])
        c_kv(h, 0).wait_recv()
        attend(h, 0)

    def late(h):
        c_kv(h, 1).wait_recv()
        attend(h, 1)
        for j in (1, 3, 2):
            ring_o(h, j).start()

    def wave(w, work):
        def one(i, carry):
            work(i + i // 2 + w * (2 + i - i // 2))
            return carry

        @pl.when((w >= 0) & (w < 2))
        def _():
            lax.fori_loop(0, 3 - w, one, 0)

    def step(s, carry):
        wave(s, spread_q)
        wave(s, lambda h: pass_on_kv(h, 0))
        wave(s, lambda h: pass_on_q(h, 0))
        wave(s - 1, lambda h: swap_cores(h, 1))
        wave(s - 2, merge_ring)
        wave(s, lambda h: pass_on_q(h, 1))
        wave(s, lambda h: swap_cores(h, 0))
        wave(s, spread_kv)
        wave(s - 1, late)
        wave(s, lambda h: pass_on_kv(h, 1))
        wave(s, early)
        wave(s - 3, finish)
        return carry

    lax.fori_loop(0, 5, step, 0)

    take(kvg.at[:, 0, 0, 0], zkv_s)
    take(qg.at[0, 0], zq_s)
    take(kvg.at[:, 0, :, pl.ds(0, NX - 1)], kv_s)
    take(qg.at[pl.ds(0, NX - 1)], q_s)
    take(kvg.at[:, 0], c_s)
    take(orecv, o_s)
    take(zs, zo_s)
    take(out_buf, out_sem)


def per_device(queries, keys, values, slot_blocks, doc_blocks):
    width = queries.shape[1]
    heads = width // D
    dma = pltpu.SemaphoreType.DMA
    anywhere = pl.BlockSpec(memory_space=pltpu.HBM)
    return pl.pallas_call(
        functools.partial(kernel, heads),
        out_shape=jax.ShapeDtypeStruct(queries.shape, BF16),
        in_specs=[anywhere] * 5,
        out_specs=anywhere,
        scratch_shapes=[
            pltpu.SMEM(slot_blocks.shape, jnp.int32),
            pltpu.SMEM(doc_blocks.shape, jnp.int32),
            pltpu.VMEM((NX, NZ, heads, R, D), BF16),
            pltpu.VMEM((2, NC, NZ, NX, heads, R, D), BF16),
            pltpu.VMEM((2, NK, NQ), F32),
            pltpu.VMEM((heads, D, NQ), F32),
            pltpu.VMEM((heads, 8, NQ), F32),
            pltpu.VMEM((heads, NX, D + STAT, D), BF16),
            pltpu.VMEM((heads, NX - 1, D + STAT, D), BF16),
            pltpu.VMEM((heads, R + 16, D), F32),
            pltpu.VMEM((heads, R + STAT, D), BF16),
            pltpu.VMEM((heads, R + STAT, D), BF16),
            pltpu.VMEM((heads, R, D), BF16),
            dma((2,)),
            dma((3, heads)),
            dma, dma((heads,)), dma, dma((heads,)),
            dma, dma((heads, 2, 3)), dma, dma((heads, 2, 3)),
            dma, dma((heads, 2)),
            dma, dma((heads,)),
            dma, dma((heads,)), dma,
        ],
        compiler_params=pltpu.CompilerParams(
            collective_id=0, has_side_effects=True, vmem_limit_bytes=64 * 1024 * 1024
        ),
        cost_estimate=pl.CostEstimate(
            flops=4 * heads * NQ * NK * D, bytes_accessed=4 * queries.size * 2, transcendentals=heads * NQ * NK
        ),
    )(queries, keys, values, slot_blocks, doc_blocks)


def solution(mesh):
    rows = P(("outer", "inner"), "head")
    return jax.shard_map(
        per_device,
        mesh=mesh,
        in_specs=(rows, rows, rows, P(), P()),
        out_specs=rows,
        check_vma=False,
    )
```

```python
import functools
import math

import jax
import jax.numpy as jnp
from jax import lax
from jax.experimental import pallas as pl
from jax.experimental.pallas import tpu as pltpu
from jax.sharding import PartitionSpec as P

D = 128
BLK = 32
R = 64
NX = 4
NZ = 2
NC = 2
NQ = NX * NZ * R
QT = NX * R
NK = NC * NZ * NX * R
STAT = 16
SCALE2 = D ** (-0.5) * math.log2(math.e)
HIDE = -1e30
FLOOR = -1e29
MESH = pl.DeviceIdType.MESH
F32 = jnp.float32
BF16 = jnp.bfloat16


def nt(a, b):
    return lax.dot_general(a, b, (((1,), (1,)), ((), ())), preferred_element_type=F32)


def tn(a, b):
    return lax.dot_general(a, b, (((0,), (0,)), ((), ())), preferred_element_type=F32)


def kernel(
    heads,
    q_ref, k_ref, v_ref, slot_hbm, doc_hbm, out_ref,
    slot_ref, doc_ref, qg, kvg, bias, half_o, half_stat, op, orecv, zs, zr_buf, out_buf,
    tab_sem, loc_sem, zkv_s, zkv_r, zq_s, zq_r, kv_s, kv_r, q_s, q_r, c_s, c_r, o_s, o_r, zo_s, zo_r, out_sem,
):
    outer = lax.axis_index("outer")
    inner = lax.axis_index("inner")
    z, c = outer // 2, outer % 2
    x, y = inner // NX, inner % NX
    za = z + 1 - 2 * (z % 2)
    zb = 3 - z
    dev_c = {"outer": z * 2 + 1 - c, "inner": inner}
    first_heads = (heads + 1) // 2
    groups = (0, 1)
    of = (pl.ds(0, first_heads), pl.ds(first_heads, heads - first_heads))

    def pick(g, even, odd):
        return even + g * (odd - even)

    def group_of(h):
        return h // first_heads

    def plane_q(g):
        return {"outer": pick(g, za, zb) * 2 + c, "inner": inner}

    def plane_kv(g):
        return {"outer": pick(g, zb, za) * 2 + c, "inner": inner}

    def along_x(j):
        return lax.rem(x + j, NX) * NX + y

    def along_y(j):
        return x * NX + lax.rem(y + j, NX)

    def ring_q(g, j):
        return {"outer": outer, "inner": pick(g, along_x(j), along_y(j))}

    def ring_kv(g, j):
        return {"outer": outer, "inner": pick(g, along_y(j), along_x(j))}

    def at_q(g, j=0):
        return lax.rem(pick(g, x, y) + j, NX)

    def at_kv(g, j=0):
        return lax.rem(pick(g, y, x) + j, NX)

    tables = (
        pltpu.make_async_copy(slot_hbm, slot_ref, tab_sem.at[0]),
        pltpu.make_async_copy(doc_hbm, doc_ref, tab_sem.at[1]),
    )

    def local(h):
        at = pl.ds(h * D, D)
        g = group_of(h)
        return (
            pltpu.make_async_copy(q_ref.at[:, at], qg.at[at_q(g), 0, h], loc_sem.at[2, h]),
            pltpu.make_async_copy(k_ref.at[:, at], kvg.at[0, 0, 0, at_kv(g), h], loc_sem.at[0, h]),
            pltpu.make_async_copy(v_ref.at[:, at], kvg.at[1, 0, 0, at_kv(g), h], loc_sem.at[1, h]),
        )

    for h in range(heads):
        for copy in local(h):
            copy.start()
    for copy in tables:
        copy.start()

    barrier = pltpu.get_barrier_semaphore()
    partners = [plane_q(0), plane_kv(0), dev_c]
    partners += [ring_q(0, j) for j in (1, 2, 3)] + [ring_kv(0, j) for j in (1, 2, 3)]
    for dev in partners:
        pl.semaphore_signal(barrier, inc=1, device_id=dev, device_id_type=MESH)
    pl.semaphore_wait(barrier, len(partners))

    def remote(src, dst, send, recv, dev):
        return pltpu.make_async_remote_copy(
            src_ref=src, dst_ref=dst, send_sem=send, recv_sem=recv, device_id=dev, device_id_type=MESH
        )

    def z_kv(g):
        here = at_kv(g)
        return remote(
            kvg.at[:, 0, 0, here, of[g]], kvg.at[:, 0, 1, here, of[g]], zkv_s, zkv_r.at[g], plane_kv(g)
        )

    def z_q(g):
        here = at_q(g)
        return remote(qg.at[here, 0, of[g]], qg.at[here, 1, of[g]], zq_s, zq_r.at[g], plane_q(g))

    def r_kv(g, zr, j):
        block = kvg.at[:, 0, zr, at_kv(g), of[g]]
        return remote(block, block, kv_s, kv_r.at[g, zr], ring_kv(g, j))

    def r_q(g, zr, j):
        block = qg.at[at_q(g), zr, of[g]]
        return remote(block, block, q_s, q_r.at[g], ring_q(g, j))

    def c_kv(g, zr):
        return remote(
            kvg.at[:, 0, zr, :, of[g]], kvg.at[:, 1, zr, :, of[g]], c_s, c_r.at[g, zr], dev_c
        )

    def ring_o(h, zr, j):
        g = group_of(h)
        return remote(
            op.at[zr, h, at_q(g, j)], orecv.at[zr, h, j - 1], o_s, o_r.at[zr, h], ring_q(g, j)
        )

    def z_o(h):
        return remote(zs.at[h], zr_buf.at[h], zo_s, zo_r.at[h], plane_q(group_of(h)))

    def take(ref, sem):
        pltpu.make_async_copy(ref, ref, sem).wait()

    def out_copy(h):
        return pltpu.make_async_copy(
            out_buf.at[h], out_ref.at[:, pl.ds(pl.multiple_of(h * D, D), D)], out_sem
        )

    for h in range(heads):
        for copy in local(h):
            copy.wait()
    for g in groups:
        z_q(g).start()
        z_kv(g).start()
    for j in (1, 3, 2):
        for g in groups:
            r_kv(g, 0, j).start()
            r_q(g, 0, j).start()
    for copy in tables:
        copy.wait()

    ends = [doc_ref[0]]
    for n in range(1, doc_ref.shape[0]):
        ends.append(ends[-1] + doc_ref[n])

    def doc_start(slot):
        start = jnp.int32(0)
        for end in ends:
            start = jnp.where(slot >= end, end, start)
        return start

    lane = lax.broadcasted_iota(jnp.int32, (8, NQ), 1)
    down = lax.broadcasted_iota(jnp.int32, (8, NQ), 0)
    part = lane // BLK

    def build_mask(g):
        q_pos = jnp.zeros((8, NQ), jnp.int32)
        q_low = jnp.zeros((8, NQ), jnp.int32)
        for t in range(NQ // BLK):
            zt, rt, half = t // 8, (t // 2) % 4, t % 2
            zq = z if zt == 0 else (zb if g else za)
            iq = x * NX + rt if g else rt * NX + y
            slot = slot_ref[2 * ((zq * 2 + c) * 16 + iq) + half]
            hit = part == t
            q_pos = jnp.where(hit, slot * BLK, q_pos)
            q_low = jnp.where(hit, doc_start(slot) * BLK, q_low)
        q_pos = q_pos + lane % BLK

        def mask(t, carry):
            ct, zt, rt, half = t // 16, (t // 8) % 2, (t // 2) % 4, t % 2
            zk = z + zt * ((za if g else zb) - z)
            ck = c + ct * (1 - 2 * c)
            ik = rt * NX + y if g else x * NX + rt
            slot = slot_ref[2 * ((zk * 2 + ck) * 16 + ik) + half]
            for row in range(0, BLK, 8):
                k_pos = down + (slot * BLK + row)
                seen = (k_pos <= q_pos) & (k_pos >= q_low)
                at = (zt * 2 + ct) * (NX * R) + rt * R + half * BLK + row
                term = jnp.where(seen, 0.0, HIDE)
                for tile in (0, 1):
                    bias[g, tile, pl.ds(pl.multiple_of(at, 8), 8), :] = term[:, tile * QT : (tile + 1) * QT]
            return carry

        lax.fori_loop(0, NK // BLK, mask, 0)

    def swap_cores(zr):
        for g in (1, 0):
            take(kvg.at[:, 0, zr, pl.ds(0, NX - 1), of[g]], kv_r.at[g, zr])
            c_kv(g, zr).start()

    left = lax.broadcasted_iota(jnp.int32, (1, D), 1) < R

    def swap_half(a):
        return pltpu.roll(a, R, axis=1)

    def attend(h, tile, zr):
        g = group_of(h)
        count = NK // NZ
        keys = kvg[0, :, zr, :, h].reshape(count, D)
        values = kvg[1, :, zr, :, h].reshape(count, D)
        queries = qg[:, tile, h].reshape(QT, D)
        scaled = nt(keys, queries) * SCALE2 + bias[g, tile, zr * count : (zr + 1) * count, :]
        top = jnp.max(scaled, axis=0, keepdims=True)
        top = jnp.maximum(top, FLOOR).astype(BF16).astype(F32)
        if zr:
            before = half_stat[h, tile, 0:1, :]
            top = jnp.maximum(top, before)
        terms = jnp.exp2(scaled - top)
        total = jnp.sum(terms, axis=0, keepdims=True)
        result = tn(values, terms.astype(BF16))
        if not zr:
            half_stat[h, tile, 0:1, :] = top
            half_stat[h, tile, 1:2, :] = total
            half_o[h, tile] = result
            return
        shrink = jnp.exp2(before - top)
        total = total + half_stat[h, tile, 1:2, :] * shrink
        result = result + half_o[h, tile] * shrink
        total_hi = total.astype(BF16).astype(F32)
        row = lax.broadcasted_iota(jnp.int32, (STAT, QT), 0)
        stats = jnp.where(row == 0, top, jnp.where(row == 1, total_hi, total - total_hi))
        for pair in range(NX // 2):
            span = slice(pair * D, (pair + 1) * D)
            low, high, stat = result[0:R, span], result[R:D, span], stats[:, span]
            stat_swapped = swap_half(stat)
            op[tile, h, 2 * pair, 0:R, :] = jnp.where(left, low, swap_half(high)).astype(BF16)
            op[tile, h, 2 * pair, R : R + STAT, :] = jnp.where(left, stat, stat_swapped).astype(BF16)
            op[tile, h, 2 * pair + 1, 0:R, :] = jnp.where(left, swap_half(low), high).astype(BF16)
            op[tile, h, 2 * pair + 1, R : R + STAT, :] = jnp.where(left, stat_swapped, stat).astype(BF16)

    def unstat(block):
        stat = block.astype(F32)
        return stat[0:1], stat[1:2] + stat[2:3]

    def merge_ring(h, zr):
        take(orecv.at[zr, h], o_r.at[zr, h])
        here = at_q(group_of(h))
        parts = [(op[zr, h, here, 0:R, :], unstat(op[zr, h, here, R : R + STAT, :]))]
        for j in (1, 2, 3):
            parts.append((orecv[zr, h, j - 1, 0:R, :], unstat(orecv[zr, h, j - 1, R : R + STAT, :])))
        top = functools.reduce(jnp.maximum, [p[1][0] for p in parts])
        total = jnp.zeros((1, D), F32)
        result = jnp.zeros((R, D), F32)
        for block, (m, l) in parts:
            w = jnp.exp2(m - top)
            total = total + w * l
            result = result + block.astype(F32) * w
        return result, top, total

    def merge_far(h):
        result, top, total = merge_ring(h, 1)
        total_hi = total.astype(BF16).astype(F32)
        row = lax.broadcasted_iota(jnp.int32, (STAT, D), 0)
        zs[h, 0:R, :] = result.astype(BF16)
        zs[h, R : R + STAT, :] = jnp.where(
            row == 0, top, jnp.where(row == 1, total_hi, total - total_hi)
        ).astype(BF16)
        z_o(h).start()

    def finish(h):
        result, m_own, l_own = merge_ring(h, 0)
        z_o(h).wait_recv()
        m_far, l_far = unstat(zr_buf[h, R : R + STAT, :])
        top = jnp.maximum(m_far, m_own)
        w_far, w_own = jnp.exp2(m_far - top), jnp.exp2(m_own - top)
        total = w_far * l_far + w_own * l_own
        w_far, w_own = w_far / total, w_own / total
        packed = result * w_own + zr_buf[h, 0:R, :].astype(F32) * w_far
        tall = jnp.concatenate([packed, swap_half(packed)], axis=0)
        out_buf[h] = tall.T[0:R].astype(BF16)
        out_copy(h).start()

    build_mask(0)
    build_mask(1)
    swap_cores(0)
    for g in groups:
        z_q(g).wait_recv()
        for j in (1, 3, 2):
            r_q(g, 1, j).start()
    for g in (1, 0):
        z_kv(g).wait_recv()
        for j in (1, 3, 2):
            r_kv(g, 1, j).start()
    for g in groups:
        take(qg.at[pl.ds(0, NX - 1), :, of[g]], q_r.at[g])
        c_kv(g, 0).wait_recv()

    def early(i, carry):
        attend(i, 1, 0)
        attend(i, 0, 0)
        return carry

    lax.fori_loop(0, heads, early, 0)
    swap_cores(1)
    for g in (1, 0):
        c_kv(g, 1).wait_recv()

    def head_of(unit):
        return lax.rem(unit * first_heads, heads)

    def late(i, carry):
        @pl.when(i < heads)
        def _():
            units = (2 * i, 2 * i + 1)
            works = [(head_of(unit), jnp.where(unit < heads, 1, 0)) for unit in units]
            for h, tile in works:
                attend(h, tile, 1)
            for h, tile in works:
                for j in (1, 3, 2):
                    ring_o(h, tile, j).start()

        for k in (0, 1):
            unit = 2 * (i - 2) + k

            @pl.when((unit >= 0) & (unit < heads))
            def _():
                merge_far(head_of(unit))

            @pl.when(unit >= heads)
            def _():
                finish(head_of(unit))

        return carry

    lax.fori_loop(0, heads + 2, late, 0)

    take(kvg.at[:, 0, 0, 0], zkv_s)
    take(qg.at[0, 0], zq_s)
    take(kvg.at[:, 0, :, pl.ds(0, NX - 1)], kv_s)
    take(qg.at[pl.ds(0, NX - 1)], q_s)
    take(kvg.at[:, 0], c_s)
    take(orecv, o_s)
    take(zs, zo_s)
    take(out_buf, out_sem)


def per_device(queries, keys, values, slot_blocks, doc_blocks):
    width = queries.shape[1]
    heads = width // D
    dma = pltpu.SemaphoreType.DMA
    anywhere = pl.BlockSpec(memory_space=pltpu.HBM)
    return pl.pallas_call(
        functools.partial(kernel, heads),
        out_shape=jax.ShapeDtypeStruct(queries.shape, BF16),
        in_specs=[anywhere] * 5,
        out_specs=anywhere,
        scratch_shapes=[
            pltpu.SMEM(slot_blocks.shape, jnp.int32),
            pltpu.SMEM(doc_blocks.shape, jnp.int32),
            pltpu.VMEM((NX, NZ, heads, R, D), BF16),
            pltpu.VMEM((2, NC, NZ, NX, heads, R, D), BF16),
            pltpu.VMEM((2, NZ, NK, QT), F32),
            pltpu.VMEM((heads, NZ, D, QT), F32),
            pltpu.VMEM((heads, NZ, 8, QT), F32),
            pltpu.VMEM((NZ, heads, NX, R + STAT, D), BF16),
            pltpu.VMEM((NZ, heads, NX - 1, R + STAT, D), BF16),
            pltpu.VMEM((heads, R + STAT, D), BF16),
            pltpu.VMEM((heads, R + STAT, D), BF16),
            pltpu.VMEM((heads, R, D), BF16),
            dma((2,)),
            dma((3, heads)),
            dma, dma((2,)), dma, dma((2,)),
            dma, dma((2, 2)), dma, dma((2,)),
            dma, dma((2, 2)),
            dma, dma((2, heads)),
            dma, dma((heads,)), dma,
        ],
        compiler_params=pltpu.CompilerParams(
            collective_id=0, has_side_effects=True, vmem_limit_bytes=64 * 1024 * 1024
        ),
        cost_estimate=pl.CostEstimate(
            flops=4 * heads * NQ * NK * D, bytes_accessed=4 * queries.size * 2, transcendentals=heads * NQ * NK
        ),
    )(queries, keys, values, slot_blocks, doc_blocks)


def solution(mesh):
    rows = P(("outer", "inner"), "head")
    return jax.shard_map(
        per_device,
        mesh=mesh,
        in_specs=(rows, rows, rows, P(), P()),
        out_specs=rows,
        check_vma=False,
    )
```

```python
import functools
import math

import jax
import jax.numpy as jnp
from jax import lax
from jax.experimental import pallas as pl
from jax.experimental.pallas import tpu as pltpu
from jax.sharding import PartitionSpec as P

D = 128
BLK = 32
R = 64
NX = 4
NZ = 2
NC = 2
NQ = NX * NZ * R
QT = NX * R
NK = NC * NZ * NX * R
STAT = 16
SCALE2 = D ** (-0.5) * math.log2(math.e)
HIDE = -1e30
FLOOR = -1e29
MESH = pl.DeviceIdType.MESH
F32 = jnp.float32
BF16 = jnp.bfloat16


def nt(a, b):
    return lax.dot_general(a, b, (((1,), (1,)), ((), ())), preferred_element_type=F32)


def tn(a, b):
    return lax.dot_general(a, b, (((0,), (0,)), ((), ())), preferred_element_type=F32)


def kernel(
    heads,
    q_ref, k_ref, v_ref, slot_hbm, doc_hbm, out_ref,
    slot_ref, doc_ref, qg, kvg, bias, half_o, half_stat, op, orecv, zs, zr_buf, out_buf,
    tab_sem, loc_sem, zkv_s, zkv_r, zq_s, zq_r, kv_s, kv_r, q_s, q_r, c_s, c_r, o_s, o_r, zo_s, zo_r, out_sem,
):
    outer = lax.axis_index("outer")
    inner = lax.axis_index("inner")
    z, c = outer // 2, outer % 2
    x, y = inner // NX, inner % NX
    za = z + 1 - 2 * (z % 2)
    zb = 3 - z
    dev_c = {"outer": z * 2 + 1 - c, "inner": inner}
    first_heads = (heads + 1) // 2
    groups = (0, 1)
    of = (pl.ds(0, first_heads), pl.ds(first_heads, heads - first_heads))

    def pick(g, even, odd):
        return even + g * (odd - even)

    def group_of(h):
        return h // first_heads

    def plane_q(g):
        return {"outer": pick(g, za, zb) * 2 + c, "inner": inner}

    def plane_kv(g):
        return {"outer": pick(g, zb, za) * 2 + c, "inner": inner}

    def along_x(j):
        return lax.rem(x + j, NX) * NX + y

    def along_y(j):
        return x * NX + lax.rem(y + j, NX)

    def ring_q(g, j):
        return {"outer": outer, "inner": pick(g, along_x(j), along_y(j))}

    def ring_kv(g, j):
        return {"outer": outer, "inner": pick(g, along_y(j), along_x(j))}

    def at_q(g, j=0):
        return lax.rem(pick(g, x, y) + j, NX)

    def at_kv(g, j=0):
        return lax.rem(pick(g, y, x) + j, NX)

    tables = (
        pltpu.make_async_copy(slot_hbm, slot_ref, tab_sem.at[0]),
        pltpu.make_async_copy(doc_hbm, doc_ref, tab_sem.at[1]),
    )

    def local(h):
        at = pl.ds(h * D, D)
        g = group_of(h)
        return (
            pltpu.make_async_copy(q_ref.at[:, at], qg.at[at_q(g), 0, h], loc_sem.at[2, h]),
            pltpu.make_async_copy(k_ref.at[:, at], kvg.at[0, 0, 0, at_kv(g), h], loc_sem.at[0, h]),
            pltpu.make_async_copy(v_ref.at[:, at], kvg.at[1, 0, 0, at_kv(g), h], loc_sem.at[1, h]),
        )

    for h in range(heads):
        for copy in local(h):
            copy.start()
    for copy in tables:
        copy.start()

    barrier = pltpu.get_barrier_semaphore()
    partners = [plane_q(0), plane_kv(0), dev_c]
    partners += [ring_q(0, j) for j in (1, 2, 3)] + [ring_kv(0, j) for j in (1, 2, 3)]
    for dev in partners:
        pl.semaphore_signal(barrier, inc=1, device_id=dev, device_id_type=MESH)
    pl.semaphore_wait(barrier, len(partners))

    def remote(src, dst, send, recv, dev):
        return pltpu.make_async_remote_copy(
            src_ref=src, dst_ref=dst, send_sem=send, recv_sem=recv, device_id=dev, device_id_type=MESH
        )

    def z_kv(g):
        here = at_kv(g)
        return remote(
            kvg.at[:, 0, 0, here, of[g]], kvg.at[:, 0, 1, here, of[g]], zkv_s, zkv_r.at[g], plane_kv(g)
        )

    def z_q(g):
        here = at_q(g)
        return remote(qg.at[here, 0, of[g]], qg.at[here, 1, of[g]], zq_s, zq_r.at[g], plane_q(g))

    def r_kv(g, zr, j):
        block = kvg.at[:, 0, zr, at_kv(g), of[g]]
        return remote(block, block, kv_s, kv_r.at[g, zr], ring_kv(g, j))

    def r_q(g, zr, j):
        block = qg.at[at_q(g), zr, of[g]]
        return remote(block, block, q_s, q_r.at[g, zr], ring_q(g, j))

    def c_kv(g, zr):
        return remote(
            kvg.at[:, 0, zr, :, of[g]], kvg.at[:, 1, zr, :, of[g]], c_s, c_r.at[g, zr], dev_c
        )

    def ring_o(h, zr, j):
        g = group_of(h)
        return remote(
            op.at[zr, h, at_q(g, j)], orecv.at[zr, h, j - 1], o_s, o_r.at[zr, h], ring_q(g, j)
        )

    def z_o(h):
        return remote(zs.at[h], zr_buf.at[h], zo_s, zo_r.at[h], plane_q(group_of(h)))

    def take(ref, sem):
        pltpu.make_async_copy(ref, ref, sem).wait()

    def out_copy(h):
        return pltpu.make_async_copy(
            out_buf.at[h], out_ref.at[:, pl.ds(pl.multiple_of(h * D, D), D)], out_sem
        )

    for h in range(heads):
        for copy in local(h):
            copy.wait()
    for g in groups:
        z_q(g).start()
        z_kv(g).start()
    for j in (1, 3, 2):
        for g in groups:
            r_kv(g, 0, j).start()
            r_q(g, 0, j).start()
    for copy in tables:
        copy.wait()

    ends = [doc_ref[0]]
    for n in range(1, doc_ref.shape[0]):
        ends.append(ends[-1] + doc_ref[n])

    def doc_start(slot):
        start = jnp.int32(0)
        for end in ends:
            start = jnp.where(slot >= end, end, start)
        return start

    lane = lax.broadcasted_iota(jnp.int32, (8, NQ), 1)
    down = lax.broadcasted_iota(jnp.int32, (8, NQ), 0)
    part = lane // BLK

    def build_mask(g):
        q_pos = jnp.zeros((8, NQ), jnp.int32)
        q_low = jnp.zeros((8, NQ), jnp.int32)
        for t in range(NQ // BLK):
            zt, rt, half = t // 8, (t // 2) % 4, t % 2
            zq = z if zt == 0 else (zb if g else za)
            iq = x * NX + rt if g else rt * NX + y
            slot = slot_ref[2 * ((zq * 2 + c) * 16 + iq) + half]
            hit = part == t
            q_pos = jnp.where(hit, slot * BLK, q_pos)
            q_low = jnp.where(hit, doc_start(slot) * BLK, q_low)
        q_pos = q_pos + lane % BLK

        def mask(t, carry):
            ct, zt, rt, half = t // 16, (t // 8) % 2, (t // 2) % 4, t % 2
            zk = z + zt * ((za if g else zb) - z)
            ck = c + ct * (1 - 2 * c)
            ik = rt * NX + y if g else x * NX + rt
            slot = slot_ref[2 * ((zk * 2 + ck) * 16 + ik) + half]
            for row in range(0, BLK, 8):
                k_pos = down + (slot * BLK + row)
                seen = (k_pos <= q_pos) & (k_pos >= q_low)
                at = (zt * 2 + ct) * (NX * R) + rt * R + half * BLK + row
                term = jnp.where(seen, 0.0, HIDE)
                for tile in (0, 1):
                    bias[g, tile, pl.ds(pl.multiple_of(at, 8), 8), :] = term[:, tile * QT : (tile + 1) * QT]
            return carry

        lax.fori_loop(0, NK // BLK, mask, 0)

    def swap_cores(zr):
        for g in (1, 0):
            take(kvg.at[:, 0, zr, pl.ds(0, NX - 1), of[g]], kv_r.at[g, zr])
            c_kv(g, zr).start()

    left = lax.broadcasted_iota(jnp.int32, (1, D), 1) < R

    def swap_half(a):
        return pltpu.roll(a, R, axis=1)

    def attend(h, tile, stage):
        g = group_of(h)
        cores, zr = ((slice(0, 2), 0), (slice(0, 1), 1), (slice(1, 2), 1))[stage]
        start, count = ((0, 512), (512, 256), (768, 256))[stage]
        keys = kvg[0, cores, zr, :, h].reshape(count, D)
        values = kvg[1, cores, zr, :, h].reshape(count, D)
        queries = qg[:, tile, h].reshape(QT, D)
        scaled = nt(keys, queries) * SCALE2 + bias[g, tile, start : start + count, :]
        top = jnp.max(scaled, axis=0, keepdims=True)
        top = jnp.maximum(top, FLOOR).astype(BF16).astype(F32)
        if stage:
            before = half_stat[h, tile, 0:1, :]
            top = jnp.maximum(top, before)
        terms = jnp.exp2(scaled - top)
        total = jnp.sum(terms, axis=0, keepdims=True)
        result = tn(values, terms.astype(BF16))
        if stage:
            shrink = jnp.exp2(before - top)
            total = total + half_stat[h, tile, 1:2, :] * shrink
            result = result + half_o[h, tile] * shrink
        if stage < 2:
            half_stat[h, tile, 0:1, :] = top
            half_stat[h, tile, 1:2, :] = total
            half_o[h, tile] = result
            return
        total_hi = total.astype(BF16).astype(F32)
        row = lax.broadcasted_iota(jnp.int32, (STAT, QT), 0)
        stats = jnp.where(row == 0, top, jnp.where(row == 1, total_hi, total - total_hi))
        for pair in range(NX // 2):
            span = slice(pair * D, (pair + 1) * D)
            low, high, stat = result[0:R, span], result[R:D, span], stats[:, span]
            stat_swapped = swap_half(stat)
            op[tile, h, 2 * pair, 0:R, :] = jnp.where(left, low, swap_half(high)).astype(BF16)
            op[tile, h, 2 * pair, R : R + STAT, :] = jnp.where(left, stat, stat_swapped).astype(BF16)
            op[tile, h, 2 * pair + 1, 0:R, :] = jnp.where(left, swap_half(low), high).astype(BF16)
            op[tile, h, 2 * pair + 1, R : R + STAT, :] = jnp.where(left, stat_swapped, stat).astype(BF16)

    def unstat(block):
        stat = block.astype(F32)
        return stat[0:1], stat[1:2] + stat[2:3]

    def merge_ring(h, zr):
        take(orecv.at[zr, h], o_r.at[zr, h])
        here = at_q(group_of(h))
        parts = [(op[zr, h, here, 0:R, :], unstat(op[zr, h, here, R : R + STAT, :]))]
        for j in (1, 2, 3):
            parts.append((orecv[zr, h, j - 1, 0:R, :], unstat(orecv[zr, h, j - 1, R : R + STAT, :])))
        top = functools.reduce(jnp.maximum, [p[1][0] for p in parts])
        total = jnp.zeros((1, D), F32)
        result = jnp.zeros((R, D), F32)
        for block, (m, l) in parts:
            w = jnp.exp2(m - top)
            total = total + w * l
            result = result + block.astype(F32) * w
        return result, top, total

    def merge_far(h):
        result, top, total = merge_ring(h, 1)
        total_hi = total.astype(BF16).astype(F32)
        row = lax.broadcasted_iota(jnp.int32, (STAT, D), 0)
        zs[h, 0:R, :] = result.astype(BF16)
        zs[h, R : R + STAT, :] = jnp.where(
            row == 0, top, jnp.where(row == 1, total_hi, total - total_hi)
        ).astype(BF16)
        z_o(h).start()

    def finish(h):
        result, m_own, l_own = merge_ring(h, 0)
        z_o(h).wait_recv()
        m_far, l_far = unstat(zr_buf[h, R : R + STAT, :])
        top = jnp.maximum(m_far, m_own)
        w_far, w_own = jnp.exp2(m_far - top), jnp.exp2(m_own - top)
        total = w_far * l_far + w_own * l_own
        w_far, w_own = w_far / total, w_own / total
        packed = result * w_own + zr_buf[h, 0:R, :].astype(F32) * w_far
        tall = jnp.concatenate([packed, swap_half(packed)], axis=0)
        out_buf[h] = tall.T[0:R].astype(BF16)
        out_copy(h).start()

    build_mask(0)
    build_mask(1)
    swap_cores(0)
    for g in groups:
        z_q(g).wait_recv()
        for j in (1, 3, 2):
            r_q(g, 1, j).start()
    for g in groups:
        take(qg.at[pl.ds(0, NX - 1), 0, of[g]], q_r.at[g, 0])
        c_kv(g, 0).wait_recv()
    for h in range(heads):
        attend(h, 0, 0)
    for g in (1, 0):
        z_kv(g).wait_recv()
        for j in (1, 3, 2):
            r_kv(g, 1, j).start()
    for g in groups:
        take(qg.at[pl.ds(0, NX - 1), 1, of[g]], q_r.at[g, 1])
    for h in range(heads):
        attend(h, 1, 0)
    swap_cores(1)

    def middle(h, carry):
        attend(h, 1, 1)
        attend(h, 0, 1)
        return carry

    lax.fori_loop(0, heads, middle, 0)
    for g in (1, 0):
        c_kv(g, 1).wait_recv()

    def head_of(unit):
        return lax.rem(unit * first_heads, heads)

    def late(i, carry):
        @pl.when(i < heads)
        def _():
            units = (2 * i, 2 * i + 1)
            works = [(head_of(unit), jnp.where(unit < heads, 1, 0)) for unit in units]
            for h, tile in works:
                attend(h, tile, 2)
            for h, tile in works:
                for j in (1, 3, 2):
                    ring_o(h, tile, j).start()

        for k in (0, 1):
            unit = 2 * (i - 2) + k

            @pl.when((unit >= 0) & (unit < heads))
            def _():
                merge_far(head_of(unit))

            @pl.when(unit >= heads)
            def _():
                finish(head_of(unit))

        return carry

    lax.fori_loop(0, heads + 2, late, 0)

    take(kvg.at[:, 0, 0, 0], zkv_s)
    take(qg.at[0, 0], zq_s)
    take(kvg.at[:, 0, :, pl.ds(0, NX - 1)], kv_s)
    take(qg.at[pl.ds(0, NX - 1)], q_s)
    take(kvg.at[:, 0], c_s)
    take(orecv, o_s)
    take(zs, zo_s)
    take(out_buf, out_sem)


def per_device(queries, keys, values, slot_blocks, doc_blocks):
    width = queries.shape[1]
    heads = width // D
    dma = pltpu.SemaphoreType.DMA
    anywhere = pl.BlockSpec(memory_space=pltpu.HBM)
    return pl.pallas_call(
        functools.partial(kernel, heads),
        out_shape=jax.ShapeDtypeStruct(queries.shape, BF16),
        in_specs=[anywhere] * 5,
        out_specs=anywhere,
        scratch_shapes=[
            pltpu.SMEM(slot_blocks.shape, jnp.int32),
            pltpu.SMEM(doc_blocks.shape, jnp.int32),
            pltpu.VMEM((NX, NZ, heads, R, D), BF16),
            pltpu.VMEM((2, NC, NZ, NX, heads, R, D), BF16),
            pltpu.VMEM((2, NZ, NK, QT), F32),
            pltpu.VMEM((heads, NZ, D, QT), F32),
            pltpu.VMEM((heads, NZ, 8, QT), F32),
            pltpu.VMEM((NZ, heads, NX, R + STAT, D), BF16),
            pltpu.VMEM((NZ, heads, NX - 1, R + STAT, D), BF16),
            pltpu.VMEM((heads, R + STAT, D), BF16),
            pltpu.VMEM((heads, R + STAT, D), BF16),
            pltpu.VMEM((heads, R, D), BF16),
            dma((2,)),
            dma((3, heads)),
            dma, dma((2,)), dma, dma((2,)),
            dma, dma((2, 2)), dma, dma((2, 2)),
            dma, dma((2, 2)),
            dma, dma((2, heads)),
            dma, dma((heads,)), dma,
        ],
        compiler_params=pltpu.CompilerParams(
            collective_id=0, has_side_effects=True, vmem_limit_bytes=64 * 1024 * 1024
        ),
        cost_estimate=pl.CostEstimate(
            flops=4 * heads * NQ * NK * D, bytes_accessed=4 * queries.size * 2, transcendentals=heads * NQ * NK
        ),
    )(queries, keys, values, slot_blocks, doc_blocks)


def solution(mesh):
    rows = P(("outer", "inner"), "head")
    return jax.shard_map(
        per_device,
        mesh=mesh,
        in_specs=(rows, rows, rows, P(), P()),
        out_specs=rows,
        check_vma=False,
    )
```

```python
import functools
import math

import jax
import jax.numpy as jnp
from jax import lax
from jax.experimental import pallas as pl
from jax.experimental.pallas import tpu as pltpu
from jax.sharding import PartitionSpec as P

D = 128
BLK = 32
R = 64
NX = 4
NZ = 2
NC = 2
NQ = NX * NZ * R
QT = NX * R
NK = NC * NZ * NX * R
STAT = 16
SCALE2 = D ** (-0.5) * math.log2(math.e)
HIDE = -1e30
FLOOR = -1e29
MESH = pl.DeviceIdType.MESH
F32 = jnp.float32
BF16 = jnp.bfloat16


def nt(a, b):
    return lax.dot_general(a, b, (((1,), (1,)), ((), ())), preferred_element_type=F32)


def nn(a, b):
    return jnp.dot(a, b, preferred_element_type=F32)


def kernel(
    heads,
    q_ref, k_ref, v_ref, slot_hbm, doc_hbm, out_ref,
    slot_ref, doc_ref, qg, kvg, vt, bias, half_o, half_stat, op, orecv, zs, zr_buf, out_buf,
    tab_sem, loc_sem, zkv_s, zkv_r, zq_s, zq_r, kv_s, kv_r, q_s, q_r, c_s, c_r, cv_s, cv_r, o_s, o_r, zo_s, zo_r, out_sem,
):
    outer = lax.axis_index("outer")
    inner = lax.axis_index("inner")
    z, c = outer // 2, outer % 2
    x, y = inner // NX, inner % NX
    za = z + 1 - 2 * (z % 2)
    zb = 3 - z
    dev_c = {"outer": z * 2 + 1 - c, "inner": inner}
    first_heads = (heads + 1) // 2
    groups = (0, 1)
    heads_of = (range(first_heads), range(first_heads, heads))
    of = (pl.ds(0, first_heads), pl.ds(first_heads, heads - first_heads))

    def pick(g, even, odd):
        return even + g * (odd - even)

    def group_of(h):
        return h // first_heads

    def plane_q(g):
        return {"outer": pick(g, za, zb) * 2 + c, "inner": inner}

    def plane_kv(g):
        return {"outer": pick(g, zb, za) * 2 + c, "inner": inner}

    def along_x(j):
        return lax.rem(x + j, NX) * NX + y

    def along_y(j):
        return x * NX + lax.rem(y + j, NX)

    def ring_q(g, j):
        return {"outer": outer, "inner": pick(g, along_x(j), along_y(j))}

    def ring_kv(g, j):
        return {"outer": outer, "inner": pick(g, along_y(j), along_x(j))}

    def at_q(g, j=0):
        return lax.rem(pick(g, x, y) + j, NX)

    def at_kv(g, j=0):
        return lax.rem(pick(g, y, x) + j, NX)

    tables = (
        pltpu.make_async_copy(slot_hbm, slot_ref, tab_sem.at[0]),
        pltpu.make_async_copy(doc_hbm, doc_ref, tab_sem.at[1]),
    )

    def local(h):
        at = pl.ds(h * D, D)
        g = group_of(h)
        return (
            pltpu.make_async_copy(q_ref.at[:, at], qg.at[at_q(g), 0, h], loc_sem.at[2, h]),
            pltpu.make_async_copy(k_ref.at[:, at], kvg.at[0, 0, 0, at_kv(g), h], loc_sem.at[0, h]),
            pltpu.make_async_copy(v_ref.at[:, at], kvg.at[1, 0, 0, at_kv(g), h], loc_sem.at[1, h]),
        )

    for h in range(heads):
        for copy in local(h):
            copy.start()
    for copy in tables:
        copy.start()

    barrier = pltpu.get_barrier_semaphore()
    partners = [plane_q(0), plane_kv(0), dev_c]
    partners += [ring_q(0, j) for j in (1, 2, 3)] + [ring_kv(0, j) for j in (1, 2, 3)]
    for dev in partners:
        pl.semaphore_signal(barrier, inc=1, device_id=dev, device_id_type=MESH)
    pl.semaphore_wait(barrier, len(partners))

    def remote(src, dst, send, recv, dev):
        return pltpu.make_async_remote_copy(
            src_ref=src, dst_ref=dst, send_sem=send, recv_sem=recv, device_id=dev, device_id_type=MESH
        )

    def z_kv(g):
        here = at_kv(g)
        return remote(
            kvg.at[:, 0, 0, here, of[g]], kvg.at[:, 0, 1, here, of[g]], zkv_s, zkv_r.at[g], plane_kv(g)
        )

    def z_q(g):
        here = at_q(g)
        return remote(qg.at[here, 0, of[g]], qg.at[here, 1, of[g]], zq_s, zq_r.at[g], plane_q(g))

    def r_kv(g, zr, j):
        block = kvg.at[:, 0, zr, at_kv(g), of[g]]
        return remote(block, block, kv_s, kv_r.at[g, zr], ring_kv(g, j))

    def r_q(g, zr, j):
        block = qg.at[at_q(g), zr, of[g]]
        return remote(block, block, q_s, q_r.at[g], ring_q(g, j))

    def c_k(g, zr):
        return remote(
            kvg.at[0, 0, zr, :, of[g]], kvg.at[0, 1, zr, :, of[g]], c_s, c_r.at[g, zr], dev_c
        )

    def c_v(g, zr):
        return remote(vt.at[zr, 0, of[g]], vt.at[zr, 1, of[g]], cv_s, cv_r.at[g, zr], dev_c)

    def ring_o(h, zr, j):
        g = group_of(h)
        return remote(
            op.at[zr, h, at_q(g, j)], orecv.at[zr, h, j - 1], o_s, o_r.at[zr, h], ring_q(g, j)
        )

    def z_o(h):
        return remote(zs.at[h], zr_buf.at[h], zo_s, zo_r.at[h], plane_q(group_of(h)))

    def take(ref, sem):
        pltpu.make_async_copy(ref, ref, sem).wait()

    def out_copy(h):
        return pltpu.make_async_copy(
            out_buf.at[h], out_ref.at[:, pl.ds(pl.multiple_of(h * D, D), D)], out_sem
        )

    for h in range(heads):
        for copy in local(h):
            copy.wait()
    for g in groups:
        z_q(g).start()
        z_kv(g).start()
    for j in (1, 3, 2):
        for g in groups:
            r_kv(g, 0, j).start()
            r_q(g, 0, j).start()
    for copy in tables:
        copy.wait()

    ends = [doc_ref[0]]
    for n in range(1, doc_ref.shape[0]):
        ends.append(ends[-1] + doc_ref[n])

    def doc_start(slot):
        start = jnp.int32(0)
        for end in ends:
            start = jnp.where(slot >= end, end, start)
        return start

    lane = lax.broadcasted_iota(jnp.int32, (8, NQ), 1)
    down = lax.broadcasted_iota(jnp.int32, (8, NQ), 0)
    part = lane // BLK

    def build_mask(g):
        q_pos = jnp.zeros((8, NQ), jnp.int32)
        q_low = jnp.zeros((8, NQ), jnp.int32)
        for t in range(NQ // BLK):
            zt, rt, half = t // 8, (t // 2) % 4, t % 2
            zq = z if zt == 0 else (zb if g else za)
            iq = x * NX + rt if g else rt * NX + y
            slot = slot_ref[2 * ((zq * 2 + c) * 16 + iq) + half]
            hit = part == t
            q_pos = jnp.where(hit, slot * BLK, q_pos)
            q_low = jnp.where(hit, doc_start(slot) * BLK, q_low)
        q_pos = q_pos + lane % BLK

        def mask(t, carry):
            ct, zt, rt, half = t // 16, (t // 8) % 2, (t // 2) % 4, t % 2
            zk = z + zt * ((za if g else zb) - z)
            ck = c + ct * (1 - 2 * c)
            ik = rt * NX + y if g else x * NX + rt
            slot = slot_ref[2 * ((zk * 2 + ck) * 16 + ik) + half]
            for row in range(0, BLK, 8):
                k_pos = down + (slot * BLK + row)
                seen = (k_pos <= q_pos) & (k_pos >= q_low)
                at = (zt * 2 + ct) * (NX * R) + rt * R + half * BLK + row
                term = jnp.where(seen, 0.0, HIDE)
                for tile in (0, 1):
                    bias[g, tile, pl.ds(pl.multiple_of(at, 8), 8), :] = term[:, tile * QT : (tile + 1) * QT]
            return carry

        lax.fori_loop(0, NK // BLK, mask, 0)

    def swap_cores(zr):
        for g in (1, 0):
            take(kvg.at[:, 0, zr, pl.ds(0, NX - 1), of[g]], kv_r.at[g, zr])
            c_k(g, zr).start()
            for h in heads_of[g]:
                vt[zr, 0, h] = kvg[1, 0, zr, :, h].reshape(NX * R, D).T
            c_v(g, zr).start()

    left = lax.broadcasted_iota(jnp.int32, (1, D), 1) < R

    def swap_half(a):
        return pltpu.roll(a, R, axis=1)

    def attend(h, tile, zr):
        g = group_of(h)
        count = NK // NZ
        keys = kvg[0, :, zr, :, h].reshape(count, D)
        queries = qg[:, tile, h].reshape(QT, D)
        scaled = nt(keys, queries) * SCALE2 + bias[g, tile, zr * count : (zr + 1) * count, :]
        top = jnp.max(scaled, axis=0, keepdims=True)
        top = jnp.maximum(top, FLOOR).astype(BF16).astype(F32)
        if zr:
            before = half_stat[h, tile, 0:1, :]
            top = jnp.maximum(top, before)
        terms = jnp.exp2(scaled - top)
        total = jnp.sum(terms, axis=0, keepdims=True)
        weights = terms.astype(BF16)
        result = nn(vt[zr, 0, h], weights[0 : count // 2]) + nn(vt[zr, 1, h], weights[count // 2 :])
        if not zr:
            half_stat[h, tile, 0:1, :] = top
            half_stat[h, tile, 1:2, :] = total
            half_o[h, tile] = result
            return
        shrink = jnp.exp2(before - top)
        total = total + half_stat[h, tile, 1:2, :] * shrink
        result = result + half_o[h, tile] * shrink
        total_hi = total.astype(BF16).astype(F32)
        row = lax.broadcasted_iota(jnp.int32, (STAT, QT), 0)
        stats = jnp.where(row == 0, top, jnp.where(row == 1, total_hi, total - total_hi))
        for pair in range(NX // 2):
            span = slice(pair * D, (pair + 1) * D)
            low, high, stat = result[0:R, span], result[R:D, span], stats[:, span]
            stat_swapped = swap_half(stat)
            op[tile, h, 2 * pair, 0:R, :] = jnp.where(left, low, swap_half(high)).astype(BF16)
            op[tile, h, 2 * pair, R : R + STAT, :] = jnp.where(left, stat, stat_swapped).astype(BF16)
            op[tile, h, 2 * pair + 1, 0:R, :] = jnp.where(left, swap_half(low), high).astype(BF16)
            op[tile, h, 2 * pair + 1, R : R + STAT, :] = jnp.where(left, stat_swapped, stat).astype(BF16)

    def unstat(block):
        stat = block.astype(F32)
        return stat[0:1], stat[1:2] + stat[2:3]

    def merge_ring(h, zr):
        take(orecv.at[zr, h], o_r.at[zr, h])
        here = at_q(group_of(h))
        parts = [(op[zr, h, here, 0:R, :], unstat(op[zr, h, here, R : R + STAT, :]))]
        for j in (1, 2, 3):
            parts.append((orecv[zr, h, j - 1, 0:R, :], unstat(orecv[zr, h, j - 1, R : R + STAT, :])))
        top = functools.reduce(jnp.maximum, [p[1][0] for p in parts])
        total = jnp.zeros((1, D), F32)
        result = jnp.zeros((R, D), F32)
        for block, (m, l) in parts:
            w = jnp.exp2(m - top)
            total = total + w * l
            result = result + block.astype(F32) * w
        return result, top, total

    def merge_far(h):
        result, top, total = merge_ring(h, 1)
        total_hi = total.astype(BF16).astype(F32)
        row = lax.broadcasted_iota(jnp.int32, (STAT, D), 0)
        zs[h, 0:R, :] = result.astype(BF16)
        zs[h, R : R + STAT, :] = jnp.where(
            row == 0, top, jnp.where(row == 1, total_hi, total - total_hi)
        ).astype(BF16)
        z_o(h).start()

    def finish(h):
        result, m_own, l_own = merge_ring(h, 0)
        z_o(h).wait_recv()
        m_far, l_far = unstat(zr_buf[h, R : R + STAT, :])
        top = jnp.maximum(m_far, m_own)
        w_far, w_own = jnp.exp2(m_far - top), jnp.exp2(m_own - top)
        total = w_far * l_far + w_own * l_own
        w_far, w_own = w_far / total, w_own / total
        packed = result * w_own + zr_buf[h, 0:R, :].astype(F32) * w_far
        tall = jnp.concatenate([packed, swap_half(packed)], axis=0)
        out_buf[h] = tall.T[0:R].astype(BF16)
        out_copy(h).start()

    build_mask(0)
    build_mask(1)
    swap_cores(0)
    for g in groups:
        z_q(g).wait_recv()
        for j in (1, 3, 2):
            r_q(g, 1, j).start()
    for g in (1, 0):
        z_kv(g).wait_recv()
        for j in (1, 3, 2):
            r_kv(g, 1, j).start()
    for g in groups:
        take(qg.at[pl.ds(0, NX - 1), :, of[g]], q_r.at[g])
        c_k(g, 0).wait_recv()
        c_v(g, 0).wait_recv()

    def early(i, carry):
        attend(i, 1, 0)
        attend(i, 0, 0)
        return carry

    lax.fori_loop(0, heads, early, 0)
    swap_cores(1)
    for g in (1, 0):
        c_k(g, 1).wait_recv()
        c_v(g, 1).wait_recv()

    def head_of(unit):
        return lax.rem(unit * first_heads, heads)

    def late(i, carry):
        @pl.when(i < heads)
        def _():
            units = (2 * i, 2 * i + 1)
            works = [(head_of(unit), jnp.where(unit < heads, 1, 0)) for unit in units]
            for h, tile in works:
                attend(h, tile, 1)
            for h, tile in works:
                for j in (1, 3, 2):
                    ring_o(h, tile, j).start()

        for k in (0, 1):
            unit = 2 * (i - 2) + k

            @pl.when((unit >= 0) & (unit < heads))
            def _():
                merge_far(head_of(unit))

            @pl.when(unit >= heads)
            def _():
                finish(head_of(unit))

        return carry

    lax.fori_loop(0, heads + 2, late, 0)

    take(kvg.at[:, 0, 0, 0], zkv_s)
    take(qg.at[0, 0], zq_s)
    take(kvg.at[:, 0, :, pl.ds(0, NX - 1)], kv_s)
    take(qg.at[pl.ds(0, NX - 1)], q_s)
    take(kvg.at[0, 0], c_s)
    take(vt.at[:, 0], cv_s)
    take(orecv, o_s)
    take(zs, zo_s)
    take(out_buf, out_sem)


def per_device(queries, keys, values, slot_blocks, doc_blocks):
    width = queries.shape[1]
    heads = width // D
    dma = pltpu.SemaphoreType.DMA
    anywhere = pl.BlockSpec(memory_space=pltpu.HBM)
    return pl.pallas_call(
        functools.partial(kernel, heads),
        out_shape=jax.ShapeDtypeStruct(queries.shape, BF16),
        in_specs=[anywhere] * 5,
        out_specs=anywhere,
        scratch_shapes=[
            pltpu.SMEM(slot_blocks.shape, jnp.int32),
            pltpu.SMEM(doc_blocks.shape, jnp.int32),
            pltpu.VMEM((NX, NZ, heads, R, D), BF16),
            pltpu.VMEM((2, NC, NZ, NX, heads, R, D), BF16),
            pltpu.VMEM((NZ, NC, heads, D, NX * R), BF16),
            pltpu.VMEM((2, NZ, NK, QT), F32),
            pltpu.VMEM((heads, NZ, D, QT), F32),
            pltpu.VMEM((heads, NZ, 8, QT), F32),
            pltpu.VMEM((NZ, heads, NX, R + STAT, D), BF16),
            pltpu.VMEM((NZ, heads, NX - 1, R + STAT, D), BF16),
            pltpu.VMEM((heads, R + STAT, D), BF16),
            pltpu.VMEM((heads, R + STAT, D), BF16),
            pltpu.VMEM((heads, R, D), BF16),
            dma((2,)),
            dma((3, heads)),
            dma, dma((2,)), dma, dma((2,)),
            dma, dma((2, 2)), dma, dma((2,)),
            dma, dma((2, 2)),
            dma, dma((2, 2)),
            dma, dma((2, heads)),
            dma, dma((heads,)), dma,
        ],
        compiler_params=pltpu.CompilerParams(
            collective_id=0, has_side_effects=True, vmem_limit_bytes=64 * 1024 * 1024
        ),
        cost_estimate=pl.CostEstimate(
            flops=4 * heads * NQ * NK * D, bytes_accessed=4 * queries.size * 2, transcendentals=heads * NQ * NK
        ),
    )(queries, keys, values, slot_blocks, doc_blocks)


def solution(mesh):
    rows = P(("outer", "inner"), "head")
    return jax.shard_map(
        per_device,
        mesh=mesh,
        in_specs=(rows, rows, rows, P(), P()),
        out_specs=rows,
        check_vma=False,
    )
```

```python
import functools
import math

import jax
import jax.numpy as jnp
from jax import lax
from jax.experimental import pallas as pl
from jax.experimental.pallas import tpu as pltpu
from jax.sharding import PartitionSpec as P

D = 128
BLK = 32
R = 64
NX = 4
NZ = 2
NC = 2
NQ = NX * NZ * R
QT = NX * R
KT = NC * NX * BLK
NK = NC * NZ * NX * R
STAT = 16
SCALE2 = D ** (-0.5) * math.log2(math.e)
HIDE = -1e30
FLOOR = -1e29
MESH = pl.DeviceIdType.MESH
F32 = jnp.float32
BF16 = jnp.bfloat16


def nt(a, b):
    return lax.dot_general(a, b, (((1,), (1,)), ((), ())), preferred_element_type=F32)


def tn(a, b):
    return lax.dot_general(a, b, (((0,), (0,)), ((), ())), preferred_element_type=F32)


def kernel(
    heads,
    q_ref, k_ref, v_ref, slot_hbm, doc_hbm, out_ref,
    slot_ref, doc_ref, qg, kvg, bias, half_o, half_stat, op, orecv, zs, zr_buf, out_buf,
    tab_sem, loc_sem, zkv_s, zkv_r, zq_s, zq_r, kv_s, kv_r, q_s, q_r, c_s, c_r, o_s, o_r, zo_s, zo_r, out_sem,
):
    outer = lax.axis_index("outer")
    inner = lax.axis_index("inner")
    z, c = outer // 2, outer % 2
    x, y = inner // NX, inner % NX
    za = z + 1 - 2 * (z % 2)
    zb = 3 - z
    dev_c = {"outer": z * 2 + 1 - c, "inner": inner}
    first_heads = (heads + 1) // 2
    groups = (0, 1)
    of = (pl.ds(0, first_heads), pl.ds(first_heads, heads - first_heads))

    def pick(g, even, odd):
        return even + g * (odd - even)

    def group_of(h):
        return h // first_heads

    def plane_q(g):
        return {"outer": pick(g, za, zb) * 2 + c, "inner": inner}

    def plane_kv(g):
        return {"outer": pick(g, zb, za) * 2 + c, "inner": inner}

    def along_x(j):
        return lax.rem(x + j, NX) * NX + y

    def along_y(j):
        return x * NX + lax.rem(y + j, NX)

    def ring_q(g, j):
        return {"outer": outer, "inner": pick(g, along_x(j), along_y(j))}

    def ring_kv(g, j):
        return {"outer": outer, "inner": pick(g, along_y(j), along_x(j))}

    def at_q(g, j=0):
        return lax.rem(pick(g, x, y) + j, NX)

    def at_kv(g, j=0):
        return lax.rem(pick(g, y, x) + j, NX)

    tables = (
        pltpu.make_async_copy(slot_hbm, slot_ref, tab_sem.at[0]),
        pltpu.make_async_copy(doc_hbm, doc_ref, tab_sem.at[1]),
    )

    def local(h):
        at = pl.ds(h * D, D)
        g = group_of(h)
        return (
            pltpu.make_async_copy(q_ref.at[:, at], qg.at[at_q(g), 0, h], loc_sem.at[2, h]),
            pltpu.make_async_copy(k_ref.at[:, at], kvg.at[0, 0, 0, at_kv(g), h], loc_sem.at[0, h]),
            pltpu.make_async_copy(v_ref.at[:, at], kvg.at[1, 0, 0, at_kv(g), h], loc_sem.at[1, h]),
        )

    for h in range(heads):
        for copy in local(h):
            copy.start()
    for copy in tables:
        copy.start()

    barrier = pltpu.get_barrier_semaphore()
    partners = [plane_q(0), plane_kv(0), dev_c]
    partners += [ring_q(0, j) for j in (1, 2, 3)] + [ring_kv(0, j) for j in (1, 2, 3)]
    for dev in partners:
        pl.semaphore_signal(barrier, inc=1, device_id=dev, device_id_type=MESH)
    pl.semaphore_wait(barrier, len(partners))

    def remote(src, dst, send, recv, dev):
        return pltpu.make_async_remote_copy(
            src_ref=src, dst_ref=dst, send_sem=send, recv_sem=recv, device_id=dev, device_id_type=MESH
        )

    def z_kv(g):
        here = at_kv(g)
        return remote(
            kvg.at[:, 0, 0, here, of[g]], kvg.at[:, 0, 1, here, of[g]], zkv_s, zkv_r.at[g], plane_kv(g)
        )

    def z_q(g):
        here = at_q(g)
        return remote(qg.at[here, 0, of[g]], qg.at[here, 1, of[g]], zq_s, zq_r.at[g], plane_q(g))

    def r_kv(g, zr, j):
        block = kvg.at[:, 0, zr, at_kv(g), of[g]]
        return remote(block, block, kv_s, kv_r.at[g, zr], ring_kv(g, j))

    def r_q(g, zr, j):
        block = qg.at[at_q(g), zr, of[g]]
        return remote(block, block, q_s, q_r.at[g], ring_q(g, j))

    def c_kv(g, zr):
        return remote(
            kvg.at[:, 0, zr, :, of[g]], kvg.at[:, 1, zr, :, of[g]], c_s, c_r.at[g, zr], dev_c
        )

    def ring_o(h, zr, j):
        g = group_of(h)
        return remote(
            op.at[zr, h, at_q(g, j)], orecv.at[zr, h, j - 1], o_s, o_r.at[zr, h], ring_q(g, j)
        )

    def z_o(h):
        return remote(zs.at[h], zr_buf.at[h], zo_s, zo_r.at[h], plane_q(group_of(h)))

    def take(ref, sem):
        pltpu.make_async_copy(ref, ref, sem).wait()

    def out_copy(h):
        return pltpu.make_async_copy(
            out_buf.at[h], out_ref.at[:, pl.ds(pl.multiple_of(h * D, D), D)], out_sem
        )

    for h in range(heads):
        for copy in local(h):
            copy.wait()
    for g in groups:
        z_q(g).start()
        z_kv(g).start()
    for j in (1, 3, 2):
        for g in groups:
            r_kv(g, 0, j).start()
            r_q(g, 0, j).start()
    for copy in tables:
        copy.wait()

    ends = [doc_ref[0]]
    for n in range(1, doc_ref.shape[0]):
        ends.append(ends[-1] + doc_ref[n])

    def doc_start(slot):
        start = jnp.int32(0)
        for end in ends:
            start = jnp.where(slot >= end, end, start)
        return start

    lane = lax.broadcasted_iota(jnp.int32, (8, NQ), 1)
    down = lax.broadcasted_iota(jnp.int32, (8, NQ), 0)
    part = lane // BLK

    def build_mask(g):
        q_pos = jnp.zeros((8, NQ), jnp.int32)
        q_low = jnp.zeros((8, NQ), jnp.int32)
        for t in range(NQ // BLK):
            zt, half, rt = t // 8, (t // 4) % 2, t % 4
            zq = z if zt == 0 else (zb if g else za)
            iq = x * NX + rt if g else rt * NX + y
            slot = slot_ref[2 * ((zq * 2 + c) * 16 + iq) + half]
            hit = part == t
            q_pos = jnp.where(hit, slot * BLK, q_pos)
            q_low = jnp.where(hit, doc_start(slot) * BLK, q_low)
        q_pos = q_pos + lane % BLK

        def mask(t, carry):
            ct, zt, rt, half = t // 16, (t // 8) % 2, (t // 2) % 4, t % 2
            zk = z + zt * ((za if g else zb) - z)
            ck = c + ct * (1 - 2 * c)
            ik = rt * NX + y if g else x * NX + rt
            slot = slot_ref[2 * ((zk * 2 + ck) * 16 + ik) + half]
            for row in range(0, BLK, 8):
                k_pos = down + (slot * BLK + row)
                seen = (k_pos <= q_pos) & (k_pos >= q_low)
                at = (zt * 2 + half) * KT + (ct * NX + rt) * BLK + row
                term = jnp.where(seen, 0.0, HIDE)
                for tile in (0, 1):
                    bias[g, tile, pl.ds(pl.multiple_of(at, 8), 8), :] = term[:, tile * QT : (tile + 1) * QT]
            return carry

        lax.fori_loop(0, NK // BLK, mask, 0)

    def swap_cores(zr):
        for g in (1, 0):
            take(kvg.at[:, 0, zr, pl.ds(0, NX - 1), of[g]], kv_r.at[g, zr])
            c_kv(g, zr).start()

    def swap_half(a):
        return pltpu.roll(a, R, axis=1)

    quarter = lax.broadcasted_iota(jnp.int32, (1, D), 1) // BLK

    def gather_lanes(pieces, n):
        moved = [pltpu.roll(p, (k - n) % 4 * BLK, axis=1) if k != n else p for k, p in enumerate(pieces)]
        return jnp.where(
            quarter < 2, jnp.where(quarter == 0, moved[0], moved[1]), jnp.where(quarter == 2, moved[2], moved[3])
        )

    def attend(units, zr):
        half = QT // 2
        scores = []
        for h, tile in units:
            low_keys = kvg[0, :, zr, :, h, 0:BLK, :].reshape(KT, D)
            high_keys = kvg[0, :, zr, :, h, BLK:R, :].reshape(KT, D)
            low_rows = qg[:, tile, h, 0:BLK, :].reshape(half, D)
            high_rows = qg[:, tile, h, BLK:R, :].reshape(half, D)
            g, first = group_of(h), zr * 2 * KT
            rows = jnp.concatenate([low_rows, high_rows], axis=0)
            wide = nt(low_keys, rows) * SCALE2 + bias[g, tile, first : first + KT, :]
            tall = nt(high_keys, high_rows) * SCALE2 + bias[g, tile, first + KT : first + 2 * KT, half:QT]
            scores.append((wide, tall))
        tops = []
        for (h, tile), (wide, tall) in zip(units, scores):
            top = jnp.max(wide, axis=0, keepdims=True)
            low_top, high_top = top[:, 0:half], jnp.maximum(top[:, half:QT], jnp.max(tall, axis=0, keepdims=True))
            top = jnp.concatenate([low_top, high_top], axis=1)
            top = jnp.maximum(top, FLOOR).astype(BF16).astype(F32)
            if zr:
                top = jnp.maximum(top, half_stat[h, tile, 0:1, :])
            tops.append(top)
        results = []
        for (h, tile), (wide, tall), top in zip(units, scores, tops):
            wide = jnp.exp2(wide - top)
            tall = jnp.exp2(tall - top[:, half:QT])
            total = jnp.sum(wide, axis=0, keepdims=True)
            total = (total[:, 0:half], total[:, half:QT] + jnp.sum(tall, axis=0, keepdims=True))
            low_values = kvg[1, :, zr, :, h, 0:BLK, :].reshape(KT, D)
            high_values = kvg[1, :, zr, :, h, BLK:R, :].reshape(KT, D)
            result = tn(low_values, wide.astype(BF16))
            high_result = result[:, half:QT] + tn(high_values, tall.astype(BF16))
            results.append((total, (result[:, 0:half], high_result)))
        row = lax.broadcasted_iota(jnp.int32, (STAT, half), 0)
        for (h, tile), top, (total, result) in zip(units, tops, results):
            sides, stats = [], []
            for side in (0, 1):
                span = slice(side * half, (side + 1) * half)
                m, l, o = top[:, span], total[side], result[side]
                if not zr:
                    half_stat[h, tile, 0:1, span] = m
                    half_stat[h, tile, 1:2, span] = l
                    half_o[h, tile, :, span] = o
                    continue
                shrink = jnp.exp2(half_stat[h, tile, 0:1, span] - m)
                l = l + half_stat[h, tile, 1:2, span] * shrink
                sides.append(o + half_o[h, tile, :, span] * shrink)
                l_hi = l.astype(BF16).astype(F32)
                stats.append(jnp.where(row == 0, m, jnp.where(row == 1, l_hi, l - l_hi)))
            if not zr:
                continue
            pieces = (sides[0][0:R], sides[1][0:R], sides[0][R:D], sides[1][R:D])
            for n in range(NX):
                op[tile, h, n, 0:R, :] = gather_lanes(pieces, n).astype(BF16)
                op[tile, h, n, R : R + STAT, :] = gather_lanes(stats * 2, n).astype(BF16)

    def unstat(block):
        stat = block.astype(F32)
        return stat[0:1], stat[1:2] + stat[2:3]

    def merge_ring(h, zr):
        take(orecv.at[zr, h], o_r.at[zr, h])
        here = at_q(group_of(h))
        parts = [(op[zr, h, here, 0:R, :], unstat(op[zr, h, here, R : R + STAT, :]))]
        for j in (1, 2, 3):
            parts.append((orecv[zr, h, j - 1, 0:R, :], unstat(orecv[zr, h, j - 1, R : R + STAT, :])))
        top = functools.reduce(jnp.maximum, [p[1][0] for p in parts])
        total = jnp.zeros((1, D), F32)
        result = jnp.zeros((R, D), F32)
        for block, (m, l) in parts:
            w = jnp.exp2(m - top)
            total = total + w * l
            result = result + block.astype(F32) * w
        return result, top, total

    def merge_far(h):
        result, top, total = merge_ring(h, 1)
        total_hi = total.astype(BF16).astype(F32)
        row = lax.broadcasted_iota(jnp.int32, (STAT, D), 0)
        zs[h, 0:R, :] = result.astype(BF16)
        zs[h, R : R + STAT, :] = jnp.where(
            row == 0, top, jnp.where(row == 1, total_hi, total - total_hi)
        ).astype(BF16)
        z_o(h).start()

    def finish(h):
        result, m_own, l_own = merge_ring(h, 0)
        z_o(h).wait_recv()
        m_far, l_far = unstat(zr_buf[h, R : R + STAT, :])
        top = jnp.maximum(m_far, m_own)
        w_far, w_own = jnp.exp2(m_far - top), jnp.exp2(m_own - top)
        total = w_far * l_far + w_own * l_own
        w_far, w_own = w_far / total, w_own / total
        packed = result * w_own + zr_buf[h, 0:R, :].astype(F32) * w_far
        tall = jnp.concatenate([packed, swap_half(packed)], axis=0)
        out_buf[h] = tall.T[0:R].astype(BF16)
        out_copy(h).start()

    build_mask(0)
    build_mask(1)
    swap_cores(0)
    for g in groups:
        z_q(g).wait_recv()
        for j in (1, 3, 2):
            r_q(g, 1, j).start()
    for g in (1, 0):
        z_kv(g).wait_recv()
        for j in (1, 3, 2):
            r_kv(g, 1, j).start()
    for g in groups:
        take(qg.at[pl.ds(0, NX - 1), :, of[g]], q_r.at[g])
        c_kv(g, 0).wait_recv()

    def early(i, carry):
        attend([(i, 1), (i, 0)], 0)
        return carry

    lax.fori_loop(0, heads, early, 0)
    swap_cores(1)
    for g in (1, 0):
        c_kv(g, 1).wait_recv()

    def head_of(unit):
        return lax.rem(unit * first_heads, heads)

    def late(i, carry):
        @pl.when(i < heads)
        def _():
            units = (2 * i, 2 * i + 1)
            works = [(head_of(unit), jnp.where(unit < heads, 1, 0)) for unit in units]
            attend(works, 1)
            for h, tile in works:
                for j in (1, 3, 2):
                    ring_o(h, tile, j).start()

        for k in (0, 1):
            unit = 2 * (i - 2) + k

            @pl.when((unit >= 0) & (unit < heads))
            def _():
                merge_far(head_of(unit))

            @pl.when(unit >= heads)
            def _():
                finish(head_of(unit))

        return carry

    lax.fori_loop(0, heads + 2, late, 0)

    take(kvg.at[:, 0, 0, 0], zkv_s)
    take(qg.at[0, 0], zq_s)
    take(kvg.at[:, 0, :, pl.ds(0, NX - 1)], kv_s)
    take(qg.at[pl.ds(0, NX - 1)], q_s)
    take(kvg.at[:, 0], c_s)
    take(orecv, o_s)
    take(zs, zo_s)
    take(out_buf, out_sem)


def per_device(queries, keys, values, slot_blocks, doc_blocks):
    width = queries.shape[1]
    heads = width // D
    dma = pltpu.SemaphoreType.DMA
    anywhere = pl.BlockSpec(memory_space=pltpu.HBM)
    return pl.pallas_call(
        functools.partial(kernel, heads),
        out_shape=jax.ShapeDtypeStruct(queries.shape, BF16),
        in_specs=[anywhere] * 5,
        out_specs=anywhere,
        scratch_shapes=[
            pltpu.SMEM(slot_blocks.shape, jnp.int32),
            pltpu.SMEM(doc_blocks.shape, jnp.int32),
            pltpu.VMEM((NX, NZ, heads, R, D), BF16),
            pltpu.VMEM((2, NC, NZ, NX, heads, R, D), BF16),
            pltpu.VMEM((2, NZ, NK, QT), F32),
            pltpu.VMEM((heads, NZ, D, QT), F32),
            pltpu.VMEM((heads, NZ, 8, QT), F32),
            pltpu.VMEM((NZ, heads, NX, R + STAT, D), BF16),
            pltpu.VMEM((NZ, heads, NX - 1, R + STAT, D), BF16),
            pltpu.VMEM((heads, R + STAT, D), BF16),
            pltpu.VMEM((heads, R + STAT, D), BF16),
            pltpu.VMEM((heads, R, D), BF16),
            dma((2,)),
            dma((3, heads)),
            dma, dma((2,)), dma, dma((2,)),
            dma, dma((2, 2)), dma, dma((2,)),
            dma, dma((2, 2)),
            dma, dma((2, heads)),
            dma, dma((heads,)), dma,
        ],
        compiler_params=pltpu.CompilerParams(
            collective_id=0, has_side_effects=True, vmem_limit_bytes=64 * 1024 * 1024
        ),
        cost_estimate=pl.CostEstimate(
            flops=4 * heads * NQ * NK * D, bytes_accessed=4 * queries.size * 2, transcendentals=heads * NQ * NK
        ),
    )(queries, keys, values, slot_blocks, doc_blocks)


def solution(mesh):
    rows = P(("outer", "inner"), "head")
    return jax.shard_map(
        per_device,
        mesh=mesh,
        in_specs=(rows, rows, rows, P(), P()),
        out_specs=rows,
        check_vma=False,
    )
```

```python
import functools
import math

import jax
import jax.numpy as jnp
from jax import lax
from jax.experimental import pallas as pl
from jax.experimental.pallas import tpu as pltpu
from jax.sharding import PartitionSpec as P

D = 128
BLK = 32
R = 64
NX = 4
NZ = 2
NC = 2
NQ = NX * NZ * R
QT = NX * R
KT = NC * NX * BLK
NK = NC * NZ * NX * R
STAT = 16
SCALE2 = D ** (-0.5) * math.log2(math.e)
HIDE = -1e30
FLOOR = -1e29
MESH = pl.DeviceIdType.MESH
F32 = jnp.float32
BF16 = jnp.bfloat16


def nt(a, b):
    return lax.dot_general(a, b, (((1,), (1,)), ((), ())), preferred_element_type=F32)


def tn(a, b):
    return lax.dot_general(a, b, (((0,), (0,)), ((), ())), preferred_element_type=F32)


def kernel(
    heads,
    q_ref, k_ref, v_ref, slot_hbm, doc_hbm, out_ref,
    slot_ref, doc_ref, qg, kvg, bias, half_o, half_stat, op, orecv, zs, zr_buf, out_buf,
    tab_sem, loc_sem, zkv_s, zkv_r, zq_s, zq_r, kv_s, kv_r, q_s, q_r, c_s, c_r, o_s, o_r, zo_s, zo_r, out_sem,
):
    outer = lax.axis_index("outer")
    inner = lax.axis_index("inner")
    z, c = outer // 2, outer % 2
    x, y = inner // NX, inner % NX
    za = z + 1 - 2 * (z % 2)
    zb = 3 - z
    dev_c = {"outer": z * 2 + 1 - c, "inner": inner}
    first_heads = (heads + 1) // 2
    groups = (0, 1)
    of = (pl.ds(0, first_heads), pl.ds(first_heads, heads - first_heads))

    def pick(g, even, odd):
        return even + g * (odd - even)

    def group_of(h):
        return h // first_heads

    def plane_q(g):
        return {"outer": pick(g, za, zb) * 2 + c, "inner": inner}

    def plane_kv(g):
        return {"outer": pick(g, zb, za) * 2 + c, "inner": inner}

    def along_x(j):
        return lax.rem(x + j, NX) * NX + y

    def along_y(j):
        return x * NX + lax.rem(y + j, NX)

    def ring_q(g, j):
        return {"outer": outer, "inner": pick(g, along_x(j), along_y(j))}

    def ring_kv(g, j):
        return {"outer": outer, "inner": pick(g, along_y(j), along_x(j))}

    def at_q(g, j=0):
        return lax.rem(pick(g, x, y) + j, NX)

    def at_kv(g, j=0):
        return lax.rem(pick(g, y, x) + j, NX)

    tables = (
        pltpu.make_async_copy(slot_hbm, slot_ref, tab_sem.at[0]),
        pltpu.make_async_copy(doc_hbm, doc_ref, tab_sem.at[1]),
    )

    def local(h):
        at = pl.ds(h * D, D)
        g = group_of(h)
        return (
            pltpu.make_async_copy(q_ref.at[:, at], qg.at[at_q(g), 0, h], loc_sem.at[2, h]),
            pltpu.make_async_copy(k_ref.at[:, at], kvg.at[0, 0, 0, at_kv(g), h], loc_sem.at[0, h]),
            pltpu.make_async_copy(v_ref.at[:, at], kvg.at[1, 0, 0, at_kv(g), h], loc_sem.at[1, h]),
        )

    for h in range(heads):
        for copy in local(h):
            copy.start()
    for copy in tables:
        copy.start()

    barrier = pltpu.get_barrier_semaphore()
    partners = [plane_q(0), plane_kv(0), dev_c]
    partners += [ring_q(0, j) for j in (1, 2, 3)] + [ring_kv(0, j) for j in (1, 2, 3)]
    for dev in partners:
        pl.semaphore_signal(barrier, inc=1, device_id=dev, device_id_type=MESH)
    pl.semaphore_wait(barrier, len(partners))

    def remote(src, dst, send, recv, dev):
        return pltpu.make_async_remote_copy(
            src_ref=src, dst_ref=dst, send_sem=send, recv_sem=recv, device_id=dev, device_id_type=MESH
        )

    def z_kv(g):
        here = at_kv(g)
        return remote(
            kvg.at[:, 0, 0, here, of[g]], kvg.at[:, 0, 1, here, of[g]], zkv_s, zkv_r.at[g], plane_kv(g)
        )

    def z_q(g):
        here = at_q(g)
        return remote(qg.at[here, 0, of[g]], qg.at[here, 1, of[g]], zq_s, zq_r.at[g], plane_q(g))

    def r_kv(g, zr, j):
        block = kvg.at[:, 0, zr, at_kv(g), of[g]]
        return remote(block, block, kv_s, kv_r.at[g, zr], ring_kv(g, j))

    def r_q(g, zr, j):
        block = qg.at[at_q(g), zr, of[g]]
        return remote(block, block, q_s, q_r.at[g], ring_q(g, j))

    def c_kv(g, zr):
        return remote(
            kvg.at[:, 0, zr, :, of[g]], kvg.at[:, 1, zr, :, of[g]], c_s, c_r.at[g, zr], dev_c
        )

    def ring_o(h, zr, j):
        g = group_of(h)
        return remote(
            op.at[zr, h, at_q(g, j)], orecv.at[zr, h, j - 1], o_s, o_r.at[zr, h], ring_q(g, j)
        )

    def z_o(h):
        return remote(zs.at[h], zr_buf.at[h], zo_s, zo_r.at[h], plane_q(group_of(h)))

    def take(ref, sem):
        pltpu.make_async_copy(ref, ref, sem).wait()

    def out_copy(h):
        return pltpu.make_async_copy(
            out_buf.at[h], out_ref.at[:, pl.ds(pl.multiple_of(h * D, D), D)], out_sem
        )

    for h in range(heads):
        for copy in local(h):
            copy.wait()
    for g in groups:
        z_q(g).start()
        z_kv(g).start()
    for j in (1, 3, 2):
        for g in groups:
            r_kv(g, 0, j).start()
            r_q(g, 0, j).start()
    for copy in tables:
        copy.wait()

    ends = [doc_ref[0]]
    for n in range(1, doc_ref.shape[0]):
        ends.append(ends[-1] + doc_ref[n])

    def doc_start(slot):
        start = jnp.int32(0)
        for end in ends:
            start = jnp.where(slot >= end, end, start)
        return start

    lane = lax.broadcasted_iota(jnp.int32, (8, NQ), 1)
    down = lax.broadcasted_iota(jnp.int32, (8, NQ), 0)
    part = lane // BLK
    diagonal = [jnp.where(down + row <= lane % BLK, 0.0, HIDE) for row in range(0, BLK, 8)]

    def build_mask(g):
        q_slot = jnp.zeros((8, NQ), jnp.int32)
        q_low = jnp.zeros((8, NQ), jnp.int32)
        for t in range(NQ // BLK):
            zt, half, rt = t // 8, (t // 4) % 2, t % 4
            zq = z if zt == 0 else (zb if g else za)
            iq = x * NX + rt if g else rt * NX + y
            slot = slot_ref[2 * ((zq * 2 + c) * 16 + iq) + half]
            hit = part == t
            q_slot = jnp.where(hit, slot, q_slot)
            q_low = jnp.where(hit, doc_start(slot), q_low)

        def mask(t, carry):
            ct, zt, half = t // 4, (t // 2) % 2, t % 2
            zk = z + zt * ((za if g else zb) - z)
            ck = c + ct * (1 - 2 * c)
            for rt in range(NX):
                ik = rt * NX + y if g else x * NX + rt
                slot = slot_ref[2 * ((zk * 2 + ck) * 16 + ik) + half]
                before = jnp.where((slot < q_slot) & (slot >= q_low), 0.0, HIDE)
                same = q_slot == slot
                for row in range(0, BLK, 8):
                    at = (zt * 2 + half) * KT + (ct * NX + rt) * BLK + row
                    term = jnp.where(same, diagonal[row // 8], before)
                    for tile in (0, 1):
                        bias[g, tile, pl.ds(pl.multiple_of(at, 8), 8), :] = term[:, tile * QT : (tile + 1) * QT]
            return carry

        lax.fori_loop(0, NC * NZ * 2, mask, 0)

    def swap_cores(zr):
        for g in (1, 0):
            take(kvg.at[:, 0, zr, pl.ds(0, NX - 1), of[g]], kv_r.at[g, zr])
            c_kv(g, zr).start()

    def swap_half(a):
        return pltpu.roll(a, R, axis=1)

    quarter = lax.broadcasted_iota(jnp.int32, (1, D), 1) // BLK

    def gather_lanes(pieces, n):
        moved = [pltpu.roll(p, (k - n) % 4 * BLK, axis=1) if k != n else p for k, p in enumerate(pieces)]
        return jnp.where(
            quarter < 2, jnp.where(quarter == 0, moved[0], moved[1]), jnp.where(quarter == 2, moved[2], moved[3])
        )

    def attend(units, zr):
        half = QT // 2
        scores = []
        for h, tile in units:
            low_keys = kvg[0, :, zr, :, h, 0:BLK, :].reshape(KT, D)
            high_keys = kvg[0, :, zr, :, h, BLK:R, :].reshape(KT, D)
            low_rows = qg[:, tile, h, 0:BLK, :].reshape(half, D)
            high_rows = qg[:, tile, h, BLK:R, :].reshape(half, D)
            g, first = group_of(h), zr * 2 * KT
            rows = jnp.concatenate([low_rows, high_rows], axis=0)
            wide = nt(low_keys, rows) * SCALE2 + bias[g, tile, first : first + KT, :]
            tall = nt(high_keys, high_rows) * SCALE2 + bias[g, tile, first + KT : first + 2 * KT, half:QT]
            scores.append((wide, tall))
        tops = []
        for (h, tile), (wide, tall) in zip(units, scores):
            top = jnp.max(wide, axis=0, keepdims=True)
            low_top, high_top = top[:, 0:half], jnp.maximum(top[:, half:QT], jnp.max(tall, axis=0, keepdims=True))
            top = jnp.concatenate([low_top, high_top], axis=1)
            top = jnp.maximum(top, FLOOR).astype(BF16).astype(F32)
            if zr:
                top = jnp.maximum(top, half_stat[h, tile, 0:1, :])
            tops.append(top)
        results = []
        for (h, tile), (wide, tall), top in zip(units, scores, tops):
            wide = jnp.exp2(wide - top)
            tall = jnp.exp2(tall - top[:, half:QT])
            total = jnp.sum(wide, axis=0, keepdims=True)
            total = (total[:, 0:half], total[:, half:QT] + jnp.sum(tall, axis=0, keepdims=True))
            low_values = kvg[1, :, zr, :, h, 0:BLK, :].reshape(KT, D)
            high_values = kvg[1, :, zr, :, h, BLK:R, :].reshape(KT, D)
            result = tn(low_values, wide.astype(BF16))
            high_result = result[:, half:QT] + tn(high_values, tall.astype(BF16))
            results.append((total, (result[:, 0:half], high_result)))
        row = lax.broadcasted_iota(jnp.int32, (STAT, half), 0)
        for (h, tile), top, (total, result) in zip(units, tops, results):
            sides, stats = [], []
            for side in (0, 1):
                span = slice(side * half, (side + 1) * half)
                m, l, o = top[:, span], total[side], result[side]
                if not zr:
                    half_stat[h, tile, 0:1, span] = m
                    half_stat[h, tile, 1:2, span] = l
                    half_o[h, tile, :, span] = o
                    continue
                shrink = jnp.exp2(half_stat[h, tile, 0:1, span] - m)
                l = l + half_stat[h, tile, 1:2, span] * shrink
                sides.append(o + half_o[h, tile, :, span] * shrink)
                l_hi = l.astype(BF16).astype(F32)
                stats.append(jnp.where(row == 0, m, jnp.where(row == 1, l_hi, l - l_hi)))
            if not zr:
                continue
            pieces = (sides[0][0:R], sides[1][0:R], sides[0][R:D], sides[1][R:D])
            for n in range(NX):
                op[tile, h, n, 0:R, :] = gather_lanes(pieces, n).astype(BF16)
                op[tile, h, n, R : R + STAT, :] = gather_lanes(stats * 2, n).astype(BF16)

    def unstat(block):
        stat = block.astype(F32)
        return stat[0:1], stat[1:2] + stat[2:3]

    def merge_ring(h, zr):
        take(orecv.at[zr, h], o_r.at[zr, h])
        here = at_q(group_of(h))
        parts = [(op[zr, h, here, 0:R, :], unstat(op[zr, h, here, R : R + STAT, :]))]
        for j in (1, 2, 3):
            parts.append((orecv[zr, h, j - 1, 0:R, :], unstat(orecv[zr, h, j - 1, R : R + STAT, :])))
        top = functools.reduce(jnp.maximum, [p[1][0] for p in parts])
        total = jnp.zeros((1, D), F32)
        result = jnp.zeros((R, D), F32)
        for block, (m, l) in parts:
            w = jnp.exp2(m - top)
            total = total + w * l
            result = result + block.astype(F32) * w
        return result, top, total

    def merge_far(h):
        result, top, total = merge_ring(h, 1)
        total_hi = total.astype(BF16).astype(F32)
        row = lax.broadcasted_iota(jnp.int32, (STAT, D), 0)
        zs[h, 0:R, :] = result.astype(BF16)
        zs[h, R : R + STAT, :] = jnp.where(
            row == 0, top, jnp.where(row == 1, total_hi, total - total_hi)
        ).astype(BF16)
        z_o(h).start()

    def finish(h):
        result, m_own, l_own = merge_ring(h, 0)
        z_o(h).wait_recv()
        m_far, l_far = unstat(zr_buf[h, R : R + STAT, :])
        top = jnp.maximum(m_far, m_own)
        w_far, w_own = jnp.exp2(m_far - top), jnp.exp2(m_own - top)
        total = w_far * l_far + w_own * l_own
        w_far, w_own = w_far / total, w_own / total
        packed = result * w_own + zr_buf[h, 0:R, :].astype(F32) * w_far
        tall = jnp.concatenate([packed, swap_half(packed)], axis=0)
        out_buf[h] = tall.T[0:R].astype(BF16)
        out_copy(h).start()

    build_mask(0)
    build_mask(1)
    swap_cores(0)
    for g in groups:
        z_q(g).wait_recv()
        for j in (1, 3, 2):
            r_q(g, 1, j).start()
    for g in (1, 0):
        z_kv(g).wait_recv()
        for j in (1, 3, 2):
            r_kv(g, 1, j).start()
    for g in groups:
        take(qg.at[pl.ds(0, NX - 1), :, of[g]], q_r.at[g])
        c_kv(g, 0).wait_recv()

    def early(i, carry):
        attend([(i, 1), (i, 0)], 0)
        return carry

    lax.fori_loop(0, heads, early, 0)
    swap_cores(1)
    for g in (1, 0):
        c_kv(g, 1).wait_recv()

    def head_of(unit):
        return lax.rem(unit * first_heads, heads)

    def late(i, carry):
        @pl.when(i < heads)
        def _():
            units = (2 * i, 2 * i + 1)
            works = [(head_of(unit), jnp.where(unit < heads, 1, 0)) for unit in units]
            attend(works, 1)
            for h, tile in works:
                for j in (1, 3, 2):
                    ring_o(h, tile, j).start()

        for k in (0, 1):
            unit = 2 * (i - 2) + k

            @pl.when((unit >= 0) & (unit < heads))
            def _():
                merge_far(head_of(unit))

            @pl.when(unit >= heads)
            def _():
                finish(head_of(unit))

        return carry

    lax.fori_loop(0, heads + 2, late, 0)

    take(kvg.at[:, 0, 0, 0], zkv_s)
    take(qg.at[0, 0], zq_s)
    take(kvg.at[:, 0, :, pl.ds(0, NX - 1)], kv_s)
    take(qg.at[pl.ds(0, NX - 1)], q_s)
    take(kvg.at[:, 0], c_s)
    take(orecv, o_s)
    take(zs, zo_s)
    take(out_buf, out_sem)


def per_device(queries, keys, values, slot_blocks, doc_blocks):
    width = queries.shape[1]
    heads = width // D
    dma = pltpu.SemaphoreType.DMA
    anywhere = pl.BlockSpec(memory_space=pltpu.HBM)
    return pl.pallas_call(
        functools.partial(kernel, heads),
        out_shape=jax.ShapeDtypeStruct(queries.shape, BF16),
        in_specs=[anywhere] * 5,
        out_specs=anywhere,
        scratch_shapes=[
            pltpu.SMEM(slot_blocks.shape, jnp.int32),
            pltpu.SMEM(doc_blocks.shape, jnp.int32),
            pltpu.VMEM((NX, NZ, heads, R, D), BF16),
            pltpu.VMEM((2, NC, NZ, NX, heads, R, D), BF16),
            pltpu.VMEM((2, NZ, NK, QT), F32),
            pltpu.VMEM((heads, NZ, D, QT), F32),
            pltpu.VMEM((heads, NZ, 8, QT), F32),
            pltpu.VMEM((NZ, heads, NX, R + STAT, D), BF16),
            pltpu.VMEM((NZ, heads, NX - 1, R + STAT, D), BF16),
            pltpu.VMEM((heads, R + STAT, D), BF16),
            pltpu.VMEM((heads, R + STAT, D), BF16),
            pltpu.VMEM((heads, R, D), BF16),
            dma((2,)),
            dma((3, heads)),
            dma, dma((2,)), dma, dma((2,)),
            dma, dma((2, 2)), dma, dma((2,)),
            dma, dma((2, 2)),
            dma, dma((2, heads)),
            dma, dma((heads,)), dma,
        ],
        compiler_params=pltpu.CompilerParams(
            collective_id=0, has_side_effects=True, vmem_limit_bytes=64 * 1024 * 1024
        ),
        cost_estimate=pl.CostEstimate(
            flops=4 * heads * NQ * NK * D, bytes_accessed=4 * queries.size * 2, transcendentals=heads * NQ * NK
        ),
    )(queries, keys, values, slot_blocks, doc_blocks)


def solution(mesh):
    rows = P(("outer", "inner"), "head")
    return jax.shard_map(
        per_device,
        mesh=mesh,
        in_specs=(rows, rows, rows, P(), P()),
        out_specs=rows,
        check_vma=False,
    )
```

```python
import functools
import math

import jax
import jax.numpy as jnp
from jax import lax
from jax.experimental import pallas as pl
from jax.experimental.pallas import tpu as pltpu
from jax.sharding import PartitionSpec as P

D = 128
BLK = 32
R = 64
NX = 4
NZ = 2
NC = 2
NQ = NX * NZ * R
QT = NX * R
KT = NC * NX * BLK
NK = NC * NZ * NX * R
STAT = 16
SCALE2 = D ** (-0.5) * math.log2(math.e)
HIDE = -1e30
FLOOR = -1e29
MESH = pl.DeviceIdType.MESH
F32 = jnp.float32
BF16 = jnp.bfloat16


def nt(a, b):
    return lax.dot_general(a, b, (((1,), (1,)), ((), ())), preferred_element_type=F32)


def tn(a, b):
    return lax.dot_general(a, b, (((0,), (0,)), ((), ())), preferred_element_type=F32)


def kernel(
    heads,
    q_ref, k_ref, v_ref, slot_hbm, doc_hbm, out_ref,
    slot_ref, doc_ref, qg, kvg, bias, half_o, half_stat, op, orecv, zs, zr_buf, out_buf,
    tab_sem, loc_sem, zkv_s, zkv_r, zq_s, zq_r, kv_s, kv_r, q_s, q_r, c_s, c_r, o_s, o_r, zo_s, zo_r, out_sem,
):
    outer = lax.axis_index("outer")
    inner = lax.axis_index("inner")
    z, c = outer // 2, outer % 2
    x, y = inner // NX, inner % NX
    za = z + 1 - 2 * (z % 2)
    zb = 3 - z
    dev_c = {"outer": z * 2 + 1 - c, "inner": inner}
    first_heads = (heads + 1) // 2
    groups = (0, 1)
    of = (pl.ds(0, first_heads), pl.ds(first_heads, heads - first_heads))

    def pick(g, even, odd):
        return even + g * (odd - even)

    def group_of(h):
        return h // first_heads

    def plane_q(g):
        return {"outer": pick(g, za, zb) * 2 + c, "inner": inner}

    def plane_kv(g):
        return {"outer": pick(g, zb, za) * 2 + c, "inner": inner}

    def along_x(j):
        return lax.rem(x + j, NX) * NX + y

    def along_y(j):
        return x * NX + lax.rem(y + j, NX)

    def ring_q(g, j):
        return {"outer": outer, "inner": pick(g, along_x(j), along_y(j))}

    def ring_kv(g, j):
        return {"outer": outer, "inner": pick(g, along_y(j), along_x(j))}

    def at_q(g, j=0):
        return lax.rem(pick(g, x, y) + j, NX)

    def at_kv(g, j=0):
        return lax.rem(pick(g, y, x) + j, NX)

    tables = (
        pltpu.make_async_copy(slot_hbm, slot_ref, tab_sem.at[0]),
        pltpu.make_async_copy(doc_hbm, doc_ref, tab_sem.at[1]),
    )

    def local(h):
        at = pl.ds(h * D, D)
        g = group_of(h)
        return (
            pltpu.make_async_copy(q_ref.at[:, at], qg.at[at_q(g), 0, h], loc_sem.at[2, h]),
            pltpu.make_async_copy(k_ref.at[:, at], kvg.at[0, 0, 0, at_kv(g), h], loc_sem.at[0, h]),
            pltpu.make_async_copy(v_ref.at[:, at], kvg.at[1, 0, 0, at_kv(g), h], loc_sem.at[1, h]),
        )

    for h in range(heads):
        for copy in local(h):
            copy.start()
    for copy in tables:
        copy.start()

    barrier = pltpu.get_barrier_semaphore()
    partners = [plane_q(0), plane_kv(0), dev_c]
    partners += [ring_q(0, j) for j in (1, 2, 3)] + [ring_kv(0, j) for j in (1, 2, 3)]
    for dev in partners:
        pl.semaphore_signal(barrier, inc=1, device_id=dev, device_id_type=MESH)
    pl.semaphore_wait(barrier, len(partners))

    def remote(src, dst, send, recv, dev):
        return pltpu.make_async_remote_copy(
            src_ref=src, dst_ref=dst, send_sem=send, recv_sem=recv, device_id=dev, device_id_type=MESH
        )

    def z_kv(g):
        here = at_kv(g)
        return remote(
            kvg.at[:, 0, 0, here, of[g]], kvg.at[:, 0, 1, here, of[g]], zkv_s.at[g], zkv_r.at[g], plane_kv(g)
        )

    def z_q(g):
        here = at_q(g)
        return remote(qg.at[here, 0, of[g]], qg.at[here, 1, of[g]], zq_s, zq_r.at[g], plane_q(g))

    def r_kv(g, zr, j):
        block = kvg.at[:, 0, zr, at_kv(g), of[g]]
        return remote(block, block, kv_s, kv_r.at[g, zr], ring_kv(g, j))

    def r_q(g, zr, j):
        block = qg.at[at_q(g), zr, of[g]]
        return remote(block, block, q_s, q_r.at[g, zr], ring_q(g, j))

    def c_kv(g, zr):
        return remote(
            kvg.at[:, 0, zr, :, of[g]], kvg.at[:, 1, zr, :, of[g]], c_s, c_r.at[g, zr], dev_c
        )

    def ring_o(h, zr, j):
        g = group_of(h)
        return remote(
            op.at[zr, h, at_q(g, j)], orecv.at[zr, h, j - 1], o_s, o_r.at[zr, h], ring_q(g, j)
        )

    def z_o(h):
        return remote(zs.at[h], zr_buf.at[h], zo_s, zo_r.at[h], plane_q(group_of(h)))

    def take(ref, sem):
        pltpu.make_async_copy(ref, ref, sem).wait()

    def out_copy(h):
        return pltpu.make_async_copy(
            out_buf.at[h], out_ref.at[:, pl.ds(pl.multiple_of(h * D, D), D)], out_sem
        )

    for h in range(heads):
        for copy in local(h):
            copy.wait()
    for g in groups:
        z_kv(g).start()
    for j in (1, 3, 2):
        for g in groups:
            r_kv(g, 0, j).start()
    for j in (1, 3, 2):
        for g in groups:
            r_q(g, 0, j).start()
    for copy in tables:
        copy.wait()

    ends = [doc_ref[0]]
    for n in range(1, doc_ref.shape[0]):
        ends.append(ends[-1] + doc_ref[n])

    def doc_start(slot):
        start = jnp.int32(0)
        for end in ends:
            start = jnp.where(slot >= end, end, start)
        return start

    lane = lax.broadcasted_iota(jnp.int32, (8, NQ), 1)
    down = lax.broadcasted_iota(jnp.int32, (8, NQ), 0)
    part = lane // BLK
    diagonal = [jnp.where(down + row <= lane % BLK, 0.0, HIDE) for row in range(0, BLK, 8)]

    def build_mask(g):
        q_slot = jnp.zeros((8, NQ), jnp.int32)
        q_low = jnp.zeros((8, NQ), jnp.int32)
        for t in range(NQ // BLK):
            zt, half, rt = t // 8, (t // 4) % 2, t % 4
            zq = z if zt == 0 else (zb if g else za)
            iq = x * NX + rt if g else rt * NX + y
            slot = slot_ref[2 * ((zq * 2 + c) * 16 + iq) + half]
            hit = part == t
            q_slot = jnp.where(hit, slot, q_slot)
            q_low = jnp.where(hit, doc_start(slot), q_low)

        def mask(t, carry):
            ct, zt, half = t // 4, (t // 2) % 2, t % 2
            zk = z + zt * ((za if g else zb) - z)
            ck = c + ct * (1 - 2 * c)
            for rt in range(NX):
                ik = rt * NX + y if g else x * NX + rt
                slot = slot_ref[2 * ((zk * 2 + ck) * 16 + ik) + half]
                before = jnp.where((slot < q_slot) & (slot >= q_low), 0.0, HIDE)
                same = q_slot == slot
                for row in range(0, BLK, 8):
                    at = (zt * 2 + half) * KT + (ct * NX + rt) * BLK + row
                    term = jnp.where(same, diagonal[row // 8], before)
                    for tile in (0, 1):
                        bias[g, tile, pl.ds(pl.multiple_of(at, 8), 8), :] = term[:, tile * QT : (tile + 1) * QT]
            return carry

        lax.fori_loop(0, NC * NZ * 2, mask, 0)

    def swap_cores(zr):
        for g in (1, 0):
            take(kvg.at[:, 0, zr, pl.ds(0, NX - 1), of[g]], kv_r.at[g, zr])
            c_kv(g, zr).start()

    def swap_half(a):
        return pltpu.roll(a, R, axis=1)

    quarter = lax.broadcasted_iota(jnp.int32, (1, D), 1) // BLK

    def gather_lanes(pieces, n):
        moved = [pltpu.roll(p, (k - n) % 4 * BLK, axis=1) if k != n else p for k, p in enumerate(pieces)]
        return jnp.where(
            quarter < 2, jnp.where(quarter == 0, moved[0], moved[1]), jnp.where(quarter == 2, moved[2], moved[3])
        )

    def attend(units, zr):
        half = QT // 2
        scores = []
        for h, tile in units:
            low_keys = kvg[0, :, zr, :, h, 0:BLK, :].reshape(KT, D)
            high_keys = kvg[0, :, zr, :, h, BLK:R, :].reshape(KT, D)
            low_rows = qg[:, tile, h, 0:BLK, :].reshape(half, D)
            high_rows = qg[:, tile, h, BLK:R, :].reshape(half, D)
            g, first = group_of(h), zr * 2 * KT
            rows = jnp.concatenate([low_rows, high_rows], axis=0)
            wide = nt(low_keys, rows) * SCALE2 + bias[g, tile, first : first + KT, :]
            tall = nt(high_keys, high_rows) * SCALE2 + bias[g, tile, first + KT : first + 2 * KT, half:QT]
            scores.append((wide, tall))
        tops = []
        for (h, tile), (wide, tall) in zip(units, scores):
            top = jnp.max(wide, axis=0, keepdims=True)
            low_top, high_top = top[:, 0:half], jnp.maximum(top[:, half:QT], jnp.max(tall, axis=0, keepdims=True))
            top = jnp.concatenate([low_top, high_top], axis=1)
            top = jnp.maximum(top, FLOOR).astype(BF16).astype(F32)
            if zr:
                top = jnp.maximum(top, half_stat[h, tile, 0:1, :])
            tops.append(top)
        results = []
        for (h, tile), (wide, tall), top in zip(units, scores, tops):
            wide = jnp.exp2(wide - top)
            tall = jnp.exp2(tall - top[:, half:QT])
            total = jnp.sum(wide, axis=0, keepdims=True)
            total = (total[:, 0:half], total[:, half:QT] + jnp.sum(tall, axis=0, keepdims=True))
            low_values = kvg[1, :, zr, :, h, 0:BLK, :].reshape(KT, D)
            high_values = kvg[1, :, zr, :, h, BLK:R, :].reshape(KT, D)
            result = tn(low_values, wide.astype(BF16))
            high_result = result[:, half:QT] + tn(high_values, tall.astype(BF16))
            results.append((total, (result[:, 0:half], high_result)))
        row = lax.broadcasted_iota(jnp.int32, (STAT, half), 0)
        for (h, tile), top, (total, result) in zip(units, tops, results):
            sides, stats = [], []
            for side in (0, 1):
                span = slice(side * half, (side + 1) * half)
                m, l, o = top[:, span], total[side], result[side]
                if not zr:
                    half_stat[h, tile, 0:1, span] = m
                    half_stat[h, tile, 1:2, span] = l
                    half_o[h, tile, :, span] = o
                    continue
                shrink = jnp.exp2(half_stat[h, tile, 0:1, span] - m)
                l = l + half_stat[h, tile, 1:2, span] * shrink
                sides.append(o + half_o[h, tile, :, span] * shrink)
                l_hi = l.astype(BF16).astype(F32)
                stats.append(jnp.where(row == 0, m, jnp.where(row == 1, l_hi, l - l_hi)))
            if not zr:
                continue
            pieces = (sides[0][0:R], sides[1][0:R], sides[0][R:D], sides[1][R:D])
            for n in range(NX):
                op[tile, h, n, 0:R, :] = gather_lanes(pieces, n).astype(BF16)
                op[tile, h, n, R : R + STAT, :] = gather_lanes(stats * 2, n).astype(BF16)

    def unstat(block):
        stat = block.astype(F32)
        return stat[0:1], stat[1:2] + stat[2:3]

    def merge_ring(h, zr):
        take(orecv.at[zr, h], o_r.at[zr, h])
        here = at_q(group_of(h))
        parts = [(op[zr, h, here, 0:R, :], unstat(op[zr, h, here, R : R + STAT, :]))]
        for j in (1, 2, 3):
            parts.append((orecv[zr, h, j - 1, 0:R, :], unstat(orecv[zr, h, j - 1, R : R + STAT, :])))
        top = functools.reduce(jnp.maximum, [p[1][0] for p in parts])
        total = jnp.zeros((1, D), F32)
        result = jnp.zeros((R, D), F32)
        for block, (m, l) in parts:
            w = jnp.exp2(m - top)
            total = total + w * l
            result = result + block.astype(F32) * w
        return result, top, total

    def merge_far(h):
        result, top, total = merge_ring(h, 1)
        total_hi = total.astype(BF16).astype(F32)
        row = lax.broadcasted_iota(jnp.int32, (STAT, D), 0)
        zs[h, 0:R, :] = result.astype(BF16)
        zs[h, R : R + STAT, :] = jnp.where(
            row == 0, top, jnp.where(row == 1, total_hi, total - total_hi)
        ).astype(BF16)
        z_o(h).start()

    def finish(h):
        result, m_own, l_own = merge_ring(h, 0)
        z_o(h).wait_recv()
        m_far, l_far = unstat(zr_buf[h, R : R + STAT, :])
        top = jnp.maximum(m_far, m_own)
        w_far, w_own = jnp.exp2(m_far - top), jnp.exp2(m_own - top)
        total = w_far * l_far + w_own * l_own
        w_far, w_own = w_far / total, w_own / total
        packed = result * w_own + zr_buf[h, 0:R, :].astype(F32) * w_far
        tall = jnp.concatenate([packed, swap_half(packed)], axis=0)
        out_buf[h] = tall.T[0:R].astype(BF16)
        out_copy(h).start()

    build_mask(0)
    build_mask(1)
    swap_cores(0)
    for g in groups:
        z_kv(g).wait_send()
        z_q(g).start()
    for g in groups:
        z_kv(g).wait_recv()
        for j in (1, 3, 2):
            r_kv(g, 1, j).start()

    def early(tile):
        for g in groups:
            take(qg.at[pl.ds(0, NX - 1), tile, of[g]], q_r.at[g, tile])
        for h in range(0, heads, 2):
            attend([(n, tile) for n in range(h, min(h + 2, heads))], 0)

    for g in groups:
        c_kv(g, 0).wait_recv()
    early(0)
    for g in groups:
        z_q(g).wait_recv()
        for j in (1, 3, 2):
            r_q(g, 1, j).start()
    early(1)
    swap_cores(1)
    for g in (1, 0):
        c_kv(g, 1).wait_recv()

    def head_of(unit):
        return lax.rem(unit * first_heads, heads)

    def late(i, carry):
        @pl.when(i < heads)
        def _():
            units = (2 * i, 2 * i + 1)
            works = [(head_of(unit), jnp.where(unit < heads, 1, 0)) for unit in units]
            attend(works, 1)
            for h, tile in works:
                for j in (1, 3, 2):
                    ring_o(h, tile, j).start()

        for k in (0, 1):
            unit = 2 * (i - 2) + k

            @pl.when((unit >= 0) & (unit < heads))
            def _():
                merge_far(head_of(unit))

            @pl.when(unit >= heads)
            def _():
                finish(head_of(unit))

        return carry

    lax.fori_loop(0, heads + 2, late, 0)

    take(qg.at[0, 0], zq_s)
    take(kvg.at[:, 0, :, pl.ds(0, NX - 1)], kv_s)
    take(qg.at[pl.ds(0, NX - 1)], q_s)
    take(kvg.at[:, 0], c_s)
    take(orecv, o_s)
    take(zs, zo_s)
    take(out_buf, out_sem)


def per_device(queries, keys, values, slot_blocks, doc_blocks):
    width = queries.shape[1]
    heads = width // D
    dma = pltpu.SemaphoreType.DMA
    anywhere = pl.BlockSpec(memory_space=pltpu.HBM)
    return pl.pallas_call(
        functools.partial(kernel, heads),
        out_shape=jax.ShapeDtypeStruct(queries.shape, BF16),
        in_specs=[anywhere] * 5,
        out_specs=anywhere,
        scratch_shapes=[
            pltpu.SMEM(slot_blocks.shape, jnp.int32),
            pltpu.SMEM(doc_blocks.shape, jnp.int32),
            pltpu.VMEM((NX, NZ, heads, R, D), BF16),
            pltpu.VMEM((2, NC, NZ, NX, heads, R, D), BF16),
            pltpu.VMEM((2, NZ, NK, QT), F32),
            pltpu.VMEM((heads, NZ, D, QT), F32),
            pltpu.VMEM((heads, NZ, 8, QT), F32),
            pltpu.VMEM((NZ, heads, NX, R + STAT, D), BF16),
            pltpu.VMEM((NZ, heads, NX - 1, R + STAT, D), BF16),
            pltpu.VMEM((heads, R + STAT, D), BF16),
            pltpu.VMEM((heads, R + STAT, D), BF16),
            pltpu.VMEM((heads, R, D), BF16),
            dma((2,)),
            dma((3, heads)),
            dma((2,)), dma((2,)), dma, dma((2,)),
            dma, dma((2, 2)), dma, dma((2, 2)),
            dma, dma((2, 2)),
            dma, dma((2, heads)),
            dma, dma((heads,)), dma,
        ],
        compiler_params=pltpu.CompilerParams(
            collective_id=0, has_side_effects=True, vmem_limit_bytes=64 * 1024 * 1024
        ),
        cost_estimate=pl.CostEstimate(
            flops=4 * heads * NQ * NK * D, bytes_accessed=4 * queries.size * 2, transcendentals=heads * NQ * NK
        ),
    )(queries, keys, values, slot_blocks, doc_blocks)


def solution(mesh):
    rows = P(("outer", "inner"), "head")
    return jax.shard_map(
        per_device,
        mesh=mesh,
        in_specs=(rows, rows, rows, P(), P()),
        out_specs=rows,
        check_vma=False,
    )
```

```python
import functools
import math

import jax
import jax.numpy as jnp
from jax import lax
from jax.experimental import pallas as pl
from jax.experimental.pallas import tpu as pltpu
from jax.sharding import PartitionSpec as P

D = 128
BLK = 32
R = 64
NX = 4
NZ = 2
NC = 2
NQ = NX * NZ * R
QT = NX * R
KT = NC * NX * BLK
NK = NC * NZ * NX * R
STAT = 16
SCALE2 = D ** (-0.5) * math.log2(math.e)
HIDE = -1e30
FLOOR = -1e29
MESH = pl.DeviceIdType.MESH
F32 = jnp.float32
BF16 = jnp.bfloat16


def nt(a, b):
    return lax.dot_general(a, b, (((1,), (1,)), ((), ())), preferred_element_type=F32)


def tn(a, b):
    return lax.dot_general(a, b, (((0,), (0,)), ((), ())), preferred_element_type=F32)


def kernel(
    heads,
    q_ref, k_ref, v_ref, slot_hbm, doc_hbm, out_ref,
    slot_ref, doc_ref, qg, kvg, bias, half_o, half_stat, op, orecv, zs, zr_buf, out_buf,
    tab_sem, loc_sem, zkv_s, zkv_r, zq_s, zq_r, kv_s, kv_r, q_s, q_r, c_s, c_r, o_s, o_r, zo_s, zo_r, out_sem,
):
    outer = lax.axis_index("outer")
    inner = lax.axis_index("inner")
    z, c = outer // 2, outer % 2
    x, y = inner // NX, inner % NX
    za = z + 1 - 2 * (z % 2)
    zb = 3 - z
    dev_c = {"outer": z * 2 + 1 - c, "inner": inner}
    first_heads = (heads + 1) // 2
    groups = (0, 1)
    of = (pl.ds(0, first_heads), pl.ds(first_heads, heads - first_heads))

    pieces = ((0, first_heads - 1, 1), (0, 0, first_heads - 1), (1, first_heads, heads - first_heads))

    def pick(g, even, odd):
        return even + g * (odd - even)

    def group_of(h):
        return h // first_heads

    def plane_q(g):
        return {"outer": pick(g, za, zb) * 2 + c, "inner": inner}

    def plane_kv(g):
        return {"outer": pick(g, zb, za) * 2 + c, "inner": inner}

    def along_x(j):
        return lax.rem(x + j, NX) * NX + y

    def along_y(j):
        return x * NX + lax.rem(y + j, NX)

    def ring_q(g, j):
        return {"outer": outer, "inner": pick(g, along_x(j), along_y(j))}

    def ring_kv(g, j):
        return {"outer": outer, "inner": pick(g, along_y(j), along_x(j))}

    def at_q(g, j=0):
        return lax.rem(pick(g, x, y) + j, NX)

    def at_kv(g, j=0):
        return lax.rem(pick(g, y, x) + j, NX)

    tables = (
        pltpu.make_async_copy(slot_hbm, slot_ref, tab_sem.at[0]),
        pltpu.make_async_copy(doc_hbm, doc_ref, tab_sem.at[1]),
    )

    def local(h):
        at = pl.ds(h * D, D)
        g = group_of(h)
        return (
            pltpu.make_async_copy(q_ref.at[:, at], qg.at[at_q(g), 0, h], loc_sem.at[2, h]),
            pltpu.make_async_copy(k_ref.at[:, at], kvg.at[0, 0, 0, at_kv(g), h], loc_sem.at[0, h]),
            pltpu.make_async_copy(v_ref.at[:, at], kvg.at[1, 0, 0, at_kv(g), h], loc_sem.at[1, h]),
        )

    for h in range(heads):
        for copy in local(h):
            copy.start()
    for copy in tables:
        copy.start()

    barrier = pltpu.get_barrier_semaphore()
    partners = [plane_q(0), plane_kv(0), dev_c]
    partners += [ring_q(0, j) for j in (1, 2, 3)] + [ring_kv(0, j) for j in (1, 2, 3)]
    for dev in partners:
        pl.semaphore_signal(barrier, inc=1, device_id=dev, device_id_type=MESH)
    pl.semaphore_wait(barrier, len(partners))

    def remote(src, dst, send, recv, dev):
        return pltpu.make_async_remote_copy(
            src_ref=src, dst_ref=dst, send_sem=send, recv_sem=recv, device_id=dev, device_id_type=MESH
        )

    def z_kv(p):
        g, first, count = pieces[p]
        at = pl.ds(first, count)
        here = at_kv(g)
        return remote(kvg.at[:, 0, 0, here, at], kvg.at[:, 0, 1, here, at], zkv_s.at[p], zkv_r.at[p], plane_kv(g))

    def z_q(g):
        here = at_q(g)
        return remote(qg.at[here, 0, of[g]], qg.at[here, 1, of[g]], zq_s, zq_r.at[g], plane_q(g))

    def r_kv(p, zr, j):
        g, first, count = pieces[p]
        block = kvg.at[:, 0, zr, at_kv(g), pl.ds(first, count)]
        return remote(block, block, kv_s, kv_r.at[p, zr], ring_kv(g, j))

    def r_q(g, zr, j):
        block = qg.at[at_q(g), zr, of[g]]
        return remote(block, block, q_s, q_r.at[g, zr], ring_q(g, j))

    def c_kv(p, zr):
        g, first, count = pieces[p]
        at = pl.ds(first, count)
        return remote(kvg.at[:, 0, zr, :, at], kvg.at[:, 1, zr, :, at], c_s, c_r.at[p, zr], dev_c)

    def ring_o(h, zr, j):
        g = group_of(h)
        return remote(
            op.at[zr, h, at_q(g, j)], orecv.at[zr, h, j - 1], o_s, o_r.at[zr, h], ring_q(g, j)
        )

    def z_o(h):
        return remote(zs.at[h], zr_buf.at[h], zo_s, zo_r.at[h], plane_q(group_of(h)))

    def take(ref, sem):
        pltpu.make_async_copy(ref, ref, sem).wait()

    def out_copy(h):
        return pltpu.make_async_copy(
            out_buf.at[h], out_ref.at[:, pl.ds(pl.multiple_of(h * D, D), D)], out_sem
        )

    for h in range(heads):
        for copy in local(h):
            copy.wait()
    for p in (0, 2, 1):
        z_kv(p).start()
    for p in (0, 2, 1):
        for j in (1, 3, 2):
            r_kv(p, 0, j).start()
    for j in (1, 3, 2):
        for g in groups:
            r_q(g, 0, j).start()
    for copy in tables:
        copy.wait()

    ends = [doc_ref[0]]
    for n in range(1, doc_ref.shape[0]):
        ends.append(ends[-1] + doc_ref[n])

    def doc_start(slot):
        start = jnp.int32(0)
        for end in ends:
            start = jnp.where(slot >= end, end, start)
        return start

    lane = lax.broadcasted_iota(jnp.int32, (8, NQ), 1)
    down = lax.broadcasted_iota(jnp.int32, (8, NQ), 0)
    part = lane // BLK
    diagonal = [jnp.where(down + row <= lane % BLK, 0.0, HIDE) for row in range(0, BLK, 8)]

    def build_mask(g):
        q_slot = jnp.zeros((8, NQ), jnp.int32)
        q_low = jnp.zeros((8, NQ), jnp.int32)
        for t in range(NQ // BLK):
            zt, half, rt = t // 8, (t // 4) % 2, t % 4
            zq = z if zt == 0 else (zb if g else za)
            iq = x * NX + rt if g else rt * NX + y
            slot = slot_ref[2 * ((zq * 2 + c) * 16 + iq) + half]
            hit = part == t
            q_slot = jnp.where(hit, slot, q_slot)
            q_low = jnp.where(hit, doc_start(slot), q_low)

        def mask(t, carry):
            ct, zt, half = t // 4, (t // 2) % 2, t % 2
            zk = z + zt * ((za if g else zb) - z)
            ck = c + ct * (1 - 2 * c)
            for rt in range(NX):
                ik = rt * NX + y if g else x * NX + rt
                slot = slot_ref[2 * ((zk * 2 + ck) * 16 + ik) + half]
                before = jnp.where((slot < q_slot) & (slot >= q_low), 0.0, HIDE)
                same = q_slot == slot
                for row in range(0, BLK, 8):
                    at = (zt * 2 + half) * KT + (ct * NX + rt) * BLK + row
                    term = jnp.where(same, diagonal[row // 8], before)
                    for tile in (0, 1):
                        bias[g, tile, pl.ds(pl.multiple_of(at, 8), 8), :] = term[:, tile * QT : (tile + 1) * QT]
            return carry

        lax.fori_loop(0, NC * NZ * 2, mask, 0)

    def swap_cores(zr):
        for p in (0, 2, 1):
            g, first, count = pieces[p]
            take(kvg.at[:, 0, zr, pl.ds(0, NX - 1), pl.ds(first, count)], kv_r.at[p, zr])
            c_kv(p, zr).start()

    def spread_kv(p):
        z_kv(p).wait_recv()
        for j in (1, 3, 2):
            r_kv(p, 1, j).start()

    def swap_half(a):
        return pltpu.roll(a, R, axis=1)

    quarter = lax.broadcasted_iota(jnp.int32, (1, D), 1) // BLK

    def gather_lanes(pieces, n):
        moved = [pltpu.roll(p, (k - n) % 4 * BLK, axis=1) if k != n else p for k, p in enumerate(pieces)]
        return jnp.where(
            quarter < 2, jnp.where(quarter == 0, moved[0], moved[1]), jnp.where(quarter == 2, moved[2], moved[3])
        )

    def attend(units, zr):
        half = QT // 2
        scores = []
        for h, tile in units:
            low_keys = kvg[0, :, zr, :, h, 0:BLK, :].reshape(KT, D)
            high_keys = kvg[0, :, zr, :, h, BLK:R, :].reshape(KT, D)
            low_rows = qg[:, tile, h, 0:BLK, :].reshape(half, D)
            high_rows = qg[:, tile, h, BLK:R, :].reshape(half, D)
            g, first = group_of(h), zr * 2 * KT
            rows = jnp.concatenate([low_rows, high_rows], axis=0)
            wide = nt(low_keys, rows) * SCALE2 + bias[g, tile, first : first + KT, :]
            tall = nt(high_keys, high_rows) * SCALE2 + bias[g, tile, first + KT : first + 2 * KT, half:QT]
            scores.append((wide, tall))
        tops = []
        for (h, tile), (wide, tall) in zip(units, scores):
            top = jnp.max(wide, axis=0, keepdims=True)
            low_top, high_top = top[:, 0:half], jnp.maximum(top[:, half:QT], jnp.max(tall, axis=0, keepdims=True))
            top = jnp.concatenate([low_top, high_top], axis=1)
            top = jnp.maximum(top, FLOOR).astype(BF16).astype(F32)
            if zr:
                top = jnp.maximum(top, half_stat[h, tile, 0:1, :])
            tops.append(top)
        results = []
        for (h, tile), (wide, tall), top in zip(units, scores, tops):
            wide = jnp.exp2(wide - top)
            tall = jnp.exp2(tall - top[:, half:QT])
            total = jnp.sum(wide, axis=0, keepdims=True)
            total = (total[:, 0:half], total[:, half:QT] + jnp.sum(tall, axis=0, keepdims=True))
            low_values = kvg[1, :, zr, :, h, 0:BLK, :].reshape(KT, D)
            high_values = kvg[1, :, zr, :, h, BLK:R, :].reshape(KT, D)
            result = tn(low_values, wide.astype(BF16))
            high_result = result[:, half:QT] + tn(high_values, tall.astype(BF16))
            results.append((total, (result[:, 0:half], high_result)))
        row = lax.broadcasted_iota(jnp.int32, (STAT, half), 0)
        for (h, tile), top, (total, result) in zip(units, tops, results):
            sides, stats = [], []
            for side in (0, 1):
                span = slice(side * half, (side + 1) * half)
                m, l, o = top[:, span], total[side], result[side]
                if not zr:
                    half_stat[h, tile, 0:1, span] = m
                    half_stat[h, tile, 1:2, span] = l
                    half_o[h, tile, :, span] = o
                    continue
                shrink = jnp.exp2(half_stat[h, tile, 0:1, span] - m)
                l = l + half_stat[h, tile, 1:2, span] * shrink
                sides.append(o + half_o[h, tile, :, span] * shrink)
                l_hi = l.astype(BF16).astype(F32)
                stats.append(jnp.where(row == 0, m, jnp.where(row == 1, l_hi, l - l_hi)))
            if not zr:
                continue
            pieces = (sides[0][0:R], sides[1][0:R], sides[0][R:D], sides[1][R:D])
            for n in range(NX):
                op[tile, h, n, 0:R, :] = gather_lanes(pieces, n).astype(BF16)
                op[tile, h, n, R : R + STAT, :] = gather_lanes(stats * 2, n).astype(BF16)

    def unstat(block):
        stat = block.astype(F32)
        return stat[0:1], stat[1:2] + stat[2:3]

    def merge_ring(h, zr):
        take(orecv.at[zr, h], o_r.at[zr, h])
        here = at_q(group_of(h))
        parts = [(op[zr, h, here, 0:R, :], unstat(op[zr, h, here, R : R + STAT, :]))]
        for j in (1, 2, 3):
            parts.append((orecv[zr, h, j - 1, 0:R, :], unstat(orecv[zr, h, j - 1, R : R + STAT, :])))
        top = functools.reduce(jnp.maximum, [p[1][0] for p in parts])
        total = jnp.zeros((1, D), F32)
        result = jnp.zeros((R, D), F32)
        for block, (m, l) in parts:
            w = jnp.exp2(m - top)
            total = total + w * l
            result = result + block.astype(F32) * w
        return result, top, total

    def merge_far(h):
        result, top, total = merge_ring(h, 1)
        total_hi = total.astype(BF16).astype(F32)
        row = lax.broadcasted_iota(jnp.int32, (STAT, D), 0)
        zs[h, 0:R, :] = result.astype(BF16)
        zs[h, R : R + STAT, :] = jnp.where(
            row == 0, top, jnp.where(row == 1, total_hi, total - total_hi)
        ).astype(BF16)
        z_o(h).start()

    def finish(h):
        result, m_own, l_own = merge_ring(h, 0)
        z_o(h).wait_recv()
        m_far, l_far = unstat(zr_buf[h, R : R + STAT, :])
        top = jnp.maximum(m_far, m_own)
        w_far, w_own = jnp.exp2(m_far - top), jnp.exp2(m_own - top)
        total = w_far * l_far + w_own * l_own
        w_far, w_own = w_far / total, w_own / total
        packed = result * w_own + zr_buf[h, 0:R, :].astype(F32) * w_far
        tall = jnp.concatenate([packed, swap_half(packed)], axis=0)
        out_buf[h] = tall.T[0:R].astype(BF16)
        out_copy(h).start()

    build_mask(0)
    build_mask(1)
    swap_cores(0)
    z_kv(2).wait_send()
    z_q(0).start()
    spread_kv(0)
    spread_kv(2)
    for p in (0, 1):
        z_kv(p).wait_send()
    z_q(1).start()
    spread_kv(1)

    def early(tile):
        for g in groups:
            take(qg.at[pl.ds(0, NX - 1), tile, of[g]], q_r.at[g, tile])
        for h in range(0, heads, 2):
            attend([(n, tile) for n in range(h, min(h + 2, heads))], 0)

    for p in (0, 1, 2):
        c_kv(p, 0).wait_recv()
    early(0)
    for g in groups:
        z_q(g).wait_recv()
        for j in (1, 3, 2):
            r_q(g, 1, j).start()
    early(1)
    swap_cores(1)
    for p in (0, 2):
        c_kv(p, 1).wait_recv()

    def head_of(unit):
        return lax.rem(unit + first_heads - 1, heads)

    def late(i, carry):
        @pl.when(i == 1)
        def _():
            c_kv(1, 1).wait_recv()

        @pl.when(i < heads)
        def _():
            units = (2 * i, 2 * i + 1)
            works = [(head_of(unit), jnp.where(unit < heads, 1, 0)) for unit in units]
            attend(works, 1)
            for h, tile in works:
                for j in (1, 3, 2):
                    ring_o(h, tile, j).start()

        for k in (0, 1):
            unit = 2 * (i - 2) + k

            @pl.when((unit >= 0) & (unit < heads))
            def _():
                merge_far(head_of(unit))

            @pl.when(unit >= heads)
            def _():
                finish(head_of(unit))

        return carry

    lax.fori_loop(0, heads + 2, late, 0)

    take(qg.at[0, 0], zq_s)
    take(kvg.at[:, 0, :, pl.ds(0, NX - 1)], kv_s)
    take(qg.at[pl.ds(0, NX - 1)], q_s)
    take(kvg.at[:, 0], c_s)
    take(orecv, o_s)
    take(zs, zo_s)
    take(out_buf, out_sem)


def per_device(queries, keys, values, slot_blocks, doc_blocks):
    width = queries.shape[1]
    heads = width // D
    dma = pltpu.SemaphoreType.DMA
    anywhere = pl.BlockSpec(memory_space=pltpu.HBM)
    return pl.pallas_call(
        functools.partial(kernel, heads),
        out_shape=jax.ShapeDtypeStruct(queries.shape, BF16),
        in_specs=[anywhere] * 5,
        out_specs=anywhere,
        scratch_shapes=[
            pltpu.SMEM(slot_blocks.shape, jnp.int32),
            pltpu.SMEM(doc_blocks.shape, jnp.int32),
            pltpu.VMEM((NX, NZ, heads, R, D), BF16),
            pltpu.VMEM((2, NC, NZ, NX, heads, R, D), BF16),
            pltpu.VMEM((2, NZ, NK, QT), F32),
            pltpu.VMEM((heads, NZ, D, QT), F32),
            pltpu.VMEM((heads, NZ, 8, QT), F32),
            pltpu.VMEM((NZ, heads, NX, R + STAT, D), BF16),
            pltpu.VMEM((NZ, heads, NX - 1, R + STAT, D), BF16),
            pltpu.VMEM((heads, R + STAT, D), BF16),
            pltpu.VMEM((heads, R + STAT, D), BF16),
            pltpu.VMEM((heads, R, D), BF16),
            dma((2,)),
            dma((3, heads)),
            dma((3,)), dma((3,)), dma, dma((2,)),
            dma, dma((3, 2)), dma, dma((2, 2)),
            dma, dma((3, 2)),
            dma, dma((2, heads)),
            dma, dma((heads,)), dma,
        ],
        compiler_params=pltpu.CompilerParams(
            collective_id=0, has_side_effects=True, vmem_limit_bytes=64 * 1024 * 1024
        ),
        cost_estimate=pl.CostEstimate(
            flops=4 * heads * NQ * NK * D, bytes_accessed=4 * queries.size * 2, transcendentals=heads * NQ * NK
        ),
    )(queries, keys, values, slot_blocks, doc_blocks)


def solution(mesh):
    rows = P(("outer", "inner"), "head")
    return jax.shard_map(
        per_device,
        mesh=mesh,
        in_specs=(rows, rows, rows, P(), P()),
        out_specs=rows,
        check_vma=False,
    )
```

```python
import functools
import math

import jax
import jax.numpy as jnp
from jax import lax
from jax.experimental import pallas as pl
from jax.experimental.pallas import tpu as pltpu
from jax.sharding import PartitionSpec as P

D = 128
BLK = 32
R = 64
NX = 4
NZ = 2
NC = 2
NQ = NX * NZ * R
QT = NX * R
KT = NC * NX * BLK
NK = NC * NZ * NX * R
STAT = 16
SCALE2 = D ** (-0.5) * math.log2(math.e)
HIDE = -1e30
FLOOR = -1e29
MESH = pl.DeviceIdType.MESH
F32 = jnp.float32
BF16 = jnp.bfloat16


def nt(a, b):
    return lax.dot_general(a, b, (((1,), (1,)), ((), ())), preferred_element_type=F32)


def tn(a, b):
    return lax.dot_general(a, b, (((0,), (0,)), ((), ())), preferred_element_type=F32)


def kernel(
    heads,
    q_ref, k_ref, v_ref, slot_hbm, doc_hbm, out_ref,
    slot_ref, doc_ref, qg, kvg, bias, half_o, half_stat, op, orecv, zs, zr_buf, out_buf,
    tab_sem, loc_sem, zkv_s, zkv_r, zq_s, zq_r, kv_s, kv_r, q_s, q_r, c_s, c_r, o_s, o_r, zo_s, zo_r, out_sem,
):
    outer = lax.axis_index("outer")
    inner = lax.axis_index("inner")
    z, c = outer // 2, outer % 2
    x, y = inner // NX, inner % NX
    za = z + 1 - 2 * (z % 2)
    zb = 3 - z
    dev_c = {"outer": z * 2 + 1 - c, "inner": inner}
    first_heads = (heads + 1) // 2
    groups = (0, 1)
    of = (pl.ds(0, first_heads), pl.ds(first_heads, heads - first_heads))

    def pick(g, even, odd):
        return even + g * (odd - even)

    def group_of(h):
        return h // first_heads

    def plane_q(g):
        return {"outer": pick(g, za, zb) * 2 + c, "inner": inner}

    def plane_kv(g):
        return {"outer": pick(g, zb, za) * 2 + c, "inner": inner}

    def along_x(j):
        return lax.rem(x + j, NX) * NX + y

    def along_y(j):
        return x * NX + lax.rem(y + j, NX)

    def ring_q(g, j):
        return {"outer": outer, "inner": pick(g, along_x(j), along_y(j))}

    def ring_kv(g, j):
        return {"outer": outer, "inner": pick(g, along_y(j), along_x(j))}

    def at_q(g, j=0):
        return lax.rem(pick(g, x, y) + j, NX)

    def at_kv(g, j=0):
        return lax.rem(pick(g, y, x) + j, NX)

    tables = (
        pltpu.make_async_copy(slot_hbm, slot_ref, tab_sem.at[0]),
        pltpu.make_async_copy(doc_hbm, doc_ref, tab_sem.at[1]),
    )

    def local(h):
        at = pl.ds(h * D, D)
        g = group_of(h)
        return (
            pltpu.make_async_copy(q_ref.at[:, at], qg.at[at_q(g), 0, h], loc_sem.at[2, h]),
            pltpu.make_async_copy(k_ref.at[:, at], kvg.at[0, 0, 0, at_kv(g), h], loc_sem.at[0, h]),
            pltpu.make_async_copy(v_ref.at[:, at], kvg.at[1, 0, 0, at_kv(g), h], loc_sem.at[1, h]),
        )

    for h in range(heads):
        for copy in local(h):
            copy.start()
    for copy in tables:
        copy.start()

    barrier = pltpu.get_barrier_semaphore()
    partners = [plane_q(0), plane_kv(0), dev_c]
    partners += [ring_q(0, j) for j in (1, 2, 3)] + [ring_kv(0, j) for j in (1, 2, 3)]
    for dev in partners:
        pl.semaphore_signal(barrier, inc=1, device_id=dev, device_id_type=MESH)
    pl.semaphore_wait(barrier, len(partners))

    def remote(src, dst, send, recv, dev):
        return pltpu.make_async_remote_copy(
            src_ref=src, dst_ref=dst, send_sem=send, recv_sem=recv, device_id=dev, device_id_type=MESH
        )

    def z_kv(g):
        here = at_kv(g)
        return remote(
            kvg.at[:, 0, 0, here, of[g]], kvg.at[:, 0, 1, here, of[g]], zkv_s.at[g], zkv_r.at[g], plane_kv(g)
        )

    def z_q(g):
        here = at_q(g)
        return remote(qg.at[here, 0, of[g]], qg.at[here, 1, of[g]], zq_s, zq_r.at[g], plane_q(g))

    def r_kv(g, zr, j):
        block = kvg.at[:, 0, zr, at_kv(g), of[g]]
        return remote(block, block, kv_s, kv_r.at[g, zr], ring_kv(g, j))

    def r_q(g, zr, j):
        block = qg.at[at_q(g), zr, of[g]]
        return remote(block, block, q_s, q_r.at[g, zr], ring_q(g, j))

    def c_kv(g, zr):
        return remote(
            kvg.at[:, 0, zr, :, of[g]], kvg.at[:, 1, zr, :, of[g]], c_s, c_r.at[g, zr], dev_c
        )

    def ring_o(h, zr, j):
        g = group_of(h)
        return remote(
            op.at[zr, h, at_q(g, j)], orecv.at[zr, h, j - 1], o_s, o_r.at[zr, h], ring_q(g, j)
        )

    def z_o(h):
        return remote(zs.at[h], zr_buf.at[h], zo_s, zo_r.at[h], plane_q(group_of(h)))

    def take(ref, sem):
        pltpu.make_async_copy(ref, ref, sem).wait()

    def out_copy(h):
        return pltpu.make_async_copy(
            out_buf.at[h], out_ref.at[:, pl.ds(pl.multiple_of(h * D, D), D)], out_sem
        )

    for h in range(heads):
        for copy in local(h):
            copy.wait()
    for g in groups:
        z_kv(g).start()
    for j in (1, 3, 2):
        for g in groups:
            r_kv(g, 0, j).start()
    for j in (1, 3, 2):
        for g in groups:
            r_q(g, 0, j).start()
    for copy in tables:
        copy.wait()

    ends = [doc_ref[0]]
    for n in range(1, doc_ref.shape[0]):
        ends.append(ends[-1] + doc_ref[n])

    def doc_start(slot):
        start = jnp.int32(0)
        for end in ends:
            start = jnp.where(slot >= end, end, start)
        return start

    lane = lax.broadcasted_iota(jnp.int32, (8, NQ), 1)
    down = lax.broadcasted_iota(jnp.int32, (8, NQ), 0)
    part = lane // BLK
    diagonal = [jnp.where(down + row <= lane % BLK, 0.0, HIDE) for row in range(0, BLK, 8)]

    def build_mask(g):
        q_slot = jnp.zeros((8, NQ), jnp.int32)
        q_low = jnp.zeros((8, NQ), jnp.int32)
        for t in range(NQ // BLK):
            zt, half, rt = t // 8, (t // 4) % 2, t % 4
            zq = z if zt == 0 else (zb if g else za)
            iq = x * NX + rt if g else rt * NX + y
            slot = slot_ref[2 * ((zq * 2 + c) * 16 + iq) + half]
            hit = part == t
            q_slot = jnp.where(hit, slot, q_slot)
            q_low = jnp.where(hit, doc_start(slot), q_low)

        def mask(t, carry):
            ct, zt, half = t // 4, (t // 2) % 2, t % 2
            zk = z + zt * ((za if g else zb) - z)
            ck = c + ct * (1 - 2 * c)
            for rt in range(NX):
                ik = rt * NX + y if g else x * NX + rt
                slot = slot_ref[2 * ((zk * 2 + ck) * 16 + ik) + half]
                before = jnp.where((slot < q_slot) & (slot >= q_low), 0.0, HIDE)
                same = q_slot == slot
                for row in range(0, BLK, 8):
                    at = (zt * 2 + half) * KT + (ct * NX + rt) * BLK + row
                    term = jnp.where(same, diagonal[row // 8], before)
                    for tile in (0, 1):
                        bias[g, tile, pl.ds(pl.multiple_of(at, 8), 8), :] = term[:, tile * QT : (tile + 1) * QT]
            return carry

        lax.fori_loop(0, NC * NZ * 2, mask, 0)

    def swap_cores(zr):
        for g in (1, 0):
            take(kvg.at[:, 0, zr, pl.ds(0, NX - 1), of[g]], kv_r.at[g, zr])
            c_kv(g, zr).start()

    def swap_half(a):
        return pltpu.roll(a, R, axis=1)

    quarter = lax.broadcasted_iota(jnp.int32, (1, D), 1) // BLK

    def gather_lanes(pieces, n):
        moved = [pltpu.roll(p, (k - n) % 4 * BLK, axis=1) if k != n else p for k, p in enumerate(pieces)]
        return jnp.where(
            quarter < 2, jnp.where(quarter == 0, moved[0], moved[1]), jnp.where(quarter == 2, moved[2], moved[3])
        )

    def attend(units, zr):
        half = QT // 2
        scores = []
        for h, tile in units:
            low_keys = kvg[0, :, zr, :, h, 0:BLK, :].reshape(KT, D)
            high_keys = kvg[0, :, zr, :, h, BLK:R, :].reshape(KT, D)
            low_rows = qg[:, tile, h, 0:BLK, :].reshape(half, D)
            high_rows = qg[:, tile, h, BLK:R, :].reshape(half, D)
            g, first = group_of(h), zr * 2 * KT
            rows = jnp.concatenate([low_rows, high_rows], axis=0)
            wide = nt(low_keys, rows) * SCALE2 + bias[g, tile, first : first + KT, :]
            tall = nt(high_keys, high_rows) * SCALE2 + bias[g, tile, first + KT : first + 2 * KT, half:QT]
            scores.append((wide, tall))
        tops = []
        for (h, tile), (wide, tall) in zip(units, scores):
            top = jnp.max(wide, axis=0, keepdims=True)
            low_top, high_top = top[:, 0:half], jnp.maximum(top[:, half:QT], jnp.max(tall, axis=0, keepdims=True))
            top = jnp.concatenate([low_top, high_top], axis=1)
            top = jnp.maximum(top, FLOOR).astype(BF16).astype(F32)
            if zr:
                top = jnp.maximum(top, half_stat[h, tile, 0:1, :])
            tops.append(top)
        results = []
        for (h, tile), (wide, tall), top in zip(units, scores, tops):
            wide = jnp.exp2(wide - top)
            tall = jnp.exp2(tall - top[:, half:QT])
            total = jnp.sum(wide, axis=0, keepdims=True)
            total = (total[:, 0:half], total[:, half:QT] + jnp.sum(tall, axis=0, keepdims=True))
            low_values = kvg[1, :, zr, :, h, 0:BLK, :].reshape(KT, D)
            high_values = kvg[1, :, zr, :, h, BLK:R, :].reshape(KT, D)
            result = tn(low_values, wide.astype(BF16))
            high_result = result[:, half:QT] + tn(high_values, tall.astype(BF16))
            results.append((total, (result[:, 0:half], high_result)))
        row = lax.broadcasted_iota(jnp.int32, (STAT, half), 0)
        for (h, tile), top, (total, result) in zip(units, tops, results):
            sides, stats = [], []
            for side in (0, 1):
                span = slice(side * half, (side + 1) * half)
                m, l, o = top[:, span], total[side], result[side]
                if not zr:
                    half_stat[h, tile, 0:1, span] = m
                    half_stat[h, tile, 1:2, span] = l
                    half_o[h, tile, :, span] = o
                    continue
                shrink = jnp.exp2(half_stat[h, tile, 0:1, span] - m)
                l = l + half_stat[h, tile, 1:2, span] * shrink
                sides.append(o + half_o[h, tile, :, span] * shrink)
                l_hi = l.astype(BF16).astype(F32)
                stats.append(jnp.where(row == 0, m, jnp.where(row == 1, l_hi, l - l_hi)))
            if not zr:
                continue
            pieces = (sides[0][0:R], sides[1][0:R], sides[0][R:D], sides[1][R:D])
            for n in range(NX):
                op[tile, h, n, 0:R, :] = gather_lanes(pieces, n).astype(BF16)
                op[tile, h, n, R : R + STAT, :] = gather_lanes(stats * 2, n).astype(BF16)

    def unstat(block):
        stat = block.astype(F32)
        return stat[0:1], stat[1:2] + stat[2:3]

    def merge_ring(h, zr):
        take(orecv.at[zr, h], o_r.at[zr, h])
        here = at_q(group_of(h))
        parts = [(op[zr, h, here, 0:R, :], unstat(op[zr, h, here, R : R + STAT, :]))]
        for j in (1, 2, 3):
            parts.append((orecv[zr, h, j - 1, 0:R, :], unstat(orecv[zr, h, j - 1, R : R + STAT, :])))
        top = functools.reduce(jnp.maximum, [p[1][0] for p in parts])
        total = jnp.zeros((1, D), F32)
        result = jnp.zeros((R, D), F32)
        for block, (m, l) in parts:
            w = jnp.exp2(m - top)
            total = total + w * l
            result = result + block.astype(F32) * w
        return result, top, total

    def merge_far(h):
        result, top, total = merge_ring(h, 1)
        total_hi = total.astype(BF16).astype(F32)
        row = lax.broadcasted_iota(jnp.int32, (STAT, D), 0)
        zs[h, 0:R, :] = result.astype(BF16)
        zs[h, R : R + STAT, :] = jnp.where(
            row == 0, top, jnp.where(row == 1, total_hi, total - total_hi)
        ).astype(BF16)
        z_o(h).start()

    def finish(h):
        result, m_own, l_own = merge_ring(h, 0)
        z_o(h).wait_recv()
        m_far, l_far = unstat(zr_buf[h, R : R + STAT, :])
        top = jnp.maximum(m_far, m_own)
        w_far, w_own = jnp.exp2(m_far - top), jnp.exp2(m_own - top)
        total = w_far * l_far + w_own * l_own
        w_far, w_own = w_far / total, w_own / total
        packed = result * w_own + zr_buf[h, 0:R, :].astype(F32) * w_far
        tall = jnp.concatenate([packed, swap_half(packed)], axis=0)
        out_buf[h] = tall.T[0:R].astype(BF16)
        out_copy(h).start()

    build_mask(0)
    build_mask(1)
    swap_cores(0)
    for g in (1, 0):
        z_kv(g).wait_send()
        z_q(1 - g).start()
    for g in (1, 0):
        z_kv(g).wait_recv()
        for j in (1, 3, 2):
            r_kv(g, 1, j).start()

    def early(tile):
        for g in groups:
            take(qg.at[pl.ds(0, NX - 1), tile, of[g]], q_r.at[g, tile])
        for h in range(0, heads, 2):
            attend([(n, tile) for n in range(h, min(h + 2, heads))], 0)

    for g in groups:
        c_kv(g, 0).wait_recv()
    early(0)
    for g in groups:
        z_q(g).wait_recv()
        for j in (1, 3, 2):
            r_q(g, 1, j).start()
    early(1)
    swap_cores(1)
    c_kv(1, 1).wait_recv()

    def head_of(unit):
        return lax.rem(unit + jnp.where(unit < heads, first_heads, 0), heads)

    def late(i, carry):
        @pl.when(i == 1)
        def _():
            c_kv(0, 1).wait_recv()

        @pl.when(i < heads)
        def _():
            units = (2 * i, 2 * i + 1)
            works = [(head_of(unit), jnp.where(unit < heads, 1, 0)) for unit in units]
            attend(works, 1)
            for h, tile in works:
                for j in (1, 3, 2):
                    ring_o(h, tile, j).start()

        for k in (0, 1):
            unit = 2 * (i - 2) + k

            @pl.when((unit >= 0) & (unit < heads))
            def _():
                merge_far(head_of(unit))

            @pl.when(unit >= heads)
            def _():
                finish(head_of(unit))

        return carry

    lax.fori_loop(0, heads + 2, late, 0)

    take(qg.at[0, 0], zq_s)
    take(kvg.at[:, 0, :, pl.ds(0, NX - 1)], kv_s)
    take(qg.at[pl.ds(0, NX - 1)], q_s)
    take(kvg.at[:, 0], c_s)
    take(orecv, o_s)
    take(zs, zo_s)
    take(out_buf, out_sem)


def per_device(queries, keys, values, slot_blocks, doc_blocks):
    width = queries.shape[1]
    heads = width // D
    dma = pltpu.SemaphoreType.DMA
    anywhere = pl.BlockSpec(memory_space=pltpu.HBM)
    return pl.pallas_call(
        functools.partial(kernel, heads),
        out_shape=jax.ShapeDtypeStruct(queries.shape, BF16),
        in_specs=[anywhere] * 5,
        out_specs=anywhere,
        scratch_shapes=[
            pltpu.SMEM(slot_blocks.shape, jnp.int32),
            pltpu.SMEM(doc_blocks.shape, jnp.int32),
            pltpu.VMEM((NX, NZ, heads, R, D), BF16),
            pltpu.VMEM((2, NC, NZ, NX, heads, R, D), BF16),
            pltpu.VMEM((2, NZ, NK, QT), F32),
            pltpu.VMEM((heads, NZ, D, QT), F32),
            pltpu.VMEM((heads, NZ, 8, QT), F32),
            pltpu.VMEM((NZ, heads, NX, R + STAT, D), BF16),
            pltpu.VMEM((NZ, heads, NX - 1, R + STAT, D), BF16),
            pltpu.VMEM((heads, R + STAT, D), BF16),
            pltpu.VMEM((heads, R + STAT, D), BF16),
            pltpu.VMEM((heads, R, D), BF16),
            dma((2,)),
            dma((3, heads)),
            dma((2,)), dma((2,)), dma, dma((2,)),
            dma, dma((2, 2)), dma, dma((2, 2)),
            dma, dma((2, 2)),
            dma, dma((2, heads)),
            dma, dma((heads,)), dma,
        ],
        compiler_params=pltpu.CompilerParams(
            collective_id=0, has_side_effects=True, vmem_limit_bytes=64 * 1024 * 1024
        ),
        cost_estimate=pl.CostEstimate(
            flops=4 * heads * NQ * NK * D, bytes_accessed=4 * queries.size * 2, transcendentals=heads * NQ * NK
        ),
    )(queries, keys, values, slot_blocks, doc_blocks)


def solution(mesh):
    rows = P(("outer", "inner"), "head")
    return jax.shard_map(
        per_device,
        mesh=mesh,
        in_specs=(rows, rows, rows, P(), P()),
        out_specs=rows,
        check_vma=False,
    )
```

```python
import functools
import math

import jax
import jax.numpy as jnp
from jax import lax
from jax.experimental import pallas as pl
from jax.experimental.pallas import tpu as pltpu
from jax.sharding import PartitionSpec as P

D = 128
BLK = 32
R = 64
NX = 4
NZ = 2
NC = 2
NQ = NX * NZ * R
QT = NX * R
KT = NC * NX * BLK
NK = NC * NZ * NX * R
STAT = 16
SCALE2 = D ** (-0.5) * math.log2(math.e)
HIDE = -1e30
FLOOR = -1e29
MESH = pl.DeviceIdType.MESH
F32 = jnp.float32
BF16 = jnp.bfloat16


def nt(a, b):
    return lax.dot_general(a, b, (((1,), (1,)), ((), ())), preferred_element_type=F32)


def tn(a, b):
    return lax.dot_general(a, b, (((0,), (0,)), ((), ())), preferred_element_type=F32)


def kernel(
    heads,
    q_ref, k_ref, v_ref, slot_hbm, doc_hbm, out_ref,
    slot_ref, doc_ref, qg, kvg, bias, half_o, half_stat, op, orecv, zs, zr_buf, out_buf,
    tab_sem, loc_sem, zkv_s, zkv_r, zq_s, zq_r, kv_s, kv_r, q_s, q_r, c_s, c_r, o_s, o_r, zo_s, zo_r, out_sem,
):
    outer = lax.axis_index("outer")
    inner = lax.axis_index("inner")
    z, c = outer // 2, outer % 2
    x, y = inner // NX, inner % NX
    za = z + 1 - 2 * (z % 2)
    zb = 3 - z
    dev_c = {"outer": z * 2 + 1 - c, "inner": inner}
    first_heads = (heads + 1) // 2
    groups = (0, 1)
    of = (pl.ds(0, first_heads), pl.ds(first_heads, heads - first_heads))

    def pick(g, even, odd):
        return even + g * (odd - even)

    def group_of(h):
        return h // first_heads

    def plane_q(g):
        return {"outer": pick(g, za, zb) * 2 + c, "inner": inner}

    def plane_kv(g):
        return {"outer": pick(g, zb, za) * 2 + c, "inner": inner}

    def along_x(j):
        return lax.rem(x + j, NX) * NX + y

    def along_y(j):
        return x * NX + lax.rem(y + j, NX)

    def ring_q(g, j):
        return {"outer": outer, "inner": pick(g, along_x(j), along_y(j))}

    def ring_kv(g, j):
        return {"outer": outer, "inner": pick(g, along_y(j), along_x(j))}

    def at_q(g, j=0):
        return lax.rem(pick(g, x, y) + j, NX)

    def at_kv(g, j=0):
        return lax.rem(pick(g, y, x) + j, NX)

    tables = (
        pltpu.make_async_copy(slot_hbm, slot_ref, tab_sem.at[0]),
        pltpu.make_async_copy(doc_hbm, doc_ref, tab_sem.at[1]),
    )

    def local(h):
        at = pl.ds(h * D, D)
        g = group_of(h)
        return (
            pltpu.make_async_copy(q_ref.at[:, at], qg.at[at_q(g), 0, h], loc_sem.at[2, h]),
            pltpu.make_async_copy(k_ref.at[:, at], kvg.at[0, 0, 0, at_kv(g), h], loc_sem.at[0, h]),
            pltpu.make_async_copy(v_ref.at[:, at], kvg.at[1, 0, 0, at_kv(g), h], loc_sem.at[1, h]),
        )

    for h in range(heads):
        for copy in local(h):
            copy.start()
    for copy in tables:
        copy.start()

    barrier = pltpu.get_barrier_semaphore()
    partners = [plane_q(0), plane_kv(0), dev_c]
    partners += [ring_q(0, j) for j in (1, 2, 3)] + [ring_kv(0, j) for j in (1, 2, 3)]
    for dev in partners:
        pl.semaphore_signal(barrier, inc=1, device_id=dev, device_id_type=MESH)
    pl.semaphore_wait(barrier, len(partners))

    def remote(src, dst, send, recv, dev):
        return pltpu.make_async_remote_copy(
            src_ref=src, dst_ref=dst, send_sem=send, recv_sem=recv, device_id=dev, device_id_type=MESH
        )

    def z_kv(g):
        here = at_kv(g)
        return remote(
            kvg.at[:, 0, 0, here, of[g]], kvg.at[:, 0, 1, here, of[g]], zkv_s.at[g], zkv_r.at[g], plane_kv(g)
        )

    def z_q(g):
        here = at_q(g)
        return remote(qg.at[here, 0, of[g]], qg.at[here, 1, of[g]], zq_s, zq_r.at[g], plane_q(g))

    def r_kv(g, zr, j):
        block = kvg.at[:, 0, zr, at_kv(g), of[g]]
        return remote(block, block, kv_s, kv_r.at[g, zr], ring_kv(g, j))

    def r_q(g, zr, j):
        block = qg.at[at_q(g), zr, of[g]]
        return remote(block, block, q_s, q_r.at[g, zr], ring_q(g, j))

    def c_kv(g, zr):
        return remote(
            kvg.at[:, 0, zr, :, of[g]], kvg.at[:, 1, zr, :, of[g]], c_s, c_r.at[g, zr], dev_c
        )

    def ring_o(h, zr, j):
        g = group_of(h)
        return remote(
            op.at[zr, h, at_q(g, j)], orecv.at[zr, h, j - 1], o_s, o_r.at[zr, h], ring_q(g, j)
        )

    def z_o(h):
        return remote(zs.at[h], zr_buf.at[h], zo_s, zo_r.at[h], plane_q(group_of(h)))

    def take(ref, sem):
        pltpu.make_async_copy(ref, ref, sem).wait()

    def out_copy(h):
        return pltpu.make_async_copy(
            out_buf.at[h], out_ref.at[:, pl.ds(pl.multiple_of(h * D, D), D)], out_sem
        )

    for h in range(heads):
        for copy in local(h):
            copy.wait()
    for g in groups:
        z_kv(g).start()
    for j in (1, 3, 2):
        for g in groups:
            r_kv(g, 0, j).start()
    for j in (1, 3, 2):
        for g in groups:
            r_q(g, 0, j).start()
    for copy in tables:
        copy.wait()

    ends = [doc_ref[0]]
    for n in range(1, doc_ref.shape[0]):
        ends.append(ends[-1] + doc_ref[n])

    def doc_start(slot):
        start = jnp.int32(0)
        for end in ends:
            start = jnp.where(slot >= end, end, start)
        return start

    lane = lax.broadcasted_iota(jnp.int32, (8, NQ), 1)
    down = lax.broadcasted_iota(jnp.int32, (8, NQ), 0)
    part = lane // BLK
    diagonal = [jnp.where(down + row <= lane % BLK, 0.0, HIDE) for row in range(0, BLK, 8)]

    def build_mask(g):
        q_slot = jnp.zeros((8, NQ), jnp.int32)
        q_low = jnp.zeros((8, NQ), jnp.int32)
        for t in range(NQ // BLK):
            zt, half, rt = t // 8, (t // 4) % 2, t % 4
            zq = z if zt == 0 else (zb if g else za)
            iq = x * NX + rt if g else rt * NX + y
            slot = slot_ref[2 * ((zq * 2 + c) * 16 + iq) + half]
            hit = part == t
            q_slot = jnp.where(hit, slot, q_slot)
            q_low = jnp.where(hit, doc_start(slot), q_low)

        def mask(t, carry):
            ct, zt, half = t // 4, (t // 2) % 2, t % 2
            zk = z + zt * ((za if g else zb) - z)
            ck = c + ct * (1 - 2 * c)
            for rt in range(NX):
                ik = rt * NX + y if g else x * NX + rt
                slot = slot_ref[2 * ((zk * 2 + ck) * 16 + ik) + half]
                before = jnp.where((slot < q_slot) & (slot >= q_low), 0.0, HIDE)
                same = q_slot == slot
                for row in range(0, BLK, 8):
                    at = (zt * 2 + half) * KT + (ct * NX + rt) * BLK + row
                    term = jnp.where(same, diagonal[row // 8], before)
                    for tile in (0, 1):
                        bias[g, tile, pl.ds(pl.multiple_of(at, 8), 8), :] = term[:, tile * QT : (tile + 1) * QT]
            return carry

        lax.fori_loop(0, NC * NZ * 2, mask, 0)

    def swap_cores(zr):
        for g in (1, 0):
            take(kvg.at[:, 0, zr, pl.ds(0, NX - 1), of[g]], kv_r.at[g, zr])
            c_kv(g, zr).start()

    def swap_half(a):
        return pltpu.roll(a, R, axis=1)

    quarter = lax.broadcasted_iota(jnp.int32, (1, D), 1) // BLK

    def gather_lanes(pieces, n):
        moved = [pltpu.roll(p, (k - n) % 4 * BLK, axis=1) if k != n else p for k, p in enumerate(pieces)]
        return jnp.where(
            quarter < 2, jnp.where(quarter == 0, moved[0], moved[1]), jnp.where(quarter == 2, moved[2], moved[3])
        )

    def attend(units, zr):
        half = QT // 2
        scores = []
        for h, tile in units:
            low_keys = kvg[0, :, zr, :, h, 0:BLK, :].reshape(KT, D)
            high_keys = kvg[0, :, zr, :, h, BLK:R, :].reshape(KT, D)
            low_rows = qg[:, tile, h, 0:BLK, :].reshape(half, D)
            high_rows = qg[:, tile, h, BLK:R, :].reshape(half, D)
            g, first = group_of(h), zr * 2 * KT
            rows = jnp.concatenate([low_rows, high_rows], axis=0)
            wide = nt(low_keys, rows) * SCALE2 + bias[g, tile, first : first + KT, :]
            tall = nt(high_keys, high_rows) * SCALE2 + bias[g, tile, first + KT : first + 2 * KT, half:QT]
            scores.append((wide, tall))
        tops = []
        for (h, tile), (wide, tall) in zip(units, scores):
            top = jnp.max(wide, axis=0, keepdims=True)
            low_top, high_top = top[:, 0:half], jnp.maximum(top[:, half:QT], jnp.max(tall, axis=0, keepdims=True))
            top = jnp.concatenate([low_top, high_top], axis=1)
            top = jnp.maximum(top, FLOOR).astype(BF16).astype(F32)
            if zr:
                top = jnp.maximum(top, half_stat[h, tile, 0:1, :])
            tops.append(top)
        results = []
        for (h, tile), (wide, tall), top in zip(units, scores, tops):
            wide = jnp.exp2(wide - top)
            tall = jnp.exp2(tall - top[:, half:QT])
            total = jnp.sum(wide, axis=0, keepdims=True)
            total = (total[:, 0:half], total[:, half:QT] + jnp.sum(tall, axis=0, keepdims=True))
            low_values = kvg[1, :, zr, :, h, 0:BLK, :].reshape(KT, D)
            high_values = kvg[1, :, zr, :, h, BLK:R, :].reshape(KT, D)
            result = tn(low_values, wide.astype(BF16))
            high_result = result[:, half:QT] + tn(high_values, tall.astype(BF16))
            results.append((total, (result[:, 0:half], high_result)))
        row = lax.broadcasted_iota(jnp.int32, (STAT, half), 0)
        for (h, tile), top, (total, result) in zip(units, tops, results):
            sides, stats = [], []
            for side in (0, 1):
                span = slice(side * half, (side + 1) * half)
                m, l, o = top[:, span], total[side], result[side]
                if not zr:
                    half_stat[h, tile, 0:1, span] = m
                    half_stat[h, tile, 1:2, span] = l
                    half_o[h, tile, :, span] = o
                    continue
                shrink = jnp.exp2(half_stat[h, tile, 0:1, span] - m)
                l = l + half_stat[h, tile, 1:2, span] * shrink
                sides.append(o + half_o[h, tile, :, span] * shrink)
                l_hi = l.astype(BF16).astype(F32)
                stats.append(jnp.where(row == 0, m, jnp.where(row == 1, l_hi, l - l_hi)))
            if not zr:
                continue
            pieces = (sides[0][0:R], sides[1][0:R], sides[0][R:D], sides[1][R:D])
            for n in range(NX):
                op[tile, h, n, 0:R, :] = gather_lanes(pieces, n).astype(BF16)
                op[tile, h, n, R : R + STAT, :] = gather_lanes(stats * 2, n).astype(BF16)

    def unstat(block):
        stat = block.astype(F32)
        return stat[0:1], stat[1:2] + stat[2:3]

    def merge_ring(h, zr):
        take(orecv.at[zr, h], o_r.at[zr, h])
        here = at_q(group_of(h))
        parts = [(op[zr, h, here, 0:R, :], unstat(op[zr, h, here, R : R + STAT, :]))]
        for j in (1, 2, 3):
            parts.append((orecv[zr, h, j - 1, 0:R, :], unstat(orecv[zr, h, j - 1, R : R + STAT, :])))
        top = functools.reduce(jnp.maximum, [p[1][0] for p in parts])
        total = jnp.zeros((1, D), F32)
        result = jnp.zeros((R, D), F32)
        for block, (m, l) in parts:
            w = jnp.exp2(m - top)
            total = total + w * l
            result = result + block.astype(F32) * w
        return result, top, total

    def merge_far(h):
        result, top, total = merge_ring(h, 1)
        total_hi = total.astype(BF16).astype(F32)
        row = lax.broadcasted_iota(jnp.int32, (STAT, D), 0)
        zs[h, 0:R, :] = result.astype(BF16)
        zs[h, R : R + STAT, :] = jnp.where(
            row == 0, top, jnp.where(row == 1, total_hi, total - total_hi)
        ).astype(BF16)
        z_o(h).start()

    def finish(h):
        result, m_own, l_own = merge_ring(h, 0)
        z_o(h).wait_recv()
        m_far, l_far = unstat(zr_buf[h, R : R + STAT, :])
        top = jnp.maximum(m_far, m_own)
        w_far, w_own = jnp.exp2(m_far - top), jnp.exp2(m_own - top)
        total = w_far * l_far + w_own * l_own
        w_far, w_own = w_far / total, w_own / total
        packed = result * w_own + zr_buf[h, 0:R, :].astype(F32) * w_far
        tall = jnp.concatenate([packed, swap_half(packed)], axis=0)
        out_buf[h] = tall.T[0:R].astype(BF16)
        out_copy(h).start()

    build_mask(0)
    build_mask(1)
    swap_cores(0)
    for g in (1, 0):
        z_kv(g).wait_send()
        z_q(1 - g).start()
    for g in groups:
        z_kv(g).wait_recv()
        for j in (1, 3, 2):
            r_kv(g, 1, j).start()

    def early(tile):
        for g in groups:
            take(qg.at[pl.ds(0, NX - 1), tile, of[g]], q_r.at[g, tile])
        for h in range(0, heads, 2):
            attend([(n, tile) for n in range(h, min(h + 2, heads))], 0)

    for g in groups:
        c_kv(g, 0).wait_recv()
    early(0)
    for g in groups:
        z_q(g).wait_recv()
        for j in (1, 3, 2):
            r_q(g, 1, j).start()
    early(1)
    swap_cores(1)
    for g in (1, 0):
        c_kv(g, 1).wait_recv()

    def head_of(unit):
        return lax.rem(unit * first_heads, heads)

    def late(i, carry):
        @pl.when(i < heads)
        def _():
            units = (2 * i, 2 * i + 1)
            works = [(head_of(unit), jnp.where(unit < heads, 1, 0)) for unit in units]
            attend(works, 1)
            for h, tile in works:
                for j in (1, 3, 2):
                    ring_o(h, tile, j).start()

        for k in (0, 1):
            unit = 2 * (i - 3) + k

            @pl.when((unit >= 0) & (unit < heads))
            def _():
                merge_far(head_of(unit))

            @pl.when(unit >= heads)
            def _():
                finish(head_of(unit))

        return carry

    lax.fori_loop(0, heads + 3, late, 0)

    take(qg.at[0, 0], zq_s)
    take(kvg.at[:, 0, :, pl.ds(0, NX - 1)], kv_s)
    take(qg.at[pl.ds(0, NX - 1)], q_s)
    take(kvg.at[:, 0], c_s)
    take(orecv, o_s)
    take(zs, zo_s)
    take(out_buf, out_sem)


def per_device(queries, keys, values, slot_blocks, doc_blocks):
    width = queries.shape[1]
    heads = width // D
    dma = pltpu.SemaphoreType.DMA
    anywhere = pl.BlockSpec(memory_space=pltpu.HBM)
    return pl.pallas_call(
        functools.partial(kernel, heads),
        out_shape=jax.ShapeDtypeStruct(queries.shape, BF16),
        in_specs=[anywhere] * 5,
        out_specs=anywhere,
        scratch_shapes=[
            pltpu.SMEM(slot_blocks.shape, jnp.int32),
            pltpu.SMEM(doc_blocks.shape, jnp.int32),
            pltpu.VMEM((NX, NZ, heads, R, D), BF16),
            pltpu.VMEM((2, NC, NZ, NX, heads, R, D), BF16),
            pltpu.VMEM((2, NZ, NK, QT), F32),
            pltpu.VMEM((heads, NZ, D, QT), F32),
            pltpu.VMEM((heads, NZ, 8, QT), F32),
            pltpu.VMEM((NZ, heads, NX, R + STAT, D), BF16),
            pltpu.VMEM((NZ, heads, NX - 1, R + STAT, D), BF16),
            pltpu.VMEM((heads, R + STAT, D), BF16),
            pltpu.VMEM((heads, R + STAT, D), BF16),
            pltpu.VMEM((heads, R, D), BF16),
            dma((2,)),
            dma((3, heads)),
            dma((2,)), dma((2,)), dma, dma((2,)),
            dma, dma((2, 2)), dma, dma((2, 2)),
            dma, dma((2, 2)),
            dma, dma((2, heads)),
            dma, dma((heads,)), dma,
        ],
        compiler_params=pltpu.CompilerParams(
            collective_id=0, has_side_effects=True, vmem_limit_bytes=64 * 1024 * 1024
        ),
        cost_estimate=pl.CostEstimate(
            flops=4 * heads * NQ * NK * D, bytes_accessed=4 * queries.size * 2, transcendentals=heads * NQ * NK
        ),
    )(queries, keys, values, slot_blocks, doc_blocks)


def solution(mesh):
    rows = P(("outer", "inner"), "head")
    return jax.shard_map(
        per_device,
        mesh=mesh,
        in_specs=(rows, rows, rows, P(), P()),
        out_specs=rows,
        check_vma=False,
    )
```

```python
import functools
import math

import jax
import jax.numpy as jnp
from jax import lax
from jax.experimental import pallas as pl
from jax.experimental.pallas import tpu as pltpu
from jax.sharding import PartitionSpec as P

D = 128
BLK = 32
R = 64
NX = 4
NZ = 2
NC = 2
NQ = NX * NZ * R
QT = NX * R
KT = NC * NX * BLK
NK = NC * NZ * NX * R
STAT = 16
SCALE2 = D ** (-0.5) * math.log2(math.e)
HIDE = -1e30
FLOOR = -1e29
MESH = pl.DeviceIdType.MESH
F32 = jnp.float32
BF16 = jnp.bfloat16


def nt(a, b):
    return lax.dot_general(a, b, (((1,), (1,)), ((), ())), preferred_element_type=F32)


def tn(a, b):
    return lax.dot_general(a, b, (((0,), (0,)), ((), ())), preferred_element_type=F32)


def kernel(
    heads,
    q_ref, k_ref, v_ref, slot_hbm, doc_hbm, out_ref,
    slot_ref, doc_ref, qg, kvg, bias, half_o, half_stat, op, orecv, zs, zr_buf, out_buf,
    tab_sem, loc_sem, zkv_s, zkv_r, zq_s, zq_r, kv_s, kv_r, q_s, q_r, c_s, c_r, o_s, o_r, zo_s, zo_r, out_sem,
):
    outer = lax.axis_index("outer")
    inner = lax.axis_index("inner")
    z, c = outer // 2, outer % 2
    x, y = inner // NX, inner % NX
    za = z + 1 - 2 * (z % 2)
    zb = 3 - z
    dev_c = {"outer": z * 2 + 1 - c, "inner": inner}
    first_heads = (heads + 1) // 2
    groups = (0, 1)
    of = (pl.ds(0, first_heads), pl.ds(first_heads, heads - first_heads))

    def pick(g, even, odd):
        return even + g * (odd - even)

    def group_of(h):
        return h // first_heads

    def plane_q(g):
        return {"outer": pick(g, za, zb) * 2 + c, "inner": inner}

    def plane_kv(g):
        return {"outer": pick(g, zb, za) * 2 + c, "inner": inner}

    def along_x(j):
        return lax.rem(x + j, NX) * NX + y

    def along_y(j):
        return x * NX + lax.rem(y + j, NX)

    def ring_q(g, j):
        return {"outer": outer, "inner": pick(g, along_x(j), along_y(j))}

    def ring_kv(g, j):
        return {"outer": outer, "inner": pick(g, along_y(j), along_x(j))}

    def at_q(g, j=0):
        return lax.rem(pick(g, x, y) + j, NX)

    def at_kv(g, j=0):
        return lax.rem(pick(g, y, x) + j, NX)

    tables = (
        pltpu.make_async_copy(slot_hbm, slot_ref, tab_sem.at[0]),
        pltpu.make_async_copy(doc_hbm, doc_ref, tab_sem.at[1]),
    )

    def local(h):
        at = pl.ds(h * D, D)
        g = group_of(h)
        return (
            pltpu.make_async_copy(q_ref.at[:, at], qg.at[at_q(g), 0, h], loc_sem.at[2, h]),
            pltpu.make_async_copy(k_ref.at[:, at], kvg.at[0, 0, 0, at_kv(g), h], loc_sem.at[0, h]),
            pltpu.make_async_copy(v_ref.at[:, at], kvg.at[1, 0, 0, at_kv(g), h], loc_sem.at[1, h]),
        )

    for h in range(heads):
        for copy in local(h):
            copy.start()
    for copy in tables:
        copy.start()

    barrier = pltpu.get_barrier_semaphore()
    partners = [plane_q(0), plane_kv(0), dev_c]
    partners += [ring_q(0, j) for j in (1, 2, 3)] + [ring_kv(0, j) for j in (1, 2, 3)]
    for dev in partners:
        pl.semaphore_signal(barrier, inc=1, device_id=dev, device_id_type=MESH)
    pl.semaphore_wait(barrier, len(partners))

    def remote(src, dst, send, recv, dev):
        return pltpu.make_async_remote_copy(
            src_ref=src, dst_ref=dst, send_sem=send, recv_sem=recv, device_id=dev, device_id_type=MESH
        )

    def z_kv(g):
        here = at_kv(g)
        return remote(
            kvg.at[:, 0, 0, here, of[g]], kvg.at[:, 0, 1, here, of[g]], zkv_s.at[g], zkv_r.at[g], plane_kv(g)
        )

    def z_q(g):
        here = at_q(g)
        return remote(qg.at[here, 0, of[g]], qg.at[here, 1, of[g]], zq_s, zq_r.at[g], plane_q(g))

    def r_kv(g, zr, j):
        block = kvg.at[:, 0, zr, at_kv(g), of[g]]
        return remote(block, block, kv_s, kv_r.at[g, zr], ring_kv(g, j))

    def r_q(g, zr, j):
        block = qg.at[at_q(g), zr, of[g]]
        return remote(block, block, q_s, q_r.at[g, zr], ring_q(g, j))

    def c_kv(g, zr):
        return remote(
            kvg.at[:, 0, zr, :, of[g]], kvg.at[:, 1, zr, :, of[g]], c_s, c_r.at[g, zr], dev_c
        )

    def ring_o(h, zr, j):
        g = group_of(h)
        return remote(
            op.at[zr, h, at_q(g, j)], orecv.at[zr, h, j - 1], o_s, o_r.at[zr, h], ring_q(g, j)
        )

    def z_o(h):
        return remote(zs.at[h], zr_buf.at[h], zo_s, zo_r.at[h], plane_q(group_of(h)))

    def take(ref, sem):
        pltpu.make_async_copy(ref, ref, sem).wait()

    def out_copy(h):
        return pltpu.make_async_copy(
            out_buf.at[h], out_ref.at[:, pl.ds(pl.multiple_of(h * D, D), D)], out_sem
        )

    for h in range(heads):
        for copy in local(h):
            copy.wait()
    for g in groups:
        z_kv(g).start()
    for j in (2, 1, 3):
        for g in groups:
            r_kv(g, 0, j).start()
    for j in (2, 1, 3):
        for g in groups:
            r_q(g, 0, j).start()
    for copy in tables:
        copy.wait()

    ends = [doc_ref[0]]
    for n in range(1, doc_ref.shape[0]):
        ends.append(ends[-1] + doc_ref[n])

    def doc_start(slot):
        start = jnp.int32(0)
        for end in ends:
            start = jnp.where(slot >= end, end, start)
        return start

    lane = lax.broadcasted_iota(jnp.int32, (8, NQ), 1)
    down = lax.broadcasted_iota(jnp.int32, (8, NQ), 0)
    part = lane // BLK
    diagonal = [jnp.where(down + row <= lane % BLK, 0.0, HIDE) for row in range(0, BLK, 8)]

    def build_mask(g):
        q_slot = jnp.zeros((8, NQ), jnp.int32)
        q_low = jnp.zeros((8, NQ), jnp.int32)
        for t in range(NQ // BLK):
            zt, half, rt = t // 8, (t // 4) % 2, t % 4
            zq = z if zt == 0 else (zb if g else za)
            iq = x * NX + rt if g else rt * NX + y
            slot = slot_ref[2 * ((zq * 2 + c) * 16 + iq) + half]
            hit = part == t
            q_slot = jnp.where(hit, slot, q_slot)
            q_low = jnp.where(hit, doc_start(slot), q_low)

        def mask(t, carry):
            ct, zt, half = t // 4, (t // 2) % 2, t % 2
            zk = z + zt * ((za if g else zb) - z)
            ck = c + ct * (1 - 2 * c)
            for rt in range(NX):
                ik = rt * NX + y if g else x * NX + rt
                slot = slot_ref[2 * ((zk * 2 + ck) * 16 + ik) + half]
                before = jnp.where((slot < q_slot) & (slot >= q_low), 0.0, HIDE)
                same = q_slot == slot
                for row in range(0, BLK, 8):
                    at = (zt * 2 + half) * KT + (ct * NX + rt) * BLK + row
                    term = jnp.where(same, diagonal[row // 8], before)
                    for tile in (0, 1):
                        bias[g, tile, pl.ds(pl.multiple_of(at, 8), 8), :] = term[:, tile * QT : (tile + 1) * QT]
            return carry

        lax.fori_loop(0, NC * NZ * 2, mask, 0)

    def swap_cores(zr):
        for g in (1, 0):
            take(kvg.at[:, 0, zr, pl.ds(0, NX - 1), of[g]], kv_r.at[g, zr])
            c_kv(g, zr).start()

    def swap_half(a):
        return pltpu.roll(a, R, axis=1)

    quarter = lax.broadcasted_iota(jnp.int32, (1, D), 1) // BLK

    def gather_lanes(pieces, n):
        moved = [pltpu.roll(p, (k - n) % 4 * BLK, axis=1) if k != n else p for k, p in enumerate(pieces)]
        return jnp.where(
            quarter < 2, jnp.where(quarter == 0, moved[0], moved[1]), jnp.where(quarter == 2, moved[2], moved[3])
        )

    def attend(units, zr):
        half = QT // 2
        scores = []
        for h, tile in units:
            low_keys = kvg[0, :, zr, :, h, 0:BLK, :].reshape(KT, D)
            high_keys = kvg[0, :, zr, :, h, BLK:R, :].reshape(KT, D)
            low_rows = qg[:, tile, h, 0:BLK, :].reshape(half, D)
            high_rows = qg[:, tile, h, BLK:R, :].reshape(half, D)
            g, first = group_of(h), zr * 2 * KT
            rows = jnp.concatenate([low_rows, high_rows], axis=0)
            wide = nt(low_keys, rows) * SCALE2 + bias[g, tile, first : first + KT, :]
            tall = nt(high_keys, high_rows) * SCALE2 + bias[g, tile, first + KT : first + 2 * KT, half:QT]
            scores.append((wide, tall))
        tops = []
        for (h, tile), (wide, tall) in zip(units, scores):
            top = jnp.max(wide, axis=0, keepdims=True)
            low_top, high_top = top[:, 0:half], jnp.maximum(top[:, half:QT], jnp.max(tall, axis=0, keepdims=True))
            top = jnp.concatenate([low_top, high_top], axis=1)
            top = jnp.maximum(top, FLOOR).astype(BF16).astype(F32)
            if zr:
                top = jnp.maximum(top, half_stat[h, tile, 0:1, :])
            tops.append(top)
        results = []
        for (h, tile), (wide, tall), top in zip(units, scores, tops):
            wide = jnp.exp2(wide - top)
            tall = jnp.exp2(tall - top[:, half:QT])
            total = jnp.sum(wide, axis=0, keepdims=True)
            total = (total[:, 0:half], total[:, half:QT] + jnp.sum(tall, axis=0, keepdims=True))
            low_values = kvg[1, :, zr, :, h, 0:BLK, :].reshape(KT, D)
            high_values = kvg[1, :, zr, :, h, BLK:R, :].reshape(KT, D)
            result = tn(low_values, wide.astype(BF16))
            high_result = result[:, half:QT] + tn(high_values, tall.astype(BF16))
            results.append((total, (result[:, 0:half], high_result)))
        row = lax.broadcasted_iota(jnp.int32, (STAT, half), 0)
        for (h, tile), top, (total, result) in zip(units, tops, results):
            sides, stats = [], []
            for side in (0, 1):
                span = slice(side * half, (side + 1) * half)
                m, l, o = top[:, span], total[side], result[side]
                if not zr:
                    half_stat[h, tile, 0:1, span] = m
                    half_stat[h, tile, 1:2, span] = l
                    half_o[h, tile, :, span] = o
                    continue
                shrink = jnp.exp2(half_stat[h, tile, 0:1, span] - m)
                l = l + half_stat[h, tile, 1:2, span] * shrink
                sides.append(o + half_o[h, tile, :, span] * shrink)
                l_hi = l.astype(BF16).astype(F32)
                stats.append(jnp.where(row == 0, m, jnp.where(row == 1, l_hi, l - l_hi)))
            if not zr:
                continue
            pieces = (sides[0][0:R], sides[1][0:R], sides[0][R:D], sides[1][R:D])
            for n in range(NX):
                op[tile, h, n, 0:R, :] = gather_lanes(pieces, n).astype(BF16)
                op[tile, h, n, R : R + STAT, :] = gather_lanes(stats * 2, n).astype(BF16)

    def unstat(block):
        stat = block.astype(F32)
        return stat[0:1], stat[1:2] + stat[2:3]

    def merge_ring(h, zr):
        take(orecv.at[zr, h], o_r.at[zr, h])
        here = at_q(group_of(h))
        parts = [(op[zr, h, here, 0:R, :], unstat(op[zr, h, here, R : R + STAT, :]))]
        for j in (1, 2, 3):
            parts.append((orecv[zr, h, j - 1, 0:R, :], unstat(orecv[zr, h, j - 1, R : R + STAT, :])))
        top = functools.reduce(jnp.maximum, [p[1][0] for p in parts])
        total = jnp.zeros((1, D), F32)
        result = jnp.zeros((R, D), F32)
        for block, (m, l) in parts:
            w = jnp.exp2(m - top)
            total = total + w * l
            result = result + block.astype(F32) * w
        return result, top, total

    def merge_far(h):
        result, top, total = merge_ring(h, 1)
        total_hi = total.astype(BF16).astype(F32)
        row = lax.broadcasted_iota(jnp.int32, (STAT, D), 0)
        zs[h, 0:R, :] = result.astype(BF16)
        zs[h, R : R + STAT, :] = jnp.where(
            row == 0, top, jnp.where(row == 1, total_hi, total - total_hi)
        ).astype(BF16)
        z_o(h).start()

    def finish(h):
        result, m_own, l_own = merge_ring(h, 0)
        z_o(h).wait_recv()
        m_far, l_far = unstat(zr_buf[h, R : R + STAT, :])
        top = jnp.maximum(m_far, m_own)
        w_far, w_own = jnp.exp2(m_far - top), jnp.exp2(m_own - top)
        total = w_far * l_far + w_own * l_own
        w_far, w_own = w_far / total, w_own / total
        packed = result * w_own + zr_buf[h, 0:R, :].astype(F32) * w_far
        tall = jnp.concatenate([packed, swap_half(packed)], axis=0)
        out_buf[h] = tall.T[0:R].astype(BF16)
        out_copy(h).start()

    build_mask(0)
    build_mask(1)
    swap_cores(0)
    for g in groups:
        z_kv(g).wait_send()
        z_q(g).start()
    for g in groups:
        z_kv(g).wait_recv()
        for j in (2, 1, 3):
            r_kv(g, 1, j).start()

    def early(tile):
        for g in groups:
            take(qg.at[pl.ds(0, NX - 1), tile, of[g]], q_r.at[g, tile])
        for h in range(0, heads, 2):
            attend([(n, tile) for n in range(h, min(h + 2, heads))], 0)

    for g in groups:
        c_kv(g, 0).wait_recv()
    early(0)
    for g in groups:
        z_q(g).wait_recv()
        for j in (2, 1, 3):
            r_q(g, 1, j).start()
    early(1)
    swap_cores(1)
    for g in (1, 0):
        c_kv(g, 1).wait_recv()

    def head_of(unit):
        return lax.rem(unit * first_heads, heads)

    def late(i, carry):
        @pl.when(i < heads)
        def _():
            units = (2 * i, 2 * i + 1)
            works = [(head_of(unit), jnp.where(unit < heads, 1, 0)) for unit in units]
            attend(works, 1)
            for h, tile in works:
                for j in (2, 1, 3):
                    ring_o(h, tile, j).start()

        for k in (0, 1):
            unit = 2 * (i - 2) + k

            @pl.when((unit >= 0) & (unit < heads))
            def _():
                merge_far(head_of(unit))

            @pl.when(unit >= heads)
            def _():
                finish(head_of(unit))

        return carry

    lax.fori_loop(0, heads + 2, late, 0)

    take(qg.at[0, 0], zq_s)
    take(kvg.at[:, 0, :, pl.ds(0, NX - 1)], kv_s)
    take(qg.at[pl.ds(0, NX - 1)], q_s)
    take(kvg.at[:, 0], c_s)
    take(orecv, o_s)
    take(zs, zo_s)
    take(out_buf, out_sem)


def per_device(queries, keys, values, slot_blocks, doc_blocks):
    width = queries.shape[1]
    heads = width // D
    dma = pltpu.SemaphoreType.DMA
    anywhere = pl.BlockSpec(memory_space=pltpu.HBM)
    return pl.pallas_call(
        functools.partial(kernel, heads),
        out_shape=jax.ShapeDtypeStruct(queries.shape, BF16),
        in_specs=[anywhere] * 5,
        out_specs=anywhere,
        scratch_shapes=[
            pltpu.SMEM(slot_blocks.shape, jnp.int32),
            pltpu.SMEM(doc_blocks.shape, jnp.int32),
            pltpu.VMEM((NX, NZ, heads, R, D), BF16),
            pltpu.VMEM((2, NC, NZ, NX, heads, R, D), BF16),
            pltpu.VMEM((2, NZ, NK, QT), F32),
            pltpu.VMEM((heads, NZ, D, QT), F32),
            pltpu.VMEM((heads, NZ, 8, QT), F32),
            pltpu.VMEM((NZ, heads, NX, R + STAT, D), BF16),
            pltpu.VMEM((NZ, heads, NX - 1, R + STAT, D), BF16),
            pltpu.VMEM((heads, R + STAT, D), BF16),
            pltpu.VMEM((heads, R + STAT, D), BF16),
            pltpu.VMEM((heads, R, D), BF16),
            dma((2,)),
            dma((3, heads)),
            dma((2,)), dma((2,)), dma, dma((2,)),
            dma, dma((2, 2)), dma, dma((2, 2)),
            dma, dma((2, 2)),
            dma, dma((2, heads)),
            dma, dma((heads,)), dma,
        ],
        compiler_params=pltpu.CompilerParams(
            collective_id=0, has_side_effects=True, vmem_limit_bytes=64 * 1024 * 1024
        ),
        cost_estimate=pl.CostEstimate(
            flops=4 * heads * NQ * NK * D, bytes_accessed=4 * queries.size * 2, transcendentals=heads * NQ * NK
        ),
    )(queries, keys, values, slot_blocks, doc_blocks)


def solution(mesh):
    rows = P(("outer", "inner"), "head")
    return jax.shard_map(
        per_device,
        mesh=mesh,
        in_specs=(rows, rows, rows, P(), P()),
        out_specs=rows,
        check_vma=False,
    )
```

```python
import functools
import math

import jax
import jax.numpy as jnp
from jax import lax
from jax.experimental import pallas as pl
from jax.experimental.pallas import tpu as pltpu
from jax.sharding import PartitionSpec as P

D = 128
BLK = 32
R = 64
NX = 4
NZ = 2
NC = 2
NQ = NX * NZ * R
QT = NX * R
KT = NC * NX * BLK
NK = NC * NZ * NX * R
STAT = 16
SCALE2 = D ** (-0.5) * math.log2(math.e)
HIDE = -1e30
FLOOR = -1e29
MESH = pl.DeviceIdType.MESH
F32 = jnp.float32
BF16 = jnp.bfloat16


def nt(a, b):
    return lax.dot_general(a, b, (((1,), (1,)), ((), ())), preferred_element_type=F32)


def tn(a, b):
    return lax.dot_general(a, b, (((0,), (0,)), ((), ())), preferred_element_type=F32)


def kernel(
    heads,
    q_ref, k_ref, v_ref, slot_hbm, doc_hbm, out_ref,
    slot_ref, doc_ref, qg, kvg, bias, half_o, half_stat, op, orecv, zs, zr_buf, out_buf,
    tab_sem, loc_sem, zkv_s, zkv_r, zq_s, zq_r, kv_s, kv_r, q_s, q_r, c_s, c_r, o_s, o_r, zo_s, zo_r, out_sem,
):
    outer = lax.axis_index("outer")
    inner = lax.axis_index("inner")
    z, c = outer // 2, outer % 2
    x, y = inner // NX, inner % NX
    za = z + 1 - 2 * (z % 2)
    zb = 3 - z
    dev_c = {"outer": z * 2 + 1 - c, "inner": inner}
    first_heads = (heads + 1) // 2
    groups = (0, 1)
    of = (pl.ds(0, first_heads), pl.ds(first_heads, heads - first_heads))

    def pick(g, even, odd):
        return even + g * (odd - even)

    def group_of(h):
        return h // first_heads

    def plane_q(g):
        return {"outer": pick(g, za, zb) * 2 + c, "inner": inner}

    def plane_kv(g):
        return {"outer": pick(g, zb, za) * 2 + c, "inner": inner}

    def along_x(j):
        return lax.rem(x + j, NX) * NX + y

    def along_y(j):
        return x * NX + lax.rem(y + j, NX)

    def ring_q(g, j):
        return {"outer": outer, "inner": pick(g, along_x(j), along_y(j))}

    def ring_kv(g, j):
        return {"outer": outer, "inner": pick(g, along_y(j), along_x(j))}

    def at_q(g, j=0):
        return lax.rem(pick(g, x, y) + j, NX)

    def at_kv(g, j=0):
        return lax.rem(pick(g, y, x) + j, NX)

    tables = (
        pltpu.make_async_copy(slot_hbm, slot_ref, tab_sem.at[0]),
        pltpu.make_async_copy(doc_hbm, doc_ref, tab_sem.at[1]),
    )

    def local(h):
        at = pl.ds(h * D, D)
        g = group_of(h)
        return (
            pltpu.make_async_copy(q_ref.at[:, at], qg.at[at_q(g), 0, h], loc_sem.at[2, h]),
            pltpu.make_async_copy(k_ref.at[:, at], kvg.at[0, 0, 0, at_kv(g), h], loc_sem.at[0, h]),
            pltpu.make_async_copy(v_ref.at[:, at], kvg.at[1, 0, 0, at_kv(g), h], loc_sem.at[1, h]),
        )

    for h in range(heads):
        for copy in local(h):
            copy.start()
    for copy in tables:
        copy.start()

    barrier = pltpu.get_barrier_semaphore()
    partners = [plane_q(0), plane_kv(0), dev_c]
    partners += [ring_q(0, j) for j in (1, 2, 3)] + [ring_kv(0, j) for j in (1, 2, 3)]
    for dev in partners:
        pl.semaphore_signal(barrier, inc=1, device_id=dev, device_id_type=MESH)
    pl.semaphore_wait(barrier, len(partners))

    def remote(src, dst, send, recv, dev):
        return pltpu.make_async_remote_copy(
            src_ref=src, dst_ref=dst, send_sem=send, recv_sem=recv, device_id=dev, device_id_type=MESH
        )

    def z_kv(g):
        here = at_kv(g)
        return remote(
            kvg.at[:, 0, 0, here, of[g]], kvg.at[:, 0, 1, here, of[g]], zkv_s.at[g], zkv_r.at[g], plane_kv(g)
        )

    def z_q(g):
        here = at_q(g)
        return remote(qg.at[here, 0, of[g]], qg.at[here, 1, of[g]], zq_s, zq_r.at[g], plane_q(g))

    def r_kv(g, zr, j):
        block = kvg.at[:, 0, zr, at_kv(g), of[g]]
        return remote(block, block, kv_s, kv_r.at[g, zr], ring_kv(g, j))

    def r_q(g, zr, j):
        block = qg.at[at_q(g), zr, of[g]]
        return remote(block, block, q_s, q_r.at[g, zr], ring_q(g, j))

    def c_kv(g, zr):
        return remote(
            kvg.at[:, 0, zr, :, of[g]], kvg.at[:, 1, zr, :, of[g]], c_s, c_r.at[g, zr], dev_c
        )

    def ring_o(h, zr, j):
        g = group_of(h)
        return remote(
            op.at[zr, h, at_q(g, j)], orecv.at[zr, h, j - 1], o_s, o_r.at[zr, h], ring_q(g, j)
        )

    def z_o(h):
        return remote(zs.at[h], zr_buf.at[h], zo_s, zo_r.at[h], plane_q(group_of(h)))

    def take(ref, sem):
        pltpu.make_async_copy(ref, ref, sem).wait()

    def out_copy(h):
        return pltpu.make_async_copy(
            out_buf.at[h], out_ref.at[:, pl.ds(pl.multiple_of(h * D, D), D)], out_sem
        )

    for h in range(heads):
        for copy in local(h):
            copy.wait()
    for g in groups:
        z_kv(g).start()
    for j in (2, 1, 3):
        for g in groups:
            r_kv(g, 0, j).start()
    for j in (2, 1, 3):
        for g in groups:
            r_q(g, 0, j).start()
    for copy in tables:
        copy.wait()

    ends = [doc_ref[0]]
    for n in range(1, doc_ref.shape[0]):
        ends.append(ends[-1] + doc_ref[n])

    def doc_start(slot):
        start = jnp.int32(0)
        for end in ends:
            start = jnp.where(slot >= end, end, start)
        return start

    lane = lax.broadcasted_iota(jnp.int32, (8, NQ), 1)
    down = lax.broadcasted_iota(jnp.int32, (8, NQ), 0)
    part = lane // BLK
    diagonal = [jnp.where(down + row <= lane % BLK, 0.0, HIDE) for row in range(0, BLK, 8)]

    def build_mask(g):
        q_slot = jnp.zeros((8, NQ), jnp.int32)
        q_low = jnp.zeros((8, NQ), jnp.int32)
        for t in range(NQ // BLK):
            zt, half, rt = t // 8, (t // 4) % 2, t % 4
            zq = z if zt == 0 else (zb if g else za)
            iq = x * NX + rt if g else rt * NX + y
            slot = slot_ref[2 * ((zq * 2 + c) * 16 + iq) + half]
            hit = part == t
            q_slot = jnp.where(hit, slot, q_slot)
            q_low = jnp.where(hit, doc_start(slot), q_low)

        def mask(t, carry):
            ct, zt, half = t // 4, (t // 2) % 2, t % 2
            zk = z + zt * ((za if g else zb) - z)
            ck = c + ct * (1 - 2 * c)
            for rt in range(NX):
                ik = rt * NX + y if g else x * NX + rt
                slot = slot_ref[2 * ((zk * 2 + ck) * 16 + ik) + half]
                before = jnp.where((slot < q_slot) & (slot >= q_low), 0.0, HIDE)
                same = q_slot == slot
                for row in range(0, BLK, 8):
                    at = (zt * 2 + half) * KT + (ct * NX + rt) * BLK + row
                    term = jnp.where(same, diagonal[row // 8], before)
                    for tile in (0, 1):
                        bias[g, tile, pl.ds(pl.multiple_of(at, 8), 8), :] = term[:, tile * QT : (tile + 1) * QT]
            return carry

        lax.fori_loop(0, NC * NZ * 2, mask, 0)

    def swap_cores(zr):
        for g in (1, 0):
            take(kvg.at[:, 0, zr, pl.ds(0, NX - 1), of[g]], kv_r.at[g, zr])
            c_kv(g, zr).start()

    def swap_half(a):
        return pltpu.roll(a, R, axis=1)

    quarter = lax.broadcasted_iota(jnp.int32, (1, D), 1) // BLK

    def gather_lanes(pieces, n):
        moved = [pltpu.roll(p, (k - n) % 4 * BLK, axis=1) if k != n else p for k, p in enumerate(pieces)]
        return jnp.where(
            quarter < 2, jnp.where(quarter == 0, moved[0], moved[1]), jnp.where(quarter == 2, moved[2], moved[3])
        )

    def attend(units, zr):
        half = QT // 2
        scores = []
        for h, tile in units:
            low_keys = kvg[0, :, zr, :, h, 0:BLK, :].reshape(KT, D)
            high_keys = kvg[0, :, zr, :, h, BLK:R, :].reshape(KT, D)
            low_rows = qg[:, tile, h, 0:BLK, :].reshape(half, D)
            high_rows = qg[:, tile, h, BLK:R, :].reshape(half, D)
            g, first = group_of(h), zr * 2 * KT
            rows = jnp.concatenate([low_rows, high_rows], axis=0)
            wide = nt(low_keys, rows) * SCALE2 + bias[g, tile, first : first + KT, :]
            tall = nt(high_keys, high_rows) * SCALE2 + bias[g, tile, first + KT : first + 2 * KT, half:QT]
            scores.append((wide, tall))
        tops = []
        for (h, tile), (wide, tall) in zip(units, scores):
            top = jnp.max(wide, axis=0, keepdims=True)
            low_top, high_top = top[:, 0:half], jnp.maximum(top[:, half:QT], jnp.max(tall, axis=0, keepdims=True))
            top = jnp.concatenate([low_top, high_top], axis=1)
            top = jnp.maximum(top, FLOOR).astype(BF16).astype(F32)
            if zr:
                top = jnp.maximum(top, half_stat[h, tile, 0:1, :])
            tops.append(top)
        results = []
        for (h, tile), (wide, tall), top in zip(units, scores, tops):
            wide = jnp.exp2(wide - top)
            tall = jnp.exp2(tall - top[:, half:QT])
            total = jnp.sum(wide, axis=0, keepdims=True)
            total = (total[:, 0:half], total[:, half:QT] + jnp.sum(tall, axis=0, keepdims=True))
            low_values = kvg[1, :, zr, :, h, 0:BLK, :].reshape(KT, D)
            high_values = kvg[1, :, zr, :, h, BLK:R, :].reshape(KT, D)
            result = tn(low_values, wide.astype(BF16))
            high_result = result[:, half:QT] + tn(high_values, tall.astype(BF16))
            results.append((total, (result[:, 0:half], high_result)))
        row = lax.broadcasted_iota(jnp.int32, (STAT, half), 0)
        for (h, tile), top, (total, result) in zip(units, tops, results):
            sides, stats = [], []
            for side in (0, 1):
                span = slice(side * half, (side + 1) * half)
                m, l, o = top[:, span], total[side], result[side]
                if not zr:
                    half_stat[h, tile, 0:1, span] = m
                    half_stat[h, tile, 1:2, span] = l
                    half_o[h, tile, :, span] = o
                    continue
                shrink = jnp.exp2(half_stat[h, tile, 0:1, span] - m)
                l = l + half_stat[h, tile, 1:2, span] * shrink
                sides.append(o + half_o[h, tile, :, span] * shrink)
                l_hi = l.astype(BF16).astype(F32)
                stats.append(jnp.where(row == 0, m, jnp.where(row == 1, l_hi, l - l_hi)))
            if not zr:
                continue
            pieces = (sides[0][0:R], sides[1][0:R], sides[0][R:D], sides[1][R:D])
            for n in range(NX):
                op[tile, h, n, 0:R, :] = gather_lanes(pieces, n).astype(BF16)
                op[tile, h, n, R : R + STAT, :] = gather_lanes(stats * 2, n).astype(BF16)

    def unstat(block):
        stat = block.astype(F32)
        return stat[0:1], stat[1:2] + stat[2:3]

    def merge_ring(h, zr):
        take(orecv.at[zr, h], o_r.at[zr, h])
        here = at_q(group_of(h))
        parts = [(op[zr, h, here, 0:R, :], unstat(op[zr, h, here, R : R + STAT, :]))]
        for j in (1, 2, 3):
            parts.append((orecv[zr, h, j - 1, 0:R, :], unstat(orecv[zr, h, j - 1, R : R + STAT, :])))
        top = functools.reduce(jnp.maximum, [p[1][0] for p in parts])
        total = jnp.zeros((1, D), F32)
        result = jnp.zeros((R, D), F32)
        for block, (m, l) in parts:
            w = jnp.exp2(m - top)
            total = total + w * l
            result = result + block.astype(F32) * w
        return result, top, total

    def merge_far(h):
        result, top, total = merge_ring(h, 1)
        total_hi = total.astype(BF16).astype(F32)
        row = lax.broadcasted_iota(jnp.int32, (STAT, D), 0)
        zs[h, 0:R, :] = result.astype(BF16)
        zs[h, R : R + STAT, :] = jnp.where(
            row == 0, top, jnp.where(row == 1, total_hi, total - total_hi)
        ).astype(BF16)
        z_o(h).start()

    def finish(h):
        result, m_own, l_own = merge_ring(h, 0)
        z_o(h).wait_recv()
        m_far, l_far = unstat(zr_buf[h, R : R + STAT, :])
        top = jnp.maximum(m_far, m_own)
        w_far, w_own = jnp.exp2(m_far - top), jnp.exp2(m_own - top)
        total = w_far * l_far + w_own * l_own
        w_far, w_own = w_far / total, w_own / total
        packed = result * w_own + zr_buf[h, 0:R, :].astype(F32) * w_far
        tall = jnp.concatenate([packed, swap_half(packed)], axis=0)
        out_buf[h] = tall.T[0:R].astype(BF16)
        out_copy(h).start()

    build_mask(0)
    build_mask(1)
    swap_cores(0)
    for g in (1, 0):
        z_kv(g).wait_send()
        z_q(1 - g).start()
    for g in groups:
        z_kv(g).wait_recv()
        for j in (2, 1, 3):
            r_kv(g, 1, j).start()

    def early(tile):
        for g in groups:
            take(qg.at[pl.ds(0, NX - 1), tile, of[g]], q_r.at[g, tile])
        for h in range(0, heads, 2):
            attend([(n, tile) for n in range(h, min(h + 2, heads))], 0)

    for g in groups:
        c_kv(g, 0).wait_recv()
    early(0)
    for g in groups:
        z_q(g).wait_recv()
        for j in (2, 1, 3):
            r_q(g, 1, j).start()
    early(1)
    swap_cores(1)
    for g in (1, 0):
        c_kv(g, 1).wait_recv()

    def head_of(unit):
        return lax.rem(unit * first_heads, heads)

    def late(i, carry):
        @pl.when(i < heads)
        def _():
            units = (2 * i, 2 * i + 1)
            works = [(head_of(unit), jnp.where(unit < heads, 1, 0)) for unit in units]
            attend(works, 1)
            for h, tile in works:
                for j in (2, 1, 3):
                    ring_o(h, tile, j).start()

        for k in (0, 1):
            unit = 2 * (i - 2) + k

            @pl.when((unit >= 0) & (unit < heads))
            def _():
                merge_far(head_of(unit))

            @pl.when(unit >= heads)
            def _():
                finish(head_of(unit))

        return carry

    lax.fori_loop(0, heads + 2, late, 0)

    take(qg.at[0, 0], zq_s)
    take(kvg.at[:, 0, :, pl.ds(0, NX - 1)], kv_s)
    take(qg.at[pl.ds(0, NX - 1)], q_s)
    take(kvg.at[:, 0], c_s)
    take(orecv, o_s)
    take(zs, zo_s)
    take(out_buf, out_sem)


def per_device(queries, keys, values, slot_blocks, doc_blocks):
    width = queries.shape[1]
    heads = width // D
    dma = pltpu.SemaphoreType.DMA
    anywhere = pl.BlockSpec(memory_space=pltpu.HBM)
    return pl.pallas_call(
        functools.partial(kernel, heads),
        out_shape=jax.ShapeDtypeStruct(queries.shape, BF16),
        in_specs=[anywhere] * 5,
        out_specs=anywhere,
        scratch_shapes=[
            pltpu.SMEM(slot_blocks.shape, jnp.int32),
            pltpu.SMEM(doc_blocks.shape, jnp.int32),
            pltpu.VMEM((NX, NZ, heads, R, D), BF16),
            pltpu.VMEM((2, NC, NZ, NX, heads, R, D), BF16),
            pltpu.VMEM((2, NZ, NK, QT), F32),
            pltpu.VMEM((heads, NZ, D, QT), F32),
            pltpu.VMEM((heads, NZ, 8, QT), F32),
            pltpu.VMEM((NZ, heads, NX, R + STAT, D), BF16),
            pltpu.VMEM((NZ, heads, NX - 1, R + STAT, D), BF16),
            pltpu.VMEM((heads, R + STAT, D), BF16),
            pltpu.VMEM((heads, R + STAT, D), BF16),
            pltpu.VMEM((heads, R, D), BF16),
            dma((2,)),
            dma((3, heads)),
            dma((2,)), dma((2,)), dma, dma((2,)),
            dma, dma((2, 2)), dma, dma((2, 2)),
            dma, dma((2, 2)),
            dma, dma((2, heads)),
            dma, dma((heads,)), dma,
        ],
        compiler_params=pltpu.CompilerParams(
            collective_id=0, has_side_effects=True, vmem_limit_bytes=64 * 1024 * 1024
        ),
        cost_estimate=pl.CostEstimate(
            flops=4 * heads * NQ * NK * D, bytes_accessed=4 * queries.size * 2, transcendentals=heads * NQ * NK
        ),
    )(queries, keys, values, slot_blocks, doc_blocks)


def solution(mesh):
    rows = P(("outer", "inner"), "head")
    return jax.shard_map(
        per_device,
        mesh=mesh,
        in_specs=(rows, rows, rows, P(), P()),
        out_specs=rows,
        check_vma=False,
    )
```
